32 devices in a mesh: seq: 8 (over z, x), head: 4 (over y, core).
Axes of the slice: x: 2, y: 2, z: 4, core: 2. Of those that a mesh axis runs over, the one named last changes fastest.
Arguments:
- hidden_in: bfloat16 [4, 2048, 1024], P(None, 'seq'), may hold values from -8 to 8
- lengths: int32 [4], replicated, may hold values from 1024 to 2048, as said below
- input_gain: float32 [1024], replicated, may hold values from 0.1 to 1.9
- query_weight: bfloat16 [1024, 1024], P(None, 'head'), may hold values from -0.1875 to 0.1875
- key_weight: bfloat16 [1024, 1024], P(None, 'head'), may hold values from -0.1875 to 0.1875
- value_weight: bfloat16 [1024, 2048], P(None, 'head'), may hold values from -0.1875 to 0.1875
- alpha_weight: bfloat16 [1024, 8], P(None, 'head'), may hold values from -0.1875 to 0.1875
- beta_weight: bfloat16 [1024, 8], P(None, 'head'), may hold values from -1 to 1
- decay_log: float32 [8], P('head'), may hold values from -12 to -3
- decay_bias: float32 [8], P('head'), may hold values from -2 to 1
- query_kernel: bfloat16 [4, 1024], P(None, 'head'), may hold values from -3 to 3
- key_kernel: bfloat16 [4, 1024], P(None, 'head'), may hold values from -3 to 3
- value_kernel: bfloat16 [4, 2048], P(None, 'head'), may hold values from -3 to 3
- gate_weight: bfloat16 [1024, 2048], P(None, 'head'), may hold values from -0.1875 to 0.1875
- output_gain: float32 [256], replicated, may hold values from 0.1 to 1.9
- output_weight: bfloat16 [2048, 1024], P('head'), may hold values from -0.25 to 0.25
- mixed_gain: float32 [1024], P('head'), may hold values from 0.1 to 1.9
- swiglu_gate: bfloat16 [1024, 2816], P(None, 'head'), may hold values from -0.1875 to 0.1875
- swiglu_up: bfloat16 [1024, 2816], P(None, 'head'), may hold values from -0.1875 to 0.1875
- swiglu_down: bfloat16 [2816, 1024], P('head'), may hold values from -0.21875 to 0.21875
- cotangent: bfloat16 [4, 2048, 1024], P(None, 'seq'), may hold values from -6 to 6
Outputs:
- block_out: bfloat16 [4, 2048, 1024], P(None, 'seq', 'head')
- input_grad: float32 [4, 2048, 1024], P(None, 'seq', 'head')
- input_gain_grad: float32 [1024], P('head')
- query_weight_grad: float32 [1024, 1024], P(None, 'head')
- key_weight_grad: float32 [1024, 1024], P(None, 'head')
- value_weight_grad: float32 [1024, 2048], P(None, 'head')
- alpha_weight_grad: float32 [1024, 8], P(None, 'head')
- beta_weight_grad: float32 [1024, 8], P(None, 'head')
- decay_log_grad: float32 [8], P('head')
- decay_bias_grad: float32 [8], P('head')
- query_kernel_grad: float32 [4, 1024], P(None, 'head')
- key_kernel_grad: float32 [4, 1024], P(None, 'head')
- value_kernel_grad: float32 [4, 2048], P(None, 'head')
- gate_weight_grad: float32 [1024, 2048], P(None, 'head')
- output_gain_grad: float32 [256], P('head')
- output_weight_grad: float32 [2048, 1024], P('head')
- mixed_gain_grad: float32 [1024], P('head')
- swiglu_gate_grad: float32 [1024, 2816], P(None, 'head')
- swiglu_up_grad: float32 [1024, 2816], P(None, 'head')
- swiglu_down_grad: float32 [2816, 1024], P('head')
The draws below stay inside these ranges and needn't reach their ends.
Inputs may be any that keep to these rules, and one draw needn't show every extreme that they name: Each slot's valid positions are its first lengths entries; one slot, drawn from the seed, is full at 2048.
All inputs are finite; a program needn't handle non-finite values.
Results may differ from the reference program's by a relative error of at most 0.015.
The reference program's roundings to bfloat16 on the way count: a program that leaves them out, or rounds other values in their place, can miss the bound.
Values may be sent and summed in bfloat16 or wider, within the bound.
A program may use at most 256 MiB of HBM per device.

```python
import jax
import jax.numpy as jnp
from jax import lax

D = 1024
HEADS = 8
DK = 128
DV = 256
FF = 2816
CONV = 4
BLOCK = 64
SLOTS = 4
SLOT_LEN = 2048


def draw_lengths(key, part):
    key = jax.random.fold_in(key, 11)
    key_length, key_choice = jax.random.split(key)
    lengths_drawn = jax.random.randint(key_length, (SLOTS,), SLOT_LEN // 2, SLOT_LEN + 1)
    chosen_slot = jax.random.randint(key_choice, (), 0, SLOTS)
    return jnp.where(jnp.arange(SLOTS) == chosen_slot, SLOT_LEN, lengths_drawn).astype(jnp.int32)


def feature_direction(key):
    direction_key = jax.random.fold_in(key, 501)
    return jnp.clip(jax.random.normal(direction_key, (D,), jnp.float32), -3.0, 3.0)


def marked_heads(key, count):
    order_key = jax.random.fold_in(key, 502)
    ranks = jax.random.permutation(order_key, HEADS)
    return (ranks < count).astype(jnp.float32)


def draw_hidden_in(key, part):
    direction = feature_direction(key)
    key = jax.random.fold_in(key, 12)
    noise = jnp.clip(jax.random.normal(key, (SLOTS, SLOT_LEN, D), jnp.float32), -6.0, 6.0)
    return (noise + 0.5 * direction).astype(jnp.bfloat16)


def draw_beta_weight(key, part):
    direction = feature_direction(key)
    marked = marked_heads(key, HEADS // 2)
    key = jax.random.fold_in(key, 13)
    base = jnp.clip(jax.random.normal(key, (D, HEADS), jnp.float32), -4.0, 4.0) * D ** (-0.5)
    shifted = base - 10.0 * direction[:, None] * marked[None, :] / D
    return shifted.astype(jnp.bfloat16)


def draw_decay_log(key, part):
    marked = marked_heads(key, HEADS // 2)
    key = jax.random.fold_in(key, 14)
    level = jax.random.uniform(key, (HEADS,), jnp.float32)
    slow_value = -12.0 + 2.5 * level
    fast_value = -6.0 + 3.0 * level
    return jnp.where(marked > 0, slow_value, fast_value).astype(jnp.float32)


def shard_levels(own_key, shape, cuts, smallest, top_value):
    def one(dim, blocks):
        heights = jax.random.uniform(jax.random.fold_in(jax.random.fold_in(own_key, 6), dim), (blocks,), jnp.float32, smallest / len(cuts), top_value / len(cuts))
        return jnp.repeat(jnp.exp(heights), shape[dim] // blocks).reshape((-1,) + (1,) * (len(shape) - dim - 1))

    loudness = one(*cuts[0])
    for cut in cuts[1:]:
        loudness = loudness * one(*cut)
    return loudness


def scatter_about(stream_key, shape, deviation, most, cuts=(), kind=jnp.bfloat16):
    values = deviation * jax.random.normal(stream_key, shape, jnp.float32)
    if cuts:
        values = values * shard_levels(stream_key, shape, cuts, -0.22, 0.18)
    return jnp.clip(values, -most, most).astype(kind)


def setup_inputs(seed: int = 0) -> dict:
    keys = jax.random.split(jax.random.key(seed), 22)
    hidden_in = draw_hidden_in(jax.random.fold_in(keys[21], 71), 0)
    lengths = draw_lengths(jax.random.fold_in(keys[21], 71), 0)
    input_gain = jnp.clip(1.0 + 0.18 * jax.random.normal(keys[2], (D,), jnp.float32), 0.1, 1.9)
    query_weight = scatter_about(keys[3], (D, HEADS * DK), D ** -0.5, 0.1875, ((1, 4),))
    key_weight = scatter_about(keys[4], (D, HEADS * DK), D ** -0.5, 0.1875, ((1, 4),))
    value_weight = scatter_about(keys[5], (D, HEADS * DV), D ** -0.5, 0.1875, ((1, 4),))
    alpha_weight = scatter_about(keys[6], (D, HEADS), D ** -0.5, 0.1875, ((1, 4),))
    beta_weight = draw_beta_weight(jax.random.fold_in(keys[21], 71), 0)
    decay_log = draw_decay_log(jax.random.fold_in(keys[21], 71), 0)
    decay_bias = jnp.clip(-2.0 + 3.0 * jax.random.uniform(keys[9], (HEADS,), jnp.float32) ** shard_levels(keys[9], (HEADS,), ((0, 4),), -0.2, 0.2), -2.0, 1.0)
    query_kernel = scatter_about(keys[10], (CONV, HEADS * DK), CONV ** -0.5, 3.0, ((1, 4),))
    key_kernel = scatter_about(keys[11], (CONV, HEADS * DK), CONV ** -0.5, 3.0, ((1, 4),))
    value_kernel = scatter_about(keys[12], (CONV, HEADS * DV), CONV ** -0.5, 3.0, ((1, 4),))
    gate_weight = scatter_about(keys[13], (D, HEADS * DV), D ** -0.5, 0.1875, ((1, 4),))
    output_gain = jnp.clip(1.0 + 0.18 * jax.random.normal(keys[14], (DV,), jnp.float32), 0.1, 1.9)
    output_weight = scatter_about(keys[15], (HEADS * DV, D), (HEADS * DV // 4) ** -0.5, 0.25, ((0, 4),))
    mixed_gain = jnp.clip(1.0 + 0.18 * jax.random.normal(keys[16], (D,), jnp.float32), 0.1, 1.9)
    swiglu_gate = scatter_about(keys[17], (D, FF), D ** -0.5, 0.1875, ((1, 4),))
    swiglu_up = scatter_about(keys[18], (D, FF), D ** -0.5, 0.1875, ((1, 4),))
    swiglu_down = scatter_about(keys[19], (FF, D), (FF // 4) ** -0.5, 0.21875, ((0, 4),))
    cotangent = scatter_about(keys[20], (SLOTS, SLOT_LEN, D), 1.0, 6.0, ((1, 8),))
    return {"hidden_in": hidden_in, "lengths": lengths, "input_gain": input_gain, "query_weight": query_weight, "key_weight": key_weight, "value_weight": value_weight, "alpha_weight": alpha_weight, "beta_weight": beta_weight, "decay_log": decay_log, "decay_bias": decay_bias, "query_kernel": query_kernel, "key_kernel": key_kernel, "value_kernel": value_kernel, "gate_weight": gate_weight, "output_gain": output_gain, "output_weight": output_weight, "mixed_gain": mixed_gain, "swiglu_gate": swiglu_gate, "swiglu_up": swiglu_up, "swiglu_down": swiglu_down, "cotangent": cotangent}


HIGHEST_PRECISION = lax.Precision.HIGHEST
NORM_EPSILON = 1e-05
UNIT_EPSILON = 1e-06

@jax.custom_vjp
def low(v):
    return lax.optimization_barrier(v.astype(jnp.bfloat16)).astype(jnp.float32)

@jax.custom_vjp
def low_back(v):
    return v

def low_keep(v):
    return (low(v), None)

def low_pass(kept, grad):
    return (grad,)

def back_keep(v):
    return (v, None)

def back_low(kept, grad):
    return (low(grad),)
low.defvjp(low_keep, low_pass)
low_back.defvjp(back_keep, back_low)

def matmul(left, right):
    return jnp.dot(left.astype(jnp.float32), right.astype(jnp.float32), precision=HIGHEST_PRECISION, preferred_element_type=jnp.float32)

def rms_norm(tensor, gain):
    return tensor * lax.rsqrt(lax.optimization_barrier(jnp.mean(tensor * tensor, axis=-1, keepdims=True)) + NORM_EPSILON) * gain

def unit_norm(tensor):
    return tensor * lax.rsqrt(lax.optimization_barrier(jnp.sum(tensor * tensor, axis=-1, keepdims=True)) + UNIT_EPSILON)

def silu_act(tensor):
    return tensor * jax.nn.sigmoid(tensor)

def causal_kernel(sequence, kernel):
    taps = kernel.shape[0]
    length_seq = sequence.shape[0]
    padded = jnp.concatenate([jnp.zeros((taps - 1, sequence.shape[1]), sequence.dtype), sequence], axis=0)
    result = kernel[0] * padded[0:length_seq]
    for offset in range(1, taps):
        result = result + kernel[offset] * padded[offset:offset + length_seq]
    return result

def block_terms(queries, key_rows, value_rows, strength, log_decay):
    length_block = queries.shape[-2]
    position = jnp.arange(length_block)
    inclusive = position[:, None] >= position[None, :]
    strictly = position[:, None] > position[None, :]
    cumulated = jnp.cumsum(log_decay, axis=-1)
    difference = cumulated[..., :, None] - cumulated[..., None, :]
    decayed = jnp.where(inclusive, jnp.exp(jnp.where(inclusive, difference, 0.0)), 0.0)
    key_products = jnp.einsum('...td,...jd->...tj', key_rows, key_rows, precision=HIGHEST_PRECISION)
    triangle = jnp.where(strictly, strength[..., :, None] * decayed * key_products, 0.0)
    right_side = jnp.concatenate([strength[..., None] * value_rows, (strength * jnp.exp(cumulated))[..., None] * key_rows], axis=-1)
    solved = lax.linalg.triangular_solve(triangle, right_side, left_side=True, lower=True, unit_diagonal=True)
    channels = value_rows.shape[-1]
    delta_value = solved[..., :channels]
    key_mix = solved[..., channels:]
    scores = decayed * jnp.einsum('...td,...jd->...tj', queries, key_rows, precision=HIGHEST_PRECISION)
    query_eff = jnp.exp(cumulated)[..., None] * queries - jnp.einsum('...tj,...jd->...td', scores, key_mix, precision=HIGHEST_PRECISION)
    end_weight = jnp.exp(cumulated[..., -1:] - cumulated)[..., None]
    identity = jnp.eye(key_rows.shape[-1], dtype=key_rows.dtype)
    transition = jnp.exp(cumulated[..., -1])[..., None, None] * identity - jnp.einsum('...jd,...je->...de', key_mix * end_weight, key_rows, precision=HIGHEST_PRECISION)
    state_bias = jnp.einsum('...jv,...jd->...vd', delta_value * end_weight, key_rows, precision=HIGHEST_PRECISION)
    intra_out = jnp.einsum('...tj,...jv->...tv', scores, delta_value, precision=HIGHEST_PRECISION)
    return (intra_out, query_eff, transition, state_bias)

def delta_rule(queries, key_rows, value_rows, strength, log_decay):
    blocks = queries.shape[0] // BLOCK

    def blocked(tensor):
        shaped = tensor.reshape((blocks, BLOCK) + tensor.shape[1:])
        return jnp.swapaxes(shaped, 1, 2)

    def advance(state, inputs):
        intra_out, query_eff, transition, state_bias = block_terms(inputs[0], inputs[1], inputs[2], inputs[3], inputs[4])
        emitted = intra_out + jnp.einsum('htd,hvd->htv', query_eff, state, precision=HIGHEST_PRECISION)
        new_state = jnp.einsum('hvd,hdf->hvf', state, transition, precision=HIGHEST_PRECISION) + state_bias
        return (new_state, emitted)
    initial = jnp.zeros((queries.shape[1], value_rows.shape[2], queries.shape[2]), queries.dtype)
    final_state, emitted_all = lax.scan(jax.checkpoint(advance), initial, (blocked(queries), blocked(key_rows), blocked(value_rows), blocked(strength), blocked(log_decay)))
    return jnp.swapaxes(emitted_all, 1, 2).reshape(queries.shape[0], queries.shape[1], value_rows.shape[2])

def reference(hidden_in, lengths, input_gain, query_weight, key_weight, value_weight, alpha_weight, beta_weight, decay_log, decay_bias, query_kernel, key_kernel, value_kernel, gate_weight, output_gain, output_weight, mixed_gain, swiglu_gate, swiglu_up, swiglu_down, cotangent):
    position = jnp.arange(SLOT_LEN)
    mask = (position[None, :] < lengths[:, None]).astype(jnp.float32)
    weights = jax.tree.map(lambda tensor: tensor.astype(jnp.float32), (input_gain, query_weight, key_weight, value_weight, alpha_weight, beta_weight, decay_log, decay_bias, query_kernel, key_kernel, value_kernel, gate_weight, output_gain, output_weight, mixed_gain, swiglu_gate, swiglu_up, swiglu_down))

    def forward(x_all, params):
        gain_first, weight_query, weight_key, weight_value, weight_alpha, weight_beta, rate_log, rate_bias, kernel_query, kernel_key, kernel_value, weight_gate, gain_output, weight_output, gain_second, weight_swiglu_gate, weight_swiglu_up, weight_swiglu_down = params

        def slot_forward(slot_in):
            slot_x, slot_mask = slot_in
            length_slot = slot_x.shape[0]
            normed_first = low(rms_norm(slot_x, gain_first))
            query_pre = low_back(low(matmul(normed_first, weight_query)))
            key_pre = low_back(low(matmul(normed_first, weight_key)))
            value_pre = low_back(low(matmul(normed_first, weight_value)))
            gate_pre = low_back(matmul(normed_first, weight_gate))
            alpha_pre = low_back(matmul(normed_first, weight_alpha))
            beta_pre = low_back(matmul(normed_first, weight_beta))
            query_act = silu_act(causal_kernel(query_pre, kernel_query)).reshape(length_slot, HEADS, DK)
            key_act = silu_act(causal_kernel(key_pre, kernel_key)).reshape(length_slot, HEADS, DK)
            value_act = silu_act(causal_kernel(value_pre, kernel_value)).reshape(length_slot, HEADS, DV)
            queries = low(unit_norm(query_act) * DK ** (-0.5))
            key_rows = low(unit_norm(key_act))
            value_rows = low(value_act)
            strength = jax.nn.sigmoid(beta_pre)
            log_decay = -jnp.exp(rate_log) * jax.nn.softplus(alpha_pre + rate_bias)
            mixer_out = delta_rule(queries, key_rows, value_rows, strength, log_decay)
            gated = low((rms_norm(mixer_out, gain_output) * silu_act(gate_pre.reshape(length_slot, HEADS, DV))).reshape(length_slot, HEADS * DV))
            attention = low_back(matmul(gated, weight_output))
            residual = slot_x + slot_mask[:, None] * attention
            normed_second = low(rms_norm(residual, gain_second))
            gate_values = low_back(matmul(normed_second, weight_swiglu_gate))
            upward_values = low_back(matmul(normed_second, weight_swiglu_up))
            activation = low(silu_act(gate_values) * upward_values)
            swiglu_out = low_back(matmul(activation, weight_swiglu_down))
            return residual + slot_mask[:, None] * swiglu_out
        return lax.map(jax.checkpoint(slot_forward), (x_all, mask))
    outputs, backward = jax.vjp(forward, hidden_in.astype(jnp.float32), weights)
    input_grad, param_grads = backward(cotangent.astype(jnp.float32))
    return (outputs.astype(jnp.bfloat16), input_grad, param_grads[0], param_grads[1], param_grads[2], param_grads[3], param_grads[4], param_grads[5], param_grads[6], param_grads[7], param_grads[8], param_grads[9], param_grads[10], param_grads[11], param_grads[12], param_grads[13], param_grads[14], param_grads[15], param_grads[16], param_grads[17])
```

```python
import functools

import jax
import jax.numpy as jnp
from jax import lax
from jax.experimental import pallas as pl
from jax.experimental.pallas import tpu as pltpu
from jax.sharding import PartitionSpec as P

NORM_EPSILON = 1e-05
UNIT_EPSILON = 1e-06
RIM = 8
LANES = 128
F32 = jnp.float32
BF16 = jnp.bfloat16
VMEM_LIMIT = 56 * 1024 * 1024

NN = (((1,), (0,)), ((), ()))
NT = (((1,), (1,)), ((), ()))
TN = (((0,), (0,)), ((), ()))


def split(x):
    high = x.astype(BF16)
    return high, (x - high.astype(F32)).astype(BF16)


def raw(a, b, dims):
    return lax.dot_general(a, b, dims, preferred_element_type=F32)


def mm(a, b, dims=NN):
    a_high, a_low = a if isinstance(a, tuple) else (a, None)
    b_high, b_low = b if isinstance(b, tuple) else (b, None)
    total = raw(a_high, b_high, dims)
    if a_low is not None:
        total = total + raw(a_low, b_high, dims)
    if b_low is not None:
        total = total + raw(a_high, b_low, dims)
    return total


def sigmoid(x):
    return 1.0 / (1.0 + jnp.exp(-x))


def softplus(x):
    return jnp.maximum(x, 0.0) + jnp.log1p(jnp.exp(-jnp.abs(x)))


def grid_masks(size):
    row = lax.broadcasted_iota(jnp.int32, (size, size), 0)
    col = lax.broadcasted_iota(jnp.int32, (size, size), 1)
    return row, col


def unit_inverse(lower, row, col):
    size = lower.shape[0]
    base = 8
    same = (row // base) == (col // base)
    block = jnp.where(same, lower, 0.0)
    one = split(block)
    square = mm(one, one)
    square_parts = split(square)
    fourth = mm(square_parts, square_parts)
    inverse = jnp.where(row == col, 1.0, 0.0) - block + square - mm(one, square_parts)
    inverse = inverse + mm(split(inverse), split(fourth))
    while base < size:
        inside = (row // (2 * base)) == (col // (2 * base))
        apart = (row // base) != (col // base)
        off = split(jnp.where(inside & apart, lower, 0.0))
        parts = split(inverse)
        inverse = inverse - mm(split(mm(parts, off)), parts)
        base *= 2
    return inverse


def gates_of(ab, rate, bias):
    return -rate * softplus(ab + bias), sigmoid(ab)


def decay_of(log_col, log_row, row, col):
    seen = row >= col
    cum_col = jnp.sum(jnp.where(seen, log_row, 0.0), axis=1, keepdims=True)
    cum_row = jnp.sum(jnp.where(row <= col, log_col, 0.0), axis=0, keepdims=True)
    end = jnp.sum(log_row, axis=1, keepdims=True)
    decayed = jnp.where(seen, jnp.exp(jnp.where(seen, cum_col - cum_row, 0.0)), 0.0)
    return cum_col, cum_row, end, decayed


def convolve(ext, taps_ref, length):
    taps = 4
    total = taps_ref[0:1, :] * ext[pl.ds(RIM - taps + 1, length), :]
    for tap in range(1, taps):
        total = total + taps_ref[tap : tap + 1, :] * ext[pl.ds(RIM - taps + 1 + tap, length), :]
    return total


def delta_forward(
    heads, key_dim, value_dim, pre_ref, rim_ref, ab_ref, abt_ref, taps_ref, lane_ref, col_ref,
    query_out, key_out, value_out, inverse_out, delta_out, mix_out, eff_out, map_out, shift_out, ext,
):
    length = pre_ref.shape[1]
    ext[0:RIM, :] = rim_ref[0]
    ext[RIM : RIM + length, :] = pre_ref[0].astype(F32)
    conv = convolve(ext, taps_ref, length)
    active = conv * sigmoid(conv)
    row, col = grid_masks(length)
    log_cols, strength_cols = gates_of(ab_ref[0], lane_ref[0:1, :], lane_ref[1:2, :])
    log_rows, strength_rows = gates_of(abt_ref[0], col_ref[0:8, 0:1], col_ref[8:16, 0:1])
    key_start = heads * key_dim
    value_start = 2 * heads * key_dim
    for h in range(heads):
        query_act = active[:, h * key_dim : (h + 1) * key_dim]
        key_act = active[:, key_start + h * key_dim : key_start + (h + 1) * key_dim]
        value_act = active[:, value_start + h * value_dim : value_start + (h + 1) * value_dim]
        query_scale = lax.rsqrt(jnp.sum(query_act * query_act, axis=1, keepdims=True) + UNIT_EPSILON)
        key_scale = lax.rsqrt(jnp.sum(key_act * key_act, axis=1, keepdims=True) + UNIT_EPSILON)
        query = (query_act * query_scale * key_dim ** (-0.5)).astype(BF16)
        key = (key_act * key_scale).astype(BF16)
        value = value_act.astype(BF16)
        query_out[0, h] = query
        key_out[0, h] = key
        value_out[0, h] = value
        strength = strength_cols[:, heads + h : heads + h + 1]
        strength_row = strength_rows[heads + h : heads + h + 1, :]
        cum_col, cum_row, end, decayed = decay_of(
            log_cols[:, h : h + 1], log_rows[h : h + 1, :], row, col
        )
        products = mm(key, key, NT)
        triangle = jnp.where(row > col, strength * decayed * products, 0.0)
        inverse = unit_inverse(triangle, row, col)
        inverse_out[0, h] = inverse
        scaled = inverse * strength_row
        delta = mm(split(scaled), value)
        mix = mm(split(scaled * jnp.exp(cum_row)), key)
        delta_out[0, h] = delta
        mix_out[0, h] = mix
        scores = split(decayed * mm(query, key, NT))
        eff_out[0, h] = jnp.exp(cum_col) * query.astype(F32) - mm(scores, split(mix))
        end_weight = jnp.exp(end - cum_col)
        small_row = lax.broadcasted_iota(jnp.int32, (key_dim, key_dim), 0)
        small_col = lax.broadcasted_iota(jnp.int32, (key_dim, key_dim), 1)
        moved = jnp.where(small_row == small_col, jnp.exp(end), 0.0)
        map_out[0, h] = moved - mm(split(mix * end_weight), key, TN)
        shift_out[0, h] = mm(split(delta * end_weight), key, TN)


def emit_forward(
    heads, query_ref, key_ref, ab_ref, abt_ref, lane_ref, col_ref, delta_ref, mix_ref, state_ref,
    gate_ref, gain_ref, rows_out, mixer_out, gated_out,
):
    length = query_ref.shape[2]
    value_dim = delta_ref.shape[3]
    row, col = grid_masks(length)
    log_cols, _ = gates_of(ab_ref[0], lane_ref[0:1, :], lane_ref[1:2, :])
    log_rows, _ = gates_of(abt_ref[0], col_ref[0:8, 0:1], col_ref[8:16, 0:1])
    for h in range(heads):
        query, key = query_ref[0, h], key_ref[0, h]
        cum_col, _, _, decayed = decay_of(log_cols[:, h : h + 1], log_rows[h : h + 1, :], row, col)
        scores = split(decayed * mm(query, key, NT))
        state = split(state_ref[0, h])
        rows = delta_ref[0, h] - mm(split(mix_ref[0, h]), state, NT)
        rows_out[0, h] = rows
        mixer = mm(scores, split(rows)) + jnp.exp(cum_col) * mm(query, state, NT)
        mixer_out[0, h] = mixer
        scale = lax.rsqrt(jnp.sum(mixer * mixer, axis=1, keepdims=True) / value_dim + NORM_EPSILON)
        gate = gate_ref[0, :, h * value_dim : (h + 1) * value_dim]
        gated = mixer * scale * gain_ref[0:1, :] * (gate * sigmoid(gate))
        gated_out[0, :, h * value_dim : (h + 1) * value_dim] = gated.astype(BF16)


def gate_backward(
    heads, gated_grad_ref, mixer_ref, gate_ref, gain_ref, eff_ref,
    mixer_grad_out, gate_grad_out, gain_grad_out, shift_grad_out,
):
    value_dim = mixer_ref.shape[3]

    @pl.when(pl.program_id(0) == 0)
    def _():
        gain_grad_out[...] = jnp.zeros_like(gain_grad_out)

    gain = gain_ref[0:1, :]
    for h in range(heads):
        here = slice(h * value_dim, (h + 1) * value_dim)
        grad = gated_grad_ref[0, :, here]
        mixer = mixer_ref[0, h]
        gate = gate_ref[0, :, here]
        scale = lax.rsqrt(jnp.sum(mixer * mixer, axis=1, keepdims=True) / value_dim + NORM_EPSILON)
        sig = sigmoid(gate)
        unit = mixer * scale
        gate_grad_out[0, :, here] = (
            grad * unit * gain * (sig * (1.0 + gate * (1.0 - sig)))
        ).astype(BF16)
        scaled_grad = grad * (gate * sig)
        gain_grad_out[0:1, :] += jnp.sum(scaled_grad * unit, axis=0, keepdims=True)
        unit_grad = scaled_grad * gain
        stat = jnp.sum(unit_grad * mixer, axis=1, keepdims=True) / value_dim
        mixer_grad = scale * (unit_grad - mixer * (scale * scale * stat))
        mixer_grad_out[0, h] = mixer_grad
        shift_grad_out[0, h] = mm(split(mixer_grad), split(eff_ref[0, h]), TN)


def delta_backward(
    heads, key_dim, value_dim, pre_ref, rim_ref, ab_ref, abt_ref, taps_ref, lane_ref, col_ref,
    query_ref, key_ref, value_ref, inverse_ref, rows_ref, state_ref, state_grad_ref, mixer_grad_ref,
    pre_grad_out, tail_out, rim_grad_out, ab_grad_out, taps_grad_out, lane_grad_out,
    ext, conv_grad,
):
    length = pre_ref.shape[1]
    taps = 4

    @pl.when(pl.program_id(0) == 0)
    def _():
        taps_grad_out[...] = jnp.zeros_like(taps_grad_out)
        lane_grad_out[...] = jnp.zeros_like(lane_grad_out)

    ext[0:RIM, :] = rim_ref[0]
    ext[RIM : RIM + length, :] = pre_ref[0].astype(F32)
    row, col = grid_masks(length)
    lane = lax.broadcasted_iota(jnp.int32, (length, LANES), 1)
    log_cols, strength_cols = gates_of(ab_ref[0], lane_ref[0:1, :], lane_ref[1:2, :])
    log_rows, strength_rows = gates_of(abt_ref[0], col_ref[0:8, 0:1], col_ref[8:16, 0:1])
    key_start = heads * key_dim
    value_start = 2 * heads * key_dim
    strict = row > col
    grads = jnp.zeros((length, LANES), F32)
    conv_grad[0:RIM, :] = jnp.zeros((RIM, conv_grad.shape[1]), F32)
    conv_grad[RIM + length : 2 * RIM + length, :] = jnp.zeros((RIM, conv_grad.shape[1]), F32)

    def activation(start, width):
        total = taps_ref[0:1, start : start + width] * ext[pl.ds(RIM - taps + 1, length), start : start + width]
        for tap in range(1, taps):
            total = total + (
                taps_ref[tap : tap + 1, start : start + width]
                * ext[pl.ds(RIM - taps + 1 + tap, length), start : start + width]
            )
        sig = sigmoid(total)
        return total * sig, sig * (1.0 + total * (1.0 - sig))

    def unit_back(grad, start, scale_by):
        act, slope = activation(start, key_dim)
        scale = lax.rsqrt(jnp.sum(act * act, axis=1, keepdims=True) + UNIT_EPSILON)
        inner = jnp.sum(act * grad, axis=1, keepdims=True)
        back = scale_by * scale * (grad - act * (scale * scale * inner))
        conv_grad[RIM : RIM + length, start : start + key_dim] = back * slope

    for h in range(heads):
        query, key, value = query_ref[0, h], key_ref[0, h], value_ref[0, h]
        query_f, key_f = query.astype(F32), key.astype(F32)
        strength = strength_cols[:, heads + h : heads + h + 1]
        cum_col, cum_row, end, decayed = decay_of(
            log_cols[:, h : h + 1], log_rows[h : h + 1, :], row, col
        )
        rise = jnp.exp(cum_col)
        end_weight = jnp.exp(end - cum_col)
        state_f, leaving_f = state_ref[0, h], state_grad_ref[0, h]
        state, leaving = split(state_f), split(leaving_f)
        rows = split(rows_ref[0, h])
        out_grad = split(mixer_grad_ref[0, h])
        products = mm(key, key, NT)
        scores = decayed * mm(query, key, NT)
        rows_grad = mm(split(scores), out_grad, TN) + end_weight * mm(key, leaving, NT)
        scores_grad = mm(out_grad, rows, NT)
        query_grad = rise * mm(out_grad, state)
        right_grad = mm(split(inverse_ref[0, h]), split(rows_grad), TN)
        key_state = mm(key, state, NT)
        triangle_grad = -jnp.where(strict, mm(split(right_grad), rows, NT), 0.0)
        value_grad = strength * right_grad
        strength_grad = jnp.sum(right_grad * (value.astype(F32) - rise * key_state), axis=1, keepdims=True)
        read_grad = -rise * value_grad
        cum_grad = jnp.sum(read_grad * key_state, axis=1, keepdims=True)
        key_grad = mm(split(read_grad), state)
        decayed_grad = triangle_grad * decayed
        strength_grad = strength_grad + jnp.sum(decayed_grad * products, axis=1, keepdims=True)
        weighted = strength * decayed_grad
        both = weighted * products + scores_grad * scores
        products_grad = split(weighted)
        overlap_grad = split(scores_grad * decayed)
        cum_grad = cum_grad + jnp.sum(both, axis=1, keepdims=True) + jnp.sum(query_f * query_grad, axis=1, keepdims=True)
        query_grad = query_grad + mm(overlap_grad, key)
        key_grad = (
            key_grad + mm(overlap_grad, query, TN) + mm(products_grad, key) + mm(products_grad, key, TN)
        )
        moved = mm(rows, leaving)
        key_grad = key_grad + end_weight * moved
        end_part = jnp.sum(moved * key_f, axis=1, keepdims=True) * end_weight
        cum_grad = cum_grad - end_part
        last = jnp.sum(end_part, axis=0, keepdims=True) + jnp.exp(end) * jnp.sum(
            jnp.sum(leaving_f * state_f, axis=1, keepdims=True), axis=0, keepdims=True
        )
        turned = jnp.sum(jnp.where(row == col, cum_grad, 0.0), axis=0, keepdims=True)
        turned = turned - jnp.sum(both, axis=0, keepdims=True)
        log_grad = jnp.sum(jnp.where(row <= col, turned, 0.0), axis=1, keepdims=True) + last
        grads = jnp.where(lane == h, log_grad, grads)
        grads = jnp.where(lane == heads + h, strength_grad, grads)
        unit_back(query_grad, h * key_dim, key_dim ** (-0.5))
        unit_back(key_grad, key_start + h * key_dim, 1.0)
        _, slope = activation(value_start + h * value_dim, value_dim)
        conv_grad[RIM : RIM + length, value_start + h * value_dim : value_start + (h + 1) * value_dim] = (
            value_grad * slope
        )

    softened = -lane_ref[0:1, :] * sigmoid(ab_ref[0] + lane_ref[1:2, :])
    decay_part = grads * softened
    is_log = lane < heads
    ab_grad_out[0] = jnp.where(is_log, decay_part, grads * strength_cols * (1.0 - strength_cols))
    lane_grad_out[0:1, :] += jnp.sum(jnp.where(is_log, grads * log_cols, 0.0), axis=0, keepdims=True)
    lane_grad_out[1:2, :] += jnp.sum(jnp.where(is_log, decay_part, 0.0), axis=0, keepdims=True)
    main = conv_grad[RIM : RIM + length, :]
    pre_grad = jnp.zeros_like(main)
    rim_grad = jnp.zeros((RIM, conv_grad.shape[1]), F32)
    for tap in range(taps):
        weight = taps_ref[tap : tap + 1, :]
        taps_grad_out[tap : tap + 1, :] += jnp.sum(
            main * ext[pl.ds(RIM - taps + 1 + tap, length), :], axis=0, keepdims=True
        )
        pre_grad = pre_grad + weight * conv_grad[pl.ds(RIM + taps - 1 - tap, length), :]
        rim_grad = rim_grad + weight * conv_grad[pl.ds(taps - 1 - tap, RIM), :]
    pre_grad_out[0] = pre_grad.astype(BF16)
    tail_out[0] = pre_grad[length - RIM : length, :]
    rim_grad_out[0] = rim_grad


def by_slot(shape):
    rest = len(shape) - 1
    return pl.BlockSpec((1,) + tuple(shape[1:]), lambda s: (s,) + (0,) * rest)


def whole(shape):
    return pl.BlockSpec(tuple(shape), lambda s: (0,) * len(shape))


def run_slots(body, slots, sliced, shared, sliced_out, shared_out=(), scratch=(), order=None):
    operands = list(sliced) + list(shared)
    specs = [by_slot(a.shape) for a in sliced] + [whole(a.shape) for a in shared]
    if order is not None:
        operands = [operands[i] for i in order]
        specs = [specs[i] for i in order]
    return pl.pallas_call(
        body,
        grid=(slots,),
        in_specs=specs,
        out_specs=[by_slot(o.shape) for o in sliced_out] + [whole(o.shape) for o in shared_out],
        out_shape=list(sliced_out) + list(shared_out),
        scratch_shapes=list(scratch),
        compiler_params=pltpu.CompilerParams(vmem_limit_bytes=VMEM_LIMIT),
    )(*operands)


def shifted(block, axis, distance):
    devices = range(lax.axis_size(axis))
    route = [(i - distance, i) for i in devices if i - distance in devices]
    return lax.ppermute(block, axis, route)


def to_units(parts, units):
    pairs, value_dim, key_dim = parts.shape
    share = units // pairs
    return parts.reshape(units, value_dim // share, key_dim)


def exchange(parts, axis):
    return lax.all_to_all(parts, axis, 0, 0, tiled=True)


def per_device(
    hidden_in, lengths, input_gain, query_weight, key_weight, value_weight, alpha_weight, beta_weight,
    decay_log, decay_bias, query_kernel, key_kernel, value_kernel, gate_weight, output_gain,
    output_weight, mixed_gain, swiglu_gate, swiglu_up, swiglu_down, cotangent,
):
    slots, segment, width = hidden_in.shape
    rows = slots * segment
    heads = decay_log.shape[0]
    key_dim = query_kernel.shape[1] // heads
    value_dim = value_kernel.shape[1] // heads
    taps = query_kernel.shape[0]
    split_key = heads * key_dim
    channels = 2 * split_key + heads * value_dim
    head_parts = lax.axis_size("head")
    seq_parts = lax.axis_size("seq")
    shard = width // head_parts
    head_start = lax.axis_index("head") * shard
    pairs = slots * heads
    sds = jax.ShapeDtypeStruct

    position = lax.axis_index("seq") * segment + jnp.arange(segment)
    mask = (position[None, :] < lengths[:, None]).astype(F32)[:, :, None]

    def norm_rows(x):
        inv = lax.rsqrt(jnp.mean(x * x, axis=-1, keepdims=True) + NORM_EPSILON)
        return inv, (x * inv * input_gain).astype(BF16)

    rim_in = shifted(hidden_in[:, segment - taps + 1 :, :], "seq", 1)
    x_full = hidden_in.astype(F32)
    inv_first, normed_first = norm_rows(x_full)
    normed_first = normed_first.reshape(rows, width)
    x_shard = lax.dynamic_slice_in_dim(x_full, head_start, shard, 2)
    qkv_weight = jnp.concatenate([query_weight, key_weight, value_weight], axis=1)
    ab_weight = jnp.concatenate(
        [alpha_weight, beta_weight, jnp.zeros((width, LANES - 2 * heads), BF16)], axis=1
    )

    def project(x, weight):
        return jnp.dot(x, weight, preferred_element_type=F32)

    pre_all = project(normed_first, qkv_weight).astype(BF16).reshape(slots, segment, channels)
    gate_pre = project(normed_first, gate_weight).reshape(slots, segment, -1)
    ab_pre = project(normed_first, ab_weight).reshape(slots, segment, LANES)
    ab_rows = jnp.swapaxes(ab_pre[:, :, :8], 1, 2)
    _, rim_normed = norm_rows(rim_in.astype(F32))
    rim_pre = project(rim_normed.reshape(slots * (taps - 1), width), qkv_weight).astype(BF16).astype(F32)
    rim_pre = jnp.pad(rim_pre.reshape(slots, taps - 1, channels), ((0, 0), (RIM - taps + 1, 0), (0, 0)))
    kernel = jnp.concatenate([query_kernel, key_kernel, value_kernel], axis=1).astype(F32)
    kernel = jnp.pad(kernel, ((0, 8 - taps), (0, 0)))
    rate = jnp.exp(decay_log)
    pad_heads = lambda v: jnp.pad(v, (0, LANES - heads))
    lane_gates = jnp.pad(jnp.stack([pad_heads(rate), pad_heads(decay_bias)]), ((0, 6), (0, 0)))
    pad_rows = lambda v: jnp.broadcast_to(jnp.pad(v, (0, 8 - heads))[:, None], (8, LANES))
    col_gates = jnp.concatenate([pad_rows(rate), pad_rows(decay_bias)], axis=0)
    gain_row = jnp.broadcast_to(output_gain[None, :], (8, value_dim))

    per_pair = lambda *tail: sds((slots, heads) + tail, F32)
    low_pair = lambda *tail: sds((slots, heads) + tail, BF16)
    query, key, value, inverse, delta, mix, eff, maps, shifts = run_slots(
        functools.partial(delta_forward, heads, key_dim, value_dim),
        slots,
        (pre_all, rim_pre, ab_pre, ab_rows),
        (kernel, lane_gates, col_gates),
        (
            low_pair(segment, key_dim), low_pair(segment, key_dim), low_pair(segment, value_dim),
            per_pair(segment, segment), per_pair(segment, value_dim), per_pair(segment, key_dim),
            per_pair(segment, key_dim), per_pair(key_dim, key_dim), per_pair(value_dim, key_dim),
        ),
        scratch=[pltpu.VMEM((segment + RIM, channels), F32)],
    )

    units = seq_parts
    share = units // pairs
    own_maps = jnp.repeat(maps.astype(BF16).reshape(pairs, key_dim, key_dim), share, axis=0)
    own_shifts = to_units(shifts.astype(BF16).reshape(pairs, value_dim, key_dim), units)
    all_maps = exchange(own_maps, "seq").astype(F32)
    all_shifts = exchange(own_shifts, "seq").astype(F32)
    high = functools.partial(jnp.dot, precision=lax.Precision.HIGHEST, preferred_element_type=F32)
    state = jnp.zeros_like(all_shifts[0])
    states = []
    for p in range(seq_parts):
        states.append(state)
        state = high(state, all_maps[p]) + all_shifts[p]
    state_in = exchange(jnp.stack(states).astype(BF16), "seq").astype(F32)
    state_in = state_in.reshape(slots, heads, value_dim, key_dim)

    value_rows, mixer, gated = run_slots(
        functools.partial(emit_forward, heads),
        slots,
        (query, key, ab_pre, ab_rows, delta, mix, state_in, gate_pre),
        (lane_gates, col_gates, gain_row),
        (
            per_pair(segment, value_dim), per_pair(segment, value_dim),
            sds((slots, segment, heads * value_dim), BF16),
        ),
        order=(0, 1, 2, 3, 8, 9, 4, 5, 6, 7, 10),
    )
    gated_low = gated.reshape(rows, heads * value_dim)

    def scatter_sum(part):
        low = part.astype(BF16).reshape(slots, segment, width)
        return lax.psum_scatter(low, "head", scatter_dimension=2, tiled=True).astype(F32)

    attention_shard = scatter_sum(project(gated_low, output_weight))
    residual = x_shard + mask * attention_shard
    square_sum = lax.psum(jnp.sum(residual * residual, axis=-1, keepdims=True), "head")
    inv_second = lax.rsqrt(square_sum / width + NORM_EPSILON)
    normed_shard = (residual * inv_second * mixed_gain).astype(BF16)
    normed_second = lax.all_gather(normed_shard, "head", axis=2, tiled=True).reshape(rows, width)
    gate_values = project(normed_second, swiglu_gate)
    upward_values = project(normed_second, swiglu_up)
    sigmoid_gate = jax.nn.sigmoid(gate_values)
    silu_gate = gate_values * sigmoid_gate
    activation = (silu_gate * upward_values).astype(BF16)
    out_grad = jnp.where(mask > 0, cotangent, jnp.zeros_like(cotangent)).reshape(rows, width)
    activation_grad = jnp.dot(out_grad, swiglu_down.T, preferred_element_type=F32)
    upward_grad = (activation_grad * silu_gate).astype(BF16)
    gate_grad = (
        activation_grad * upward_values * sigmoid_gate * (1.0 + gate_values * (1.0 - sigmoid_gate))
    ).astype(BF16)
    normed_part = jnp.dot(upward_grad, swiglu_up.T, preferred_element_type=F32) + jnp.dot(
        gate_grad, swiglu_gate.T, preferred_element_type=F32
    )
    normed_grad = scatter_sum(normed_part)
    swiglu_shard = scatter_sum(project(activation, swiglu_down))
    block_out = (residual + mask * swiglu_shard).astype(BF16)
    swiglu_down_grad = project(activation.T, out_grad)
    swiglu_up_grad = project(normed_second.T, upward_grad)
    swiglu_gate_grad = project(normed_second.T, gate_grad)

    def sum_low(parts):
        flat = jnp.concatenate([p.astype(BF16).reshape(-1, LANES) for p in parts], axis=0)
        total = lax.psum(flat, "seq")
        out, at = [], 0
        for p in parts:
            size = p.size // LANES
            out.append(total[at : at + size].reshape(p.shape).astype(F32))
            at += size
        return out

    swiglu_sums = sum_low((swiglu_down_grad, swiglu_up_grad, swiglu_gate_grad))
    mixed_gain_grad = jnp.sum(normed_grad * residual * inv_second, axis=(0, 1))
    weighted_second = normed_grad * mixed_gain
    second_stat = lax.psum(jnp.sum(weighted_second * residual, axis=-1, keepdims=True), "head")
    out_shard = lax.dynamic_slice_in_dim(cotangent, head_start, shard, 2).astype(F32)
    residual_grad = out_shard + inv_second * (
        weighted_second - residual * inv_second * inv_second * second_stat / width
    )
    mixer_grad_low = (mask * residual_grad).astype(BF16)
    mixer_grad = lax.all_gather(mixer_grad_low, "head", axis=2, tiled=True).reshape(rows, width)
    gated_grad = jnp.dot(mixer_grad, output_weight.T, preferred_element_type=F32)
    output_weight_grad = project(gated_low.T, mixer_grad)

    mixer_out_grad, gate_low, gain_part, shift_grads = gate_backward_call(
        heads, slots, segment, value_dim, key_dim, gated_grad, mixer, gate_pre, eff, gain_row
    )
    gate_low = gate_low.reshape(rows, heads * value_dim)
    gate_weight_grad = project(normed_first.T, gate_low)
    middle_sums = sum_low((output_weight_grad, gate_weight_grad))

    all_grads = exchange(
        to_units(shift_grads.astype(BF16).reshape(pairs, value_dim, key_dim), units), "seq"
    ).astype(F32)
    leaving = jnp.zeros_like(all_grads[0])
    leavings = [None] * seq_parts
    for p in reversed(range(seq_parts)):
        leavings[p] = leaving
        leaving = high(leaving, all_maps[p].T) + all_grads[p]
    state_grad = exchange(jnp.stack(leavings).astype(BF16), "seq").astype(F32)
    state_grad = state_grad.reshape(slots, heads, value_dim, key_dim)

    pre_low, tail, rim_grad, ab_grad, taps_grad, lane_grad = run_slots(
        functools.partial(delta_backward, heads, key_dim, value_dim),
        slots,
        (pre_all, rim_pre, ab_pre, ab_rows, query, key, value, inverse, value_rows, state_in, state_grad, mixer_out_grad),
        (kernel, lane_gates, col_gates),
        (
            sds((slots, segment, channels), BF16), sds((slots, RIM, channels), F32),
            sds((slots, RIM, channels), F32), sds((slots, segment, LANES), F32),
        ),
        (sds((8, channels), F32), sds((8, LANES), F32)),
        scratch=[
            pltpu.VMEM((segment + RIM, channels), F32),
            pltpu.VMEM((segment + 2 * RIM, channels), F32),
        ],
        order=(0, 1, 2, 3, 12, 13, 14, 4, 5, 6, 7, 8, 9, 10, 11),
    )
    rim_back = shifted(rim_grad[:, RIM - taps + 1 :, :], "seq", -1)
    last_rows = (tail[:, RIM - taps + 1 :, :] + rim_back).astype(BF16)
    pre_low = lax.dynamic_update_slice_in_dim(pre_low, last_rows, segment - taps + 1, 1)
    pre_low = pre_low.reshape(rows, channels)
    ab_low = ab_grad.reshape(rows, LANES).astype(BF16)

    first_part = (
        jnp.dot(pre_low, qkv_weight.T, preferred_element_type=F32)
        + jnp.dot(gate_low, gate_weight.T, preferred_element_type=F32)
        + jnp.dot(ab_low, ab_weight.T, preferred_element_type=F32)
    )
    first_sum = scatter_sum(first_part)
    pre_weight_grad = project(normed_first.T, pre_low)
    ab_weight_grad = project(normed_first.T, ab_low)[:, : 2 * heads]
    (pre_sums,) = sum_low((pre_weight_grad,))
    weighted_first = first_sum * lax.dynamic_slice_in_dim(input_gain, head_start, shard, 0)
    first_stat = lax.psum(jnp.sum(weighted_first * x_shard, axis=-1, keepdims=True), "head")
    input_grad = (
        residual_grad
        + inv_first * (weighted_first - x_shard * inv_first * inv_first * first_stat / width)
    )
    input_gain_grad = jnp.sum(first_sum * x_shard * inv_first, axis=(0, 1))
    gain_sum = lax.psum(gain_part[0], ("head", "seq"))
    value_share = value_dim // head_parts
    output_gain_grad = lax.dynamic_slice_in_dim(
        gain_sum, lax.axis_index("head") * value_share, value_share, 0
    )
    small = lax.psum(
        (input_gain_grad, ab_weight_grad, lane_grad[0, :heads], lane_grad[1, :heads], taps_grad[:taps], mixed_gain_grad),
        "seq",
    )
    taps_sum = small[4]
    return (
        block_out,
        input_grad,
        small[0],
        pre_sums[:, :split_key],
        pre_sums[:, split_key : 2 * split_key],
        pre_sums[:, 2 * split_key :],
        small[1][:, :heads],
        small[1][:, heads:],
        small[2],
        small[3],
        taps_sum[:, :split_key],
        taps_sum[:, split_key : 2 * split_key],
        taps_sum[:, 2 * split_key :],
        middle_sums[1],
        output_gain_grad,
        middle_sums[0],
        small[5],
        swiglu_sums[2],
        swiglu_sums[1],
        swiglu_sums[0],
    )


def gate_backward_call(heads, slots, segment, value_dim, key_dim, gated_grad, mixer, gate_pre, eff, gain_row):
    sds = jax.ShapeDtypeStruct
    gated_grad = gated_grad.reshape(slots, segment, -1)
    outs = [
        sds((slots, heads, segment, value_dim), F32),
        sds((slots, segment, heads * value_dim), BF16),
        sds((8, value_dim), F32),
        sds((slots, heads, value_dim, key_dim), F32),
    ]
    return pl.pallas_call(
        functools.partial(gate_backward, heads),
        grid=(slots,),
        in_specs=[
            by_slot(gated_grad.shape), by_slot(mixer.shape), by_slot(gate_pre.shape),
            whole(gain_row.shape), by_slot(eff.shape),
        ],
        out_specs=[by_slot(outs[0].shape), by_slot(outs[1].shape), whole(outs[2].shape), by_slot(outs[3].shape)],
        out_shape=outs,
        compiler_params=pltpu.CompilerParams(vmem_limit_bytes=VMEM_LIMIT),
    )(gated_grad, mixer, gate_pre, gain_row, eff)


def solution(mesh):
    seq, cols, lines = P(None, "seq", None), P(None, "head"), P("head", None)
    one = P("head")
    placed = (
        seq, P(), P(), cols, cols, cols, cols, cols, one, one, cols, cols, cols, cols, P(), lines, one,
        cols, cols, lines, seq,
    )
    both = P(None, "seq", "head")
    return jax.shard_map(
        per_device,
        mesh=mesh,
        in_specs=placed,
        out_specs=(
            both, both, one, cols, cols, cols, cols, cols, one, one, cols, cols, cols, cols, one, lines,
            one, cols, cols, lines,
        ),
        check_vma=False,
    )
```

```python
import functools

import jax
import jax.numpy as jnp
from jax import lax
from jax.experimental import pallas as pl
from jax.experimental.pallas import tpu as pltpu
from jax.sharding import PartitionSpec as P

NORM_EPSILON = 1e-05
UNIT_EPSILON = 1e-06
RIM = 8
LANES = 128
F32 = jnp.float32
BF16 = jnp.bfloat16
VMEM_LIMIT = 56 * 1024 * 1024

NN = (((1,), (0,)), ((), ()))
NT = (((1,), (1,)), ((), ()))
TN = (((0,), (0,)), ((), ()))


def split(x):
    high = x.astype(BF16)
    return high, (x - high.astype(F32)).astype(BF16)


def raw(a, b, dims):
    return lax.dot_general(a, b, dims, preferred_element_type=F32)


def mm(a, b, dims=NN):
    a_high, a_low = a if isinstance(a, tuple) else (a, None)
    b_high, b_low = b if isinstance(b, tuple) else (b, None)
    total = raw(a_high, b_high, dims)
    if a_low is not None:
        total = total + raw(a_low, b_high, dims)
    if b_low is not None:
        total = total + raw(a_high, b_low, dims)
    return total


def sigmoid(x):
    return 1.0 / (1.0 + jnp.exp(-x))


def softplus(x):
    return jnp.maximum(x, 0.0) + jnp.log1p(jnp.exp(-jnp.abs(x)))


def grid_masks(size):
    row = lax.broadcasted_iota(jnp.int32, (size, size), 0)
    col = lax.broadcasted_iota(jnp.int32, (size, size), 1)
    return row, col


def unit_inverse(lower, row, col):
    size = lower.shape[0]
    base = 8
    same = (row // base) == (col // base)
    block = jnp.where(same, lower, 0.0)
    one = split(block)
    square = mm(one, one)
    square_parts = split(square)
    fourth = mm(square_parts, square_parts)
    inverse = jnp.where(row == col, 1.0, 0.0) - block + square - mm(one, square_parts)
    inverse = inverse + mm(split(inverse), split(fourth))
    while base < size:
        inside = (row // (2 * base)) == (col // (2 * base))
        apart = (row // base) != (col // base)
        off = split(jnp.where(inside & apart, lower, 0.0))
        parts = split(inverse)
        inverse = inverse - mm(split(mm(parts, off)), parts)
        base *= 2
    return inverse


def gates_of(ab, rate, bias):
    return -rate * softplus(ab + bias), sigmoid(ab)


def decay_of(log_col, log_row, row, col):
    seen = row >= col
    cum_col = jnp.sum(jnp.where(seen, log_row, 0.0), axis=1, keepdims=True)
    cum_row = jnp.sum(jnp.where(row <= col, log_col, 0.0), axis=0, keepdims=True)
    end = jnp.sum(log_row, axis=1, keepdims=True)
    decayed = jnp.where(seen, jnp.exp(jnp.where(seen, cum_col - cum_row, 0.0)), 0.0)
    return cum_col, cum_row, end, decayed


def convolve(ext, taps_ref, length):
    taps = 4
    total = taps_ref[0:1, :] * ext[pl.ds(RIM - taps + 1, length), :]
    for tap in range(1, taps):
        total = total + taps_ref[tap : tap + 1, :] * ext[pl.ds(RIM - taps + 1 + tap, length), :]
    return total


def delta_forward(
    heads, key_dim, value_dim, pre_ref, rim_ref, ab_ref, abt_ref, taps_ref, lane_ref, col_ref,
    query_out, key_out, value_out, inverse_out, delta_out, mix_out, eff_out, map_out, shift_out, ext,
):
    length = pre_ref.shape[1]
    ext[0:RIM, :] = rim_ref[0]
    ext[RIM : RIM + length, :] = pre_ref[0].astype(F32)
    conv = convolve(ext, taps_ref, length)
    active = conv * sigmoid(conv)
    row, col = grid_masks(length)
    log_cols, strength_cols = gates_of(ab_ref[0], lane_ref[0:1, :], lane_ref[1:2, :])
    log_rows, strength_rows = gates_of(abt_ref[0], col_ref[0:8, 0:1], col_ref[8:16, 0:1])
    key_start = heads * key_dim
    value_start = 2 * heads * key_dim
    for h in range(heads):
        query_act = active[:, h * key_dim : (h + 1) * key_dim]
        key_act = active[:, key_start + h * key_dim : key_start + (h + 1) * key_dim]
        value_act = active[:, value_start + h * value_dim : value_start + (h + 1) * value_dim]
        query_scale = lax.rsqrt(jnp.sum(query_act * query_act, axis=1, keepdims=True) + UNIT_EPSILON)
        key_scale = lax.rsqrt(jnp.sum(key_act * key_act, axis=1, keepdims=True) + UNIT_EPSILON)
        query = (query_act * query_scale * key_dim ** (-0.5)).astype(BF16)
        key = (key_act * key_scale).astype(BF16)
        value = value_act.astype(BF16)
        query_out[0, h] = query
        key_out[0, h] = key
        value_out[0, h] = value
        strength = strength_cols[:, heads + h : heads + h + 1]
        strength_row = strength_rows[heads + h : heads + h + 1, :]
        cum_col, cum_row, end, decayed = decay_of(
            log_cols[:, h : h + 1], log_rows[h : h + 1, :], row, col
        )
        products = mm(key, key, NT)
        triangle = jnp.where(row > col, strength * decayed * products, 0.0)
        inverse = unit_inverse(triangle, row, col)
        inverse_out[0, h] = inverse
        scaled = inverse * strength_row
        delta = mm(split(scaled), value)
        mix = mm(split(scaled * jnp.exp(cum_row)), key)
        delta_out[0, h] = delta
        mix_out[0, h] = mix
        scores = split(decayed * mm(query, key, NT))
        eff_out[0, h] = jnp.exp(cum_col) * query.astype(F32) - mm(scores, split(mix))
        end_weight = jnp.exp(end - cum_col)
        small_row = lax.broadcasted_iota(jnp.int32, (key_dim, key_dim), 0)
        small_col = lax.broadcasted_iota(jnp.int32, (key_dim, key_dim), 1)
        moved = jnp.where(small_row == small_col, jnp.exp(end), 0.0)
        map_out[0, h] = moved - mm(split(mix * end_weight), key, TN)
        shift_out[0, h] = mm(split(delta * end_weight), key, TN)


def emit_forward(
    heads, query_ref, key_ref, ab_ref, abt_ref, lane_ref, col_ref, delta_ref, mix_ref, state_ref,
    gate_ref, gain_ref, rows_out, mixer_out, gated_out,
):
    length = query_ref.shape[2]
    value_dim = delta_ref.shape[3]
    row, col = grid_masks(length)
    log_cols, _ = gates_of(ab_ref[0], lane_ref[0:1, :], lane_ref[1:2, :])
    log_rows, _ = gates_of(abt_ref[0], col_ref[0:8, 0:1], col_ref[8:16, 0:1])
    for h in range(heads):
        query, key = query_ref[0, h], key_ref[0, h]
        cum_col, _, _, decayed = decay_of(log_cols[:, h : h + 1], log_rows[h : h + 1, :], row, col)
        scores = split(decayed * mm(query, key, NT))
        state = split(state_ref[0, h])
        rows = delta_ref[0, h] - mm(split(mix_ref[0, h]), state, NT)
        rows_out[0, h] = rows
        mixer = mm(scores, split(rows)) + jnp.exp(cum_col) * mm(query, state, NT)
        mixer_out[0, h] = mixer
        scale = lax.rsqrt(jnp.sum(mixer * mixer, axis=1, keepdims=True) / value_dim + NORM_EPSILON)
        gate = gate_ref[0, :, h * value_dim : (h + 1) * value_dim]
        gated = mixer * scale * gain_ref[0:1, :] * (gate * sigmoid(gate))
        gated_out[0, :, h * value_dim : (h + 1) * value_dim] = gated.astype(BF16)


def gate_backward(
    heads, gated_grad_ref, mixer_ref, gate_ref, gain_ref, eff_ref,
    mixer_grad_out, gate_grad_out, gain_grad_out, shift_grad_out,
):
    value_dim = mixer_ref.shape[3]

    @pl.when(pl.program_id(0) == 0)
    def _():
        gain_grad_out[...] = jnp.zeros_like(gain_grad_out)

    gain = gain_ref[0:1, :]
    for h in range(heads):
        here = slice(h * value_dim, (h + 1) * value_dim)
        grad = gated_grad_ref[0, :, here]
        mixer = mixer_ref[0, h]
        gate = gate_ref[0, :, here]
        scale = lax.rsqrt(jnp.sum(mixer * mixer, axis=1, keepdims=True) / value_dim + NORM_EPSILON)
        sig = sigmoid(gate)
        unit = mixer * scale
        gate_grad_out[0, :, here] = (
            grad * unit * gain * (sig * (1.0 + gate * (1.0 - sig)))
        ).astype(BF16)
        scaled_grad = grad * (gate * sig)
        gain_grad_out[0:1, :] += jnp.sum(scaled_grad * unit, axis=0, keepdims=True)
        unit_grad = scaled_grad * gain
        stat = jnp.sum(unit_grad * mixer, axis=1, keepdims=True) / value_dim
        mixer_grad = scale * (unit_grad - mixer * (scale * scale * stat))
        mixer_grad_out[0, h] = mixer_grad
        shift_grad_out[0, h] = mm(split(mixer_grad), split(eff_ref[0, h]), TN)


def delta_backward(
    heads, key_dim, value_dim, pre_ref, rim_ref, ab_ref, abt_ref, taps_ref, lane_ref, col_ref,
    query_ref, key_ref, value_ref, inverse_ref, rows_ref, state_ref, state_grad_ref, mixer_grad_ref,
    pre_grad_out, tail_out, rim_grad_out, ab_grad_out, taps_grad_out, lane_grad_out,
    ext, conv_grad,
):
    length = pre_ref.shape[1]
    taps = 4

    @pl.when(pl.program_id(0) == 0)
    def _():
        taps_grad_out[...] = jnp.zeros_like(taps_grad_out)
        lane_grad_out[...] = jnp.zeros_like(lane_grad_out)

    ext[0:RIM, :] = rim_ref[0]
    ext[RIM : RIM + length, :] = pre_ref[0].astype(F32)
    row, col = grid_masks(length)
    lane = lax.broadcasted_iota(jnp.int32, (length, LANES), 1)
    log_cols, strength_cols = gates_of(ab_ref[0], lane_ref[0:1, :], lane_ref[1:2, :])
    log_rows, strength_rows = gates_of(abt_ref[0], col_ref[0:8, 0:1], col_ref[8:16, 0:1])
    key_start = heads * key_dim
    value_start = 2 * heads * key_dim
    strict = row > col
    grads = jnp.zeros((length, LANES), F32)
    conv_grad[0:RIM, :] = jnp.zeros((RIM, conv_grad.shape[1]), F32)
    conv_grad[RIM + length : 2 * RIM + length, :] = jnp.zeros((RIM, conv_grad.shape[1]), F32)

    def activation(start, width):
        total = taps_ref[0:1, start : start + width] * ext[pl.ds(RIM - taps + 1, length), start : start + width]
        for tap in range(1, taps):
            total = total + (
                taps_ref[tap : tap + 1, start : start + width]
                * ext[pl.ds(RIM - taps + 1 + tap, length), start : start + width]
            )
        sig = sigmoid(total)
        return total * sig, sig * (1.0 + total * (1.0 - sig))

    def unit_back(grad, start, scale_by):
        act, slope = activation(start, key_dim)
        scale = lax.rsqrt(jnp.sum(act * act, axis=1, keepdims=True) + UNIT_EPSILON)
        inner = jnp.sum(act * grad, axis=1, keepdims=True)
        back = scale_by * scale * (grad - act * (scale * scale * inner))
        conv_grad[RIM : RIM + length, start : start + key_dim] = back * slope

    for h in range(heads):
        query, key, value = query_ref[0, h], key_ref[0, h], value_ref[0, h]
        query_f, key_f = query.astype(F32), key.astype(F32)
        strength = strength_cols[:, heads + h : heads + h + 1]
        cum_col, cum_row, end, decayed = decay_of(
            log_cols[:, h : h + 1], log_rows[h : h + 1, :], row, col
        )
        rise = jnp.exp(cum_col)
        end_weight = jnp.exp(end - cum_col)
        state_f, leaving_f = state_ref[0, h], state_grad_ref[0, h]
        state, leaving = split(state_f), split(leaving_f)
        rows = split(rows_ref[0, h])
        out_grad = split(mixer_grad_ref[0, h])
        products = mm(key, key, NT)
        scores = decayed * mm(query, key, NT)
        rows_grad = mm(split(scores), out_grad, TN) + end_weight * mm(key, leaving, NT)
        scores_grad = mm(out_grad, rows, NT)
        query_grad = rise * mm(out_grad, state)
        right_grad = mm(split(inverse_ref[0, h]), split(rows_grad), TN)
        key_state = mm(key, state, NT)
        triangle_grad = -jnp.where(strict, mm(split(right_grad), rows, NT), 0.0)
        value_grad = strength * right_grad
        strength_grad = jnp.sum(right_grad * (value.astype(F32) - rise * key_state), axis=1, keepdims=True)
        read_grad = -rise * value_grad
        cum_grad = jnp.sum(read_grad * key_state, axis=1, keepdims=True)
        key_grad = mm(split(read_grad), state)
        decayed_grad = triangle_grad * decayed
        strength_grad = strength_grad + jnp.sum(decayed_grad * products, axis=1, keepdims=True)
        weighted = strength * decayed_grad
        both = weighted * products + scores_grad * scores
        products_grad = split(weighted)
        overlap_grad = split(scores_grad * decayed)
        cum_grad = cum_grad + jnp.sum(both, axis=1, keepdims=True) + jnp.sum(query_f * query_grad, axis=1, keepdims=True)
        query_grad = query_grad + mm(overlap_grad, key)
        key_grad = (
            key_grad + mm(overlap_grad, query, TN) + mm(products_grad, key) + mm(products_grad, key, TN)
        )
        moved = mm(rows, leaving)
        key_grad = key_grad + end_weight * moved
        end_part = jnp.sum(moved * key_f, axis=1, keepdims=True) * end_weight
        cum_grad = cum_grad - end_part
        last = jnp.sum(end_part, axis=0, keepdims=True) + jnp.exp(end) * jnp.sum(
            jnp.sum(leaving_f * state_f, axis=1, keepdims=True), axis=0, keepdims=True
        )
        turned = jnp.sum(jnp.where(row == col, cum_grad, 0.0), axis=0, keepdims=True)
        turned = turned - jnp.sum(both, axis=0, keepdims=True)
        log_grad = jnp.sum(jnp.where(row <= col, turned, 0.0), axis=1, keepdims=True) + last
        grads = jnp.where(lane == h, log_grad, grads)
        grads = jnp.where(lane == heads + h, strength_grad, grads)
        unit_back(query_grad, h * key_dim, key_dim ** (-0.5))
        unit_back(key_grad, key_start + h * key_dim, 1.0)
        _, slope = activation(value_start + h * value_dim, value_dim)
        conv_grad[RIM : RIM + length, value_start + h * value_dim : value_start + (h + 1) * value_dim] = (
            value_grad * slope
        )

    softened = -lane_ref[0:1, :] * sigmoid(ab_ref[0] + lane_ref[1:2, :])
    decay_part = grads * softened
    is_log = lane < heads
    ab_grad_out[0] = jnp.where(is_log, decay_part, grads * strength_cols * (1.0 - strength_cols))
    lane_grad_out[0:1, :] += jnp.sum(jnp.where(is_log, grads * log_cols, 0.0), axis=0, keepdims=True)
    lane_grad_out[1:2, :] += jnp.sum(jnp.where(is_log, decay_part, 0.0), axis=0, keepdims=True)
    main = conv_grad[RIM : RIM + length, :]
    pre_grad = jnp.zeros_like(main)
    rim_grad = jnp.zeros((RIM, conv_grad.shape[1]), F32)
    for tap in range(taps):
        weight = taps_ref[tap : tap + 1, :]
        taps_grad_out[tap : tap + 1, :] += jnp.sum(
            main * ext[pl.ds(RIM - taps + 1 + tap, length), :], axis=0, keepdims=True
        )
        pre_grad = pre_grad + weight * conv_grad[pl.ds(RIM + taps - 1 - tap, length), :]
        rim_grad = rim_grad + weight * conv_grad[pl.ds(taps - 1 - tap, RIM), :]
    pre_grad_out[0] = pre_grad.astype(BF16)
    tail_out[0] = pre_grad[length - RIM : length, :]
    rim_grad_out[0] = rim_grad


def by_slot(shape):
    rest = len(shape) - 1
    return pl.BlockSpec((1,) + tuple(shape[1:]), lambda s: (s,) + (0,) * rest)


def whole(shape):
    return pl.BlockSpec(tuple(shape), lambda s: (0,) * len(shape))


def run_slots(body, slots, sliced, shared, sliced_out, shared_out=(), scratch=(), order=None):
    operands = list(sliced) + list(shared)
    specs = [by_slot(a.shape) for a in sliced] + [whole(a.shape) for a in shared]
    if order is not None:
        operands = [operands[i] for i in order]
        specs = [specs[i] for i in order]
    return pl.pallas_call(
        body,
        grid=(slots,),
        in_specs=specs,
        out_specs=[by_slot(o.shape) for o in sliced_out] + [whole(o.shape) for o in shared_out],
        out_shape=list(sliced_out) + list(shared_out),
        scratch_shapes=list(scratch),
        compiler_params=pltpu.CompilerParams(vmem_limit_bytes=VMEM_LIMIT),
    )(*operands)


MESH = pl.DeviceIdType.MESH


def remote(src, dst, send_sem, recv_sem, device):
    return pltpu.make_async_remote_copy(
        src_ref=src, dst_ref=dst, send_sem=send_sem, recv_sem=recv_sem, device_id=device, device_id_type=MESH
    )


def turn_to_row(column, row, col):
    return jnp.sum(jnp.where(row == col, column, 0.0), axis=0, keepdims=True)


def turn_to_column(line, row, col):
    return jnp.sum(jnp.where(row == col, line, 0.0), axis=1, keepdims=True)


def middle_kernel(
    slots, head_parts, gated, x_shard, out_grad, cot_shard, mask, out_weight, gate_weight, up_weight,
    down_weight, gain,
    block_out, normed_out, act_out, up_grad_out, gate_grad_out, mixer_grad_out, residual_grad_out,
    gated_grad_out, gain_grad_out,
    whole_part, part, low, from_core, to_line, from_line, residual, inverse, stat_own, stat_in, spread, grad_shard,
    core_send, core_recv, line_send, line_recv, stat_send, stat_recv,
    spread_line_send, spread_line_recv, spread_core_send, spread_core_recv,
):
    me = lax.axis_index("head")
    place = lax.axis_index("seq")
    lines = head_parts // 2
    core = lax.rem(me, 2)
    line = me // 2
    sibling = 2 * line + (1 - core)
    length, shard = x_shard.shape[1], x_shard.shape[2]
    width = shard * head_parts
    row, col = grid_masks(length)

    barrier = pltpu.get_barrier_semaphore()
    for away in range(1, head_parts):
        pl.semaphore_signal(
            barrier, inc=1, device_id=(place, lax.rem(me + away, head_parts)), device_id_type=MESH
        )
    pl.semaphore_wait(barrier, head_parts - 1)
    gain_grad_out[...] = jnp.zeros_like(gain_grad_out)

    def core_copy(kind, s, y):
        return remote(
            low.at[kind, s, y], from_core.at[kind, s, y],
            core_send.at[kind, s, y], core_recv.at[kind, s, y], (place, sibling),
        )

    def line_copy(kind, s, away):
        return remote(
            to_line.at[kind, s, away - 1], from_line.at[kind, s, away - 1],
            line_send.at[kind, s, away - 1], line_recv.at[kind, s, away - 1],
            (place, 2 * lax.rem(line + away, lines) + core),
        )

    def stat_copy(kind, s, away):
        return remote(
            stat_own.at[kind, s], stat_in.at[kind, s, away - 1],
            stat_send.at[kind, s, away - 1], stat_recv.at[kind, s, away - 1],
            (place, lax.rem(me + away, head_parts)),
        )

    def spread_line_copy(kind, s, away):
        return remote(
            spread.at[kind, s, me], spread.at[kind, s, me],
            spread_line_send.at[kind, s, away - 1], spread_line_recv.at[kind, s, away - 1],
            (place, 2 * lax.rem(line + away, lines) + core),
        )

    def spread_core_copy(kind, s, away):
        y = lax.rem(line + away, lines)
        return remote(
            spread.at[kind, s, 2 * y + core], spread.at[kind, s, 2 * y + core],
            spread_core_send.at[kind, s, away], spread_core_recv.at[kind, s, away], (place, sibling),
        )

    def spread_core_arrival(kind, s, away):
        y = lax.rem(line + away, lines)
        return remote(
            spread.at[kind, s, 2 * y + (1 - core)], spread.at[kind, s, 2 * y + (1 - core)],
            spread_core_send.at[kind, s, away], spread_core_recv.at[kind, s, away], (place, sibling),
        )

    def spread_line_arrival(kind, s, away):
        y = lax.rem(line + lines - away, lines)
        return remote(
            spread.at[kind, s, 2 * y + core], spread.at[kind, s, 2 * y + core],
            spread_line_send.at[kind, s, away - 1], spread_line_recv.at[kind, s, away - 1],
            (place, 2 * y + core),
        )

    def send_part(kind, s, value):
        for j in range(head_parts):
            whole_part[j] = value[:, j * shard : (j + 1) * shard]
        for y in range(lines):
            low[kind, s, y] = whole_part[2 * y + (1 - core)].astype(BF16)
            core_copy(kind, s, y).start()
            part[kind, s, y] = whole_part[2 * y + core]

    def join_core(kind, s):
        for y in range(lines):
            core_copy(kind, s, y).wait_recv()
        for away in range(1, lines):
            y = lax.rem(line + away, lines)
            joined = part[kind, s, y] + from_core[kind, s, y].astype(F32)
            to_line[kind, s, away - 1] = joined.astype(BF16)
            line_copy(kind, s, away).start()
        part[kind, s, line] = part[kind, s, line] + from_core[kind, s, line].astype(F32)

    def join_line(kind, s):
        total = part[kind, s, line]
        for away in range(1, lines):
            line_copy(kind, s, away).wait_recv()
            total = total + from_line[kind, s, away - 1].astype(F32)
        return total

    def send_stat(kind, s, column):
        stat_own[kind, s] = jnp.broadcast_to(turn_to_row(column, row, col), (8, length))
        for away in range(1, head_parts):
            stat_copy(kind, s, away).start()

    def join_stat(kind, s):
        total = stat_own[kind, s]
        for away in range(1, head_parts):
            stat_copy(kind, s, away).wait_recv()
            total = total + stat_in[kind, s, away - 1]
        return turn_to_column(total[0:1, :], row, col)

    def send_spread(kind, s, value):
        spread[kind, s, me] = value
        for away in range(1, lines):
            spread_line_copy(kind, s, away).start()
        spread_core_copy(kind, s, 0).start()

    def pass_spread(kind, s):
        for away in range(1, lines):
            spread_line_arrival(kind, s, lines - away).wait_recv()
            spread_core_copy(kind, s, away).start()

    def take_spread(kind, s):
        for away in range(lines):
            spread_core_arrival(kind, s, away).wait_recv()
        return jnp.concatenate([spread[kind, s, j] for j in range(head_parts)], axis=1)

    def attention(s):
        send_part(0, s, raw(gated[s], out_weight[...], NN))

    def rows_in(s):
        total = x_shard[s].astype(F32) + mask[s][:, 0:1] * join_line(0, s)
        residual[s] = total
        send_stat(0, s, jnp.sum(total * total, axis=1, keepdims=True))

    def norm_second(s):
        inv = lax.rsqrt(join_stat(0, s) / width + NORM_EPSILON)
        inverse[s] = jnp.broadcast_to(inv, (length, LANES))
        send_spread(0, s, (residual[s] * inv * gain[0:1, :]).astype(BF16))

    def swiglu(s):
        normed = take_spread(0, s)
        normed_out[s] = normed
        gate_values = raw(normed, gate_weight[...], NN)
        up_values = raw(normed, up_weight[...], NN)
        act_grad = raw(out_grad[s], down_weight[...], NT)
        sig = sigmoid(gate_values)
        silu = gate_values * sig
        act_out[s] = (silu * up_values).astype(BF16)
        up_grad = (act_grad * silu).astype(BF16)
        gate_grad = (act_grad * up_values * sig * (1.0 + gate_values * (1.0 - sig))).astype(BF16)
        up_grad_out[s] = up_grad
        gate_grad_out[s] = gate_grad
        send_part(1, s, raw(up_grad, up_weight[...], NT) + raw(gate_grad, gate_weight[...], NT))

    def swiglu_out(s):
        send_part(2, s, raw(act_out[s], down_weight[...], NN))

    def block_rows(s):
        block_out[s] = (residual[s] + mask[s][:, 0:1] * join_line(2, s)).astype(BF16)

    def norm_back(s):
        grad = join_line(1, s)
        inv = inverse[s][:, 0:1]
        gain_grad_out[0:1, :] += jnp.sum(grad * residual[s] * inv, axis=0, keepdims=True)
        weighted = grad * gain[0:1, :]
        grad_shard[s] = weighted
        send_stat(1, s, jnp.sum(weighted * residual[s], axis=1, keepdims=True))

    def residual_back(s):
        stat = join_stat(1, s) / width
        inv = inverse[s][:, 0:1]
        grad = cot_shard[s].astype(F32) + inv * (grad_shard[s] - residual[s] * (inv * inv * stat))
        residual_grad_out[s] = grad
        send_spread(1, s, (mask[s][:, 0:1] * grad).astype(BF16))

    def mixer_rows(s):
        grad = take_spread(1, s)
        mixer_grad_out[s] = grad
        gated_grad_out[s] = raw(grad, out_weight[...], NT)

    stages = (
        (10, mixer_rows),
        (9, functools.partial(pass_spread, 1)),
        (8, residual_back),
        (7, norm_back),
        (6, functools.partial(join_core, 1)),
        (8, block_rows),
        (7, functools.partial(join_core, 2)),
        (4, functools.partial(pass_spread, 0)),
        (3, norm_second),
        (2, rows_in),
        (1, functools.partial(join_core, 0)),
        (0, attention),
        (5, swiglu),
        (6, swiglu_out),
    )

    def step(t, carry):
        for offset, stage in stages:
            s = t - offset

            @pl.when((s >= 0) & (s < slots))
            def _(stage=stage, s=s):
                stage(s)

        return carry

    lax.fori_loop(0, slots + 10, step, 0)

    def drain(s, carry):
        for kind in range(3):
            for y in range(lines):
                core_copy(kind, s, y).wait_send()
            for away in range(1, lines):
                line_copy(kind, s, away).wait_send()
        for kind in range(2):
            for away in range(1, head_parts):
                stat_copy(kind, s, away).wait_send()
            for away in range(1, lines):
                spread_line_copy(kind, s, away).wait_send()
            for away in range(lines):
                spread_core_copy(kind, s, away).wait_send()
        return carry

    lax.fori_loop(0, slots, drain, 0)


def middle_call(
    head_parts, gated, x_shard, out_grad, cot_shard, mask, out_weight, gate_weight, up_weight, down_weight, gain
):
    slots, length, shard = x_shard.shape
    width = shard * head_parts
    hidden = gate_weight.shape[1]
    lines = head_parts // 2
    sds = jax.ShapeDtypeStruct
    vmem = pl.BlockSpec(memory_space=pltpu.VMEM)
    dma = pltpu.SemaphoreType.DMA
    outs = (
        sds((slots, length, shard), BF16), sds((slots, length, width), BF16),
        sds((slots, length, hidden), BF16), sds((slots, length, hidden), BF16),
        sds((slots, length, hidden), BF16), sds((slots, length, width), BF16),
        sds((slots, length, shard), F32), sds((slots, length, gated.shape[2]), F32), sds((8, shard), F32),
    )
    return pl.pallas_call(
        functools.partial(middle_kernel, slots, head_parts),
        in_specs=[vmem] * 10,
        out_specs=[vmem] * len(outs),
        out_shape=outs,
        scratch_shapes=[
            pltpu.VMEM((head_parts, length, shard), F32),
            pltpu.VMEM((3, slots, lines, length, shard), F32),
            pltpu.VMEM((3, slots, lines, length, shard), BF16),
            pltpu.VMEM((3, slots, lines, length, shard), BF16),
            pltpu.VMEM((3, slots, lines - 1, length, shard), BF16),
            pltpu.VMEM((3, slots, lines - 1, length, shard), BF16),
            pltpu.VMEM((slots, length, shard), F32),
            pltpu.VMEM((slots, length, LANES), F32),
            pltpu.VMEM((2, slots, 8, length), F32),
            pltpu.VMEM((2, slots, head_parts - 1, 8, length), F32),
            pltpu.VMEM((2, slots, head_parts, length, shard), BF16),
            pltpu.VMEM((slots, length, shard), F32),
            dma((3, slots, lines)), dma((3, slots, lines)),
            dma((3, slots, lines - 1)), dma((3, slots, lines - 1)),
            dma((2, slots, head_parts - 1)), dma((2, slots, head_parts - 1)),
            dma((2, slots, lines - 1)), dma((2, slots, lines - 1)),
            dma((2, slots, lines)), dma((2, slots, lines)),
        ],
        compiler_params=pltpu.CompilerParams(
            collective_id=0, has_side_effects=True, vmem_limit_bytes=VMEM_LIMIT
        ),
        cost_estimate=pl.CostEstimate(flops=12 * 10**9, bytes_accessed=30 * 10**6, transcendentals=0),
    )(gated, x_shard, out_grad, cot_shard, mask, out_weight, gate_weight, up_weight, down_weight, gain)


def ring_kernel(parts, count, *refs):
    ins, outs, held = refs[:count], refs[count : 2 * count], refs[2 * count : 3 * count]
    send, recv, spread_send, spread_recv = refs[3 * count :]
    index = lax.axis_index("seq")
    other = lax.axis_index("head")
    side = lax.rem(index, 2)
    level = index // 2
    levels = parts // 2
    position = jnp.where(side == 1, level, parts - 1 - level)
    up = jnp.where(side == 1, jnp.where(level == levels - 1, index - 1, index + 2),
                   jnp.where(level == 0, index + 1, index - 2))
    down = jnp.where(side == 1, jnp.where(level == 0, index - 1, index - 2),
                     jnp.where(level == levels - 1, index + 1, index + 2))
    targets = (up, down)
    barrier = pltpu.get_barrier_semaphore()
    for target in targets:
        pl.semaphore_signal(barrier, inc=1, device_id=(target, other), device_id_type=MESH)

    def rows_of(a, way, chunk):
        size = ins[a].shape[0] // (2 * parts)
        return pl.ds(pl.multiple_of((chunk * 2 + way) * size, size), size)

    def chunk_at(way, step):
        if way == 0:
            return lax.rem(position - step + 2 * parts, parts)
        return lax.rem(position + step + 2 * parts, parts)

    def sum_copy(a, way, step):
        return remote(
            held[a].at[way, step], held[a].at[way, step + 1], send.at[a, way], recv.at[a, way, step],
            (targets[way], other),
        )

    def spread_copy(a, way, step):
        block = rows_of(a, way, chunk_at(way, step - 1))
        return remote(
            outs[a].at[block, :], outs[a].at[block, :], spread_send.at[a, way], spread_recv.at[a, way, step],
            (targets[way], other),
        )

    def spread_arrival(a, way, step):
        block = rows_of(a, way, chunk_at(way, step))
        return remote(
            outs[a].at[block, :], outs[a].at[block, :], spread_send.at[a, way], spread_recv.at[a, way, step],
            (targets[way], other),
        )

    lanes = [(a, way) for a in range(count) for way in range(2)]
    for a, way in lanes:
        held[a][way, 0] = ins[a][rows_of(a, way, chunk_at(way, 0)), :]
    pl.semaphore_wait(barrier, 2)
    for a, way in lanes:
        sum_copy(a, way, 0).start()

    def add(step, a, way):
        sum_copy(a, way, step).wait_recv()
        mine = ins[a][rows_of(a, way, chunk_at(way, step + 1)), :].astype(F32)
        return (held[a][way, step + 1].astype(F32) + mine).astype(BF16)

    def one(step, carry):
        for a, way in lanes:
            held[a][way, step + 1] = add(step, a, way)
            sum_copy(a, way, step).wait_send()
            sum_copy(a, way, step + 1).start()
        return carry

    lax.fori_loop(0, parts - 2, one, 0)
    last = parts - 2
    for a, way in lanes:
        outs[a][rows_of(a, way, chunk_at(way, parts - 1)), :] = add(last, a, way)
        sum_copy(a, way, last).wait_send()
        spread_copy(a, way, 0).start()

    def pass_on(step, carry):
        for a, way in lanes:
            spread_arrival(a, way, step).wait_recv()
            spread_copy(a, way, step).wait_send()
            spread_copy(a, way, step + 1).start()
        return carry

    lax.fori_loop(0, parts - 2, pass_on, 0)
    for a, way in lanes:
        spread_arrival(a, way, last).wait_recv()
        spread_copy(a, way, last).wait_send()


def ring_sum(parts, arrays):
    count = len(arrays)
    unit = 32 * parts
    padded = [jnp.pad(a, ((0, -a.shape[0] % unit), (0, 0))) for a in arrays]
    vmem = pl.BlockSpec(memory_space=pltpu.VMEM)
    dma = pltpu.SemaphoreType.DMA
    sds = jax.ShapeDtypeStruct
    sums = pl.pallas_call(
        functools.partial(ring_kernel, parts, count),
        in_specs=[vmem] * count,
        out_specs=[vmem] * count,
        out_shape=[sds(a.shape, BF16) for a in padded],
        scratch_shapes=[
            pltpu.VMEM((2, parts, a.shape[0] // (2 * parts), a.shape[1]), BF16) for a in padded
        ]
        + [dma((count, 2)), dma((count, 2, parts - 1)), dma((count, 2)), dma((count, 2, parts - 1))],
        compiler_params=pltpu.CompilerParams(
            collective_id=1, has_side_effects=True, vmem_limit_bytes=VMEM_LIMIT
        ),
        cost_estimate=pl.CostEstimate(flops=10**8, bytes_accessed=500 * 10**6, transcendentals=0),
    )(*padded)
    return [t[: a.shape[0]] for t, a in zip(sums, arrays)]


def shifted(block, axis, distance):
    devices = range(lax.axis_size(axis))
    route = [(i - distance, i) for i in devices if i - distance in devices]
    return lax.ppermute(block, axis, route)


def to_units(parts, units):
    pairs, value_dim, key_dim = parts.shape
    share = units // pairs
    return parts.reshape(units, value_dim // share, key_dim)


def exchange(parts, axis):
    return lax.all_to_all(parts, axis, 0, 0, tiled=True)


def per_device(
    hidden_in, lengths, input_gain, query_weight, key_weight, value_weight, alpha_weight, beta_weight,
    decay_log, decay_bias, query_kernel, key_kernel, value_kernel, gate_weight, output_gain,
    output_weight, mixed_gain, swiglu_gate, swiglu_up, swiglu_down, cotangent,
):
    slots, segment, width = hidden_in.shape
    rows = slots * segment
    heads = decay_log.shape[0]
    key_dim = query_kernel.shape[1] // heads
    value_dim = value_kernel.shape[1] // heads
    taps = query_kernel.shape[0]
    split_key = heads * key_dim
    channels = 2 * split_key + heads * value_dim
    head_parts = lax.axis_size("head")
    seq_parts = lax.axis_size("seq")
    shard = width // head_parts
    head_start = lax.axis_index("head") * shard
    pairs = slots * heads
    sds = jax.ShapeDtypeStruct

    position = lax.axis_index("seq") * segment + jnp.arange(segment)
    mask = (position[None, :] < lengths[:, None]).astype(F32)[:, :, None]

    def norm_rows(x):
        inv = lax.rsqrt(jnp.mean(x * x, axis=-1, keepdims=True) + NORM_EPSILON)
        return inv, (x * inv * input_gain).astype(BF16)

    rim_in = shifted(hidden_in[:, segment - taps + 1 :, :], "seq", 1)
    x_full = hidden_in.astype(F32)
    inv_first, normed_first = norm_rows(x_full)
    normed_first = normed_first.reshape(rows, width)
    x_shard = lax.dynamic_slice_in_dim(x_full, head_start, shard, 2)
    qkv_weight = jnp.concatenate([query_weight, key_weight, value_weight], axis=1)
    ab_weight = jnp.concatenate(
        [alpha_weight, beta_weight, jnp.zeros((width, LANES - 2 * heads), BF16)], axis=1
    )

    def project(x, weight):
        return jnp.dot(x, weight, preferred_element_type=F32)

    pre_all = project(normed_first, qkv_weight).astype(BF16).reshape(slots, segment, channels)
    gate_pre = project(normed_first, gate_weight).reshape(slots, segment, -1)
    ab_pre = project(normed_first, ab_weight).reshape(slots, segment, LANES)
    ab_rows = jnp.swapaxes(ab_pre[:, :, :8], 1, 2)
    _, rim_normed = norm_rows(rim_in.astype(F32))
    rim_pre = project(rim_normed.reshape(slots * (taps - 1), width), qkv_weight).astype(BF16).astype(F32)
    rim_pre = jnp.pad(rim_pre.reshape(slots, taps - 1, channels), ((0, 0), (RIM - taps + 1, 0), (0, 0)))
    kernel = jnp.concatenate([query_kernel, key_kernel, value_kernel], axis=1).astype(F32)
    kernel = jnp.pad(kernel, ((0, 8 - taps), (0, 0)))
    rate = jnp.exp(decay_log)
    pad_heads = lambda v: jnp.pad(v, (0, LANES - heads))
    lane_gates = jnp.pad(jnp.stack([pad_heads(rate), pad_heads(decay_bias)]), ((0, 6), (0, 0)))
    pad_rows = lambda v: jnp.broadcast_to(jnp.pad(v, (0, 8 - heads))[:, None], (8, LANES))
    col_gates = jnp.concatenate([pad_rows(rate), pad_rows(decay_bias)], axis=0)
    gain_row = jnp.broadcast_to(output_gain[None, :], (8, value_dim))

    per_pair = lambda *tail: sds((slots, heads) + tail, F32)
    low_pair = lambda *tail: sds((slots, heads) + tail, BF16)
    query, key, value, inverse, delta, mix, eff, maps, shifts = run_slots(
        functools.partial(delta_forward, heads, key_dim, value_dim),
        slots,
        (pre_all, rim_pre, ab_pre, ab_rows),
        (kernel, lane_gates, col_gates),
        (
            low_pair(segment, key_dim), low_pair(segment, key_dim), low_pair(segment, value_dim),
            per_pair(segment, segment), per_pair(segment, value_dim), per_pair(segment, key_dim),
            per_pair(segment, key_dim), per_pair(key_dim, key_dim), per_pair(value_dim, key_dim),
        ),
        scratch=[pltpu.VMEM((segment + RIM, channels), F32)],
    )

    units = seq_parts
    share = units // pairs
    own_maps = jnp.repeat(maps.astype(BF16).reshape(pairs, key_dim, key_dim), share, axis=0)
    own_shifts = to_units(shifts.astype(BF16).reshape(pairs, value_dim, key_dim), units)
    all_maps = exchange(own_maps, "seq").astype(F32)
    all_shifts = exchange(own_shifts, "seq").astype(F32)
    high = functools.partial(jnp.dot, precision=lax.Precision.HIGHEST, preferred_element_type=F32)
    state = jnp.zeros_like(all_shifts[0])
    states = []
    for p in range(seq_parts):
        states.append(state)
        state = high(state, all_maps[p]) + all_shifts[p]
    state_in = exchange(jnp.stack(states).astype(BF16), "seq").astype(F32)
    state_in = state_in.reshape(slots, heads, value_dim, key_dim)

    value_rows, mixer, gated = run_slots(
        functools.partial(emit_forward, heads),
        slots,
        (query, key, ab_pre, ab_rows, delta, mix, state_in, gate_pre),
        (lane_gates, col_gates, gain_row),
        (
            per_pair(segment, value_dim), per_pair(segment, value_dim),
            sds((slots, segment, heads * value_dim), BF16),
        ),
        order=(0, 1, 2, 3, 8, 9, 4, 5, 6, 7, 10),
    )
    gated_low = gated.reshape(rows, heads * value_dim)

    def scatter_sum(part):
        low = part.astype(BF16).reshape(slots, segment, width)
        return lax.psum_scatter(low, "head", scatter_dimension=2, tiled=True).astype(F32)

    out_grad = jnp.where(mask > 0, cotangent, jnp.zeros_like(cotangent))
    cot_shard = lax.dynamic_slice_in_dim(cotangent, head_start, shard, 2)
    (
        block_out, normed_second, activation, upward_grad, gate_grad, mixer_grad, residual_grad, gated_grad,
        mixed_gain_part,
    ) = middle_call(
        head_parts, gated, lax.dynamic_slice_in_dim(hidden_in, head_start, shard, 2), out_grad, cot_shard,
        jnp.broadcast_to(mask, (slots, segment, LANES)), output_weight, swiglu_gate, swiglu_up, swiglu_down,
        jnp.broadcast_to(mixed_gain[None, :], (8, shard)),
    )
    gated_grad = gated_grad.reshape(rows, heads * value_dim)

    def flat(a):
        return a.reshape(rows, a.shape[2])

    def weight_grad(left, right):
        return lax.dot_general(left, right, TN, preferred_element_type=F32).astype(BF16)

    normed_second = flat(normed_second)
    swiglu_down_grad = weight_grad(flat(activation), flat(out_grad))
    swiglu_grads = jnp.concatenate(
        [weight_grad(normed_second, flat(upward_grad)), weight_grad(normed_second, flat(gate_grad))], axis=1
    )
    output_weight_grad = weight_grad(gated_low, flat(mixer_grad))

    mixer_out_grad, gate_low, gain_part, shift_grads = gate_backward_call(
        heads, slots, segment, value_dim, key_dim, gated_grad, mixer, gate_pre, eff, gain_row
    )
    gate_low = gate_low.reshape(rows, heads * value_dim)

    all_grads = exchange(
        to_units(shift_grads.astype(BF16).reshape(pairs, value_dim, key_dim), units), "seq"
    ).astype(F32)
    leaving = jnp.zeros_like(all_grads[0])
    leavings = [None] * seq_parts
    for p in reversed(range(seq_parts)):
        leavings[p] = leaving
        leaving = high(leaving, all_maps[p].T) + all_grads[p]
    state_grad = exchange(jnp.stack(leavings).astype(BF16), "seq").astype(F32)
    state_grad = state_grad.reshape(slots, heads, value_dim, key_dim)

    pre_low, tail, rim_grad, ab_grad, taps_grad, lane_grad = run_slots(
        functools.partial(delta_backward, heads, key_dim, value_dim),
        slots,
        (pre_all, rim_pre, ab_pre, ab_rows, query, key, value, inverse, value_rows, state_in, state_grad, mixer_out_grad),
        (kernel, lane_gates, col_gates),
        (
            sds((slots, segment, channels), BF16), sds((slots, RIM, channels), F32),
            sds((slots, RIM, channels), F32), sds((slots, segment, LANES), F32),
        ),
        (sds((8, channels), F32), sds((8, LANES), F32)),
        scratch=[
            pltpu.VMEM((segment + RIM, channels), F32),
            pltpu.VMEM((segment + 2 * RIM, channels), F32),
        ],
        order=(0, 1, 2, 3, 12, 13, 14, 4, 5, 6, 7, 8, 9, 10, 11),
    )
    rim_back = shifted(rim_grad[:, RIM - taps + 1 :, :], "seq", -1)
    last_rows = (tail[:, RIM - taps + 1 :, :] + rim_back).astype(BF16)
    pre_low = lax.dynamic_update_slice_in_dim(pre_low, last_rows, segment - taps + 1, 1)
    pre_low = pre_low.reshape(rows, channels)
    ab_low = ab_grad.reshape(rows, LANES).astype(BF16)

    first_part = (
        jnp.dot(pre_low, qkv_weight.T, preferred_element_type=F32)
        + jnp.dot(gate_low, gate_weight.T, preferred_element_type=F32)
        + jnp.dot(ab_low, ab_weight.T, preferred_element_type=F32)
    )
    first_sum = scatter_sum(first_part)
    weighted_first = first_sum * lax.dynamic_slice_in_dim(input_gain, head_start, shard, 0)
    first_stat = lax.psum(jnp.sum(weighted_first * x_shard, axis=-1, keepdims=True), "head")
    input_grad = (
        residual_grad
        + inv_first * (weighted_first - x_shard * inv_first * inv_first * first_stat / width)
    )
    input_gain_grad = jnp.sum(first_sum * x_shard * inv_first, axis=(0, 1))
    small_rows = jnp.concatenate(
        [
            taps_grad[:taps].reshape(-1), gain_part[0], lane_grad[:2].reshape(-1), mixed_gain_part[0],
            lax.dot_general(ab_low, normed_first, TN, preferred_element_type=F32)[: 2 * heads].reshape(-1),
        ]
    )
    sizes = (taps * channels, value_dim, 2 * LANES, shard, 2 * heads * width)
    small_rows = jnp.pad(small_rows, (0, -small_rows.shape[0] % width)).reshape(-1, width)
    first_grads = jnp.concatenate(
        [weight_grad(normed_first, pre_low), weight_grad(normed_first, gate_low)], axis=1
    )
    line_grads = jnp.concatenate([swiglu_down_grad, output_weight_grad, small_rows.astype(BF16)], axis=0)
    swiglu_sum, first_grad_sum, line_sum = ring_sum(seq_parts, (swiglu_grads, first_grads, line_grads))
    hidden = swiglu_gate.shape[1]
    small_sum = line_sum[hidden + heads * value_dim :].reshape(-1).astype(F32)
    pieces, at = [], 0
    for size in sizes:
        pieces.append(small_sum[at : at + size])
        at += size
    taps_sum = pieces[0].reshape(taps, channels)
    lane_sum = pieces[2].reshape(2, LANES)
    ab_sum = pieces[4].reshape(2 * heads, width).T
    input_gain_sum = lax.psum(input_gain_grad, "seq")
    gain_sum = lax.psum(pieces[1], "head")
    value_share = value_dim // head_parts
    output_gain_grad = lax.dynamic_slice_in_dim(
        gain_sum, lax.axis_index("head") * value_share, value_share, 0
    )
    wide = first_grad_sum.astype(F32)
    lines = line_sum.astype(F32)
    both = swiglu_sum.astype(F32)
    return (
        block_out,
        input_grad,
        input_gain_sum,
        wide[:, :split_key],
        wide[:, split_key : 2 * split_key],
        wide[:, 2 * split_key : channels],
        ab_sum[:, :heads],
        ab_sum[:, heads:],
        lane_sum[0, :heads],
        lane_sum[1, :heads],
        taps_sum[:, :split_key],
        taps_sum[:, split_key : 2 * split_key],
        taps_sum[:, 2 * split_key :],
        wide[:, channels:],
        output_gain_grad,
        lines[hidden : hidden + heads * value_dim],
        pieces[3],
        both[:, hidden:],
        both[:, :hidden],
        lines[:hidden],
    )


def gate_backward_call(heads, slots, segment, value_dim, key_dim, gated_grad, mixer, gate_pre, eff, gain_row):
    sds = jax.ShapeDtypeStruct
    gated_grad = gated_grad.reshape(slots, segment, -1)
    outs = [
        sds((slots, heads, segment, value_dim), F32),
        sds((slots, segment, heads * value_dim), BF16),
        sds((8, value_dim), F32),
        sds((slots, heads, value_dim, key_dim), F32),
    ]
    return pl.pallas_call(
        functools.partial(gate_backward, heads),
        grid=(slots,),
        in_specs=[
            by_slot(gated_grad.shape), by_slot(mixer.shape), by_slot(gate_pre.shape),
            whole(gain_row.shape), by_slot(eff.shape),
        ],
        out_specs=[by_slot(outs[0].shape), by_slot(outs[1].shape), whole(outs[2].shape), by_slot(outs[3].shape)],
        out_shape=outs,
        compiler_params=pltpu.CompilerParams(vmem_limit_bytes=VMEM_LIMIT),
    )(gated_grad, mixer, gate_pre, gain_row, eff)


def solution(mesh):
    seq, cols, lines = P(None, "seq", None), P(None, "head"), P("head", None)
    one = P("head")
    placed = (
        seq, P(), P(), cols, cols, cols, cols, cols, one, one, cols, cols, cols, cols, P(), lines, one,
        cols, cols, lines, seq,
    )
    both = P(None, "seq", "head")
    return jax.shard_map(
        per_device,
        mesh=mesh,
        in_specs=placed,
        out_specs=(
            both, both, one, cols, cols, cols, cols, cols, one, one, cols, cols, cols, cols, one, lines,
            one, cols, cols, lines,
        ),
        check_vma=False,
    )
```

```python
import functools
import types

import jax
import jax.numpy as jnp
from jax import lax
from jax.experimental import pallas as pl
from jax.experimental.pallas import tpu as pltpu
from jax.sharding import PartitionSpec as P

NORM_EPSILON = 1e-05
UNIT_EPSILON = 1e-06
RIM = 8
LANES = 128
F32 = jnp.float32
BF16 = jnp.bfloat16
VMEM_LIMIT = 58 * 1024 * 1024

NN = (((1,), (0,)), ((), ()))
NT = (((1,), (1,)), ((), ()))
TN = (((0,), (0,)), ((), ()))


def split(x):
    high = x.astype(BF16)
    return high, (x - high.astype(F32)).astype(BF16)


def raw(a, b, dims):
    return lax.dot_general(a, b, dims, preferred_element_type=F32)


def mm(a, b, dims=NN):
    a_high, a_low = a if isinstance(a, tuple) else (a, None)
    b_high, b_low = b if isinstance(b, tuple) else (b, None)
    total = raw(a_high, b_high, dims)
    if a_low is not None:
        total = total + raw(a_low, b_high, dims)
    if b_low is not None:
        total = total + raw(a_high, b_low, dims)
    return total


def sigmoid(x):
    return 1.0 / (1.0 + jnp.exp(-x))


def softplus(x):
    return jnp.maximum(x, 0.0) + jnp.log1p(jnp.exp(-jnp.abs(x)))


def grid_masks(size):
    row = lax.broadcasted_iota(jnp.int32, (size, size), 0)
    col = lax.broadcasted_iota(jnp.int32, (size, size), 1)
    return row, col


def join(a, b, dims=NN):
    return raw(
        jnp.concatenate([a[0], a[1], a[0]], axis=1), jnp.concatenate([b[0], b[0], b[1]], axis=0), dims
    )


def unit_inverse(lower):
    size = lower.shape[0]
    if size > LANES:
        half = size // 2
        first = unit_inverse(lower[:half, :half])
        second = unit_inverse(lower[half:, half:])
        corner = -join(split(join(split(second), split(lower[half:, :half]))), split(first))
        top = jnp.concatenate([first, jnp.zeros((half, half), F32)], axis=1)
        return jnp.concatenate([top, jnp.concatenate([corner, second], axis=1)], axis=0)
    row, col = grid_masks(size)
    apart = row ^ col
    base = 8
    block = jnp.where(apart < base, lower, 0.0)
    one = split(block)
    square = join(one, one)
    square_parts = split(square)
    fourth = join(square_parts, square_parts)
    inverse = jnp.where(row == col, 1.0, 0.0) - block + square - join(one, square_parts)
    inverse = inverse + join(split(inverse), split(fourth))
    while base < size:
        off = split(jnp.where((apart >= base) & (apart < 2 * base), lower, 0.0))
        parts = split(inverse)
        inverse = inverse - join(split(join(parts, off)), parts)
        base *= 2
    return inverse


def gates_of(ab, rate, bias):
    return -rate * softplus(ab + bias), sigmoid(ab)


def decay_of(log_col, log_row, row, col):
    seen = row >= col
    cum_col = jnp.sum(jnp.where(seen, log_row, 0.0), axis=1, keepdims=True)
    cum_row = jnp.sum(jnp.where(row <= col, log_col, 0.0), axis=0, keepdims=True)
    end = jnp.sum(log_row, axis=1, keepdims=True)
    decayed = jnp.where(seen, jnp.exp(jnp.where(seen, cum_col - cum_row, 0.0)), 0.0)
    return cum_col, cum_row, end, decayed


def convolve(ext, taps_ref, length):
    taps = 4
    total = taps_ref[0:1, :] * ext[pl.ds(RIM - taps + 1, length), :]
    for tap in range(1, taps):
        total = total + taps_ref[tap : tap + 1, :] * ext[pl.ds(RIM - taps + 1 + tap, length), :]
    return total


MESH = pl.DeviceIdType.MESH


def remote(src, dst, send_sem, recv_sem, device):
    return pltpu.make_async_remote_copy(
        src_ref=src, dst_ref=dst, send_sem=send_sem, recv_sem=recv_sem, device_id=device, device_id_type=MESH
    )


def turn_to_row(column, row, col):
    return jnp.sum(jnp.where(row == col, column, 0.0), axis=0, keepdims=True)


def turn_to_column(line, row, col):
    return jnp.sum(jnp.where(row == col, line, 0.0), axis=1, keepdims=True)


def staged_call(kernel, operands, outs, scratch, collective_id, late=(), leaving=(), kept=(), slots=0, flops=10**10):
    dma = pltpu.SemaphoreType.DMA
    order = [i for group in late for i in group]
    vmem, free = pl.BlockSpec(memory_space=pltpu.VMEM), pl.BlockSpec(memory_space=pl.ANY)
    count, total = len(operands), len(operands) + len(outs)
    stages = [pltpu.VMEM(operands[i].shape, operands[i].dtype) for i in order]
    stages += [pltpu.VMEM(outs[i].shape, outs[i].dtype) for i in leaving]
    sems = [dma((max(1, len(order)),)), dma((max(1, len(leaving)), max(1, slots)))]

    def body(*refs):
        ins, results, rest = list(refs[:count]), list(refs[count:total]), refs[total:]
        held, (in_sem, out_sem), rest = rest[: len(stages)], rest[len(stages) : len(stages) + 2], rest[len(stages) + 2 :]
        copies = {}
        for j, i in enumerate(order):
            copies[i] = pltpu.make_async_copy(ins[i], held[j], in_sem.at[j])
            copies[i].start()
            ins[i] = held[j]
        targets = {}
        for j, i in enumerate(leaving):
            targets[i] = (results[i], held[len(order) + j], j)
            results[i] = held[len(order) + j]
        left = {}

        def arrive(group):
            for i in late[group]:
                copies[i].wait()

        def out_copy(i, slot):
            target, source, j = targets[i]
            if slot is None:
                return pltpu.make_async_copy(source, target, out_sem.at[j, 0])
            return pltpu.make_async_copy(source.at[slot], target.at[slot], out_sem.at[j, slot])

        def leave(slot, *indices):
            for i in indices:
                left[i] = slot is not None
                out_copy(i, slot).start()

        kernel(arrive, leave, *ins, *results, *rest)
        for i in leaving:
            for slot in range(slots) if left[i] else (None,):
                out_copy(i, slot).wait()

    late_set = set(order)
    return pl.pallas_call(
        body,
        in_specs=[free if i in late_set else vmem for i in range(count)],
        out_specs=[free if i in leaving or i in kept else vmem for i in range(len(outs))],
        out_shape=tuple(outs),
        scratch_shapes=stages + sems + list(scratch),
        compiler_params=pltpu.CompilerParams(
            collective_id=collective_id, has_side_effects=True, vmem_limit_bytes=VMEM_LIMIT
        ),
        cost_estimate=pl.CostEstimate(flops=flops, bytes_accessed=60 * 10**6, transcendentals=0),
    )(*operands)


class Units:
    def __init__(self, count, pairs):
        self.count, self.pairs, self.share = count, pairs, count // pairs
        self.me, self.other = lax.axis_index("seq"), lax.axis_index("head")

    def ahead(self, place):
        return lax.rem(place - self.me + self.count, self.count) - 1

    def behind(self, place):
        return lax.rem(self.me - place + self.count, self.count) - 1

    def to_owner(self, src, dst, send, recv, unit):
        return remote(src, dst.at[self.me], send.at[self.ahead(unit)], recv.at[self.ahead(unit)], (unit, self.other))

    def at_owner(self, src, dst, send, recv, place):
        return remote(src, dst.at[place], send.at[self.behind(place)], recv.at[self.behind(place)], (place, self.other))

    def pieces(self, value):
        size = value.shape[0] // self.share
        return [value[i * size : (i + 1) * size] for i in range(self.share)]

    def whole(self, ref, pair):
        return jnp.concatenate([ref[pair * self.share + i] for i in range(self.share)], axis=0)

    def greet(self, barrier):
        def one(away, carry):
            pl.semaphore_signal(
                barrier, inc=1, device_id=(lax.rem(self.me + away, self.count), self.other), device_id_type=MESH
            )
            return carry

        lax.fori_loop(1, self.count, one, 0)


def forward_kernel(
    slots, heads, key_dim, value_dim, parts, arrive, leave,
    hidden, input_gain, query_weight, key_weight, value_weight, gate_weight, ab_weight, taps_ref, lanes, cols, gain,
    query_out, key_out, value_out, inverse_out, eff_out, rows_out, mixer_out, gated_out,
    normed, pre, gate, x_out, inv_out, rim, ab, abt, states, maps_in,
    ext, rim_rows, delta, mix, maps_low, shifts_low, shifts_in, state_send, edge_send, edge_recv,
    map_send, map_recv, shift_send, shift_recv, back_send, back_recv,
):
    length = pre.shape[1]
    units = Units(parts, slots * heads)
    me = units.me
    barrier = pltpu.get_barrier_semaphore()
    units.greet(barrier)
    row, col = grid_masks(length)
    key_start = heads * key_dim
    value_start = 2 * heads * key_dim
    width = hidden.shape[2]
    shard = x_out.shape[2]
    edge = rim_rows.shape[1]
    shard_start = pl.multiple_of(units.other * shard, shard)

    def edge_copy():
        return remote(
            hidden.at[:, length - edge : length, :], rim_rows, edge_send.at[0], edge_recv.at[0],
            (lax.rem(me + 1, parts), units.other),
        )

    def norm_rows(x):
        inv = lax.rsqrt(jnp.sum(x * x, axis=1, keepdims=True) / width + NORM_EPSILON)
        return inv, (x * inv * input_gain[0:1, :]).astype(BF16)

    def project(s, carry):
        inv, low = norm_rows(hidden[s].astype(F32))
        normed[s] = low
        x_out[s] = hidden[s, :, pl.ds(shard_start, shard)]
        inv_out[s] = jnp.broadcast_to(inv, (length, LANES))
        pre[s, :, :key_start] = raw(low, query_weight[...], NN).astype(BF16)
        pre[s, :, key_start:value_start] = raw(low, key_weight[...], NN).astype(BF16)
        pre[s, :, value_start:] = raw(low, value_weight[...], NN).astype(BF16)
        gate[s] = raw(low, gate_weight[...], NN)
        gates = raw(low, ab_weight[...], NN)
        ab[s] = gates
        abt[s] = jnp.transpose(gates)[0:8, :]
        leave(s, 8, 9, 10, 11, 12)

        @pl.when(s == 0)
        def _():
            pl.semaphore_wait(barrier, parts - 1)
            edge_copy().start()

        return carry

    lax.fori_loop(0, slots, project, 0)
    edge_copy().wait_recv()
    _, edge_low = norm_rows(rim_rows[...].reshape(slots * edge, width).astype(F32))
    edge_pre = jnp.concatenate(
        [raw(edge_low, weight[...], NN) for weight in (query_weight, key_weight, value_weight)], axis=1
    ).astype(BF16).astype(F32)
    for s in range(slots):
        rim[s] = jnp.where(me > 0, edge_pre[(s + 1) * edge - RIM : (s + 1) * edge, :], 0.0)

    def map_copy(unit):
        return units.to_owner(maps_low.at[unit // units.share], maps_in, map_send, map_recv, unit)

    def shift_copy(unit):
        return units.to_owner(shifts_low.at[unit], shifts_in, shift_send, shift_recv, unit)

    def back_copy(place):
        ahead = units.ahead(place)
        return remote(
            state_send.at[place], states.at[me], back_send.at[ahead], back_recv.at[ahead], (place, units.other)
        )

    def back_arrival(unit):
        behind = units.behind(unit)
        return remote(
            state_send.at[unit], states.at[unit], back_send.at[behind], back_recv.at[behind], (unit, units.other)
        )

    def slot_terms(s, carry):
        ext[0:RIM, :] = rim[s]
        ext[RIM : RIM + length, :] = pre[s].astype(F32)
        conv = convolve(ext, taps_ref, length)
        active = conv * sigmoid(conv)
        log_cols, strength_cols = gates_of(ab[s], lanes[0:1, :], lanes[1:2, :])
        log_rows, strength_rows = gates_of(abt[s], cols[0:8, 0:1], cols[8:16, 0:1])
        for h in range(heads):
            query_act = active[:, h * key_dim : (h + 1) * key_dim]
            key_act = active[:, key_start + h * key_dim : key_start + (h + 1) * key_dim]
            value_act = active[:, value_start + h * value_dim : value_start + (h + 1) * value_dim]
            query_scale = lax.rsqrt(jnp.sum(query_act * query_act, axis=1, keepdims=True) + UNIT_EPSILON)
            key_scale = lax.rsqrt(jnp.sum(key_act * key_act, axis=1, keepdims=True) + UNIT_EPSILON)
            query = (query_act * query_scale * key_dim ** (-0.5)).astype(BF16)
            key = (key_act * key_scale).astype(BF16)
            value = value_act.astype(BF16)
            query_out[s, h] = query
            key_out[s, h] = key
            value_out[s, h] = value
            strength = strength_cols[:, heads + h : heads + h + 1]
            strength_row = strength_rows[heads + h : heads + h + 1, :]
            cum_col, cum_row, end, decayed = decay_of(
                log_cols[:, h : h + 1], log_rows[h : h + 1, :], row, col
            )
            products = mm(key, key, NT)
            inverse = unit_inverse(jnp.where(row > col, strength * decayed * products, 0.0))
            inverse_out[s, h] = inverse
            scaled = inverse * strength_row
            delta_h = mm(split(scaled), value)
            mix_h = mm(split(scaled * jnp.exp(cum_row)), key)
            delta[s, h] = delta_h
            mix[s, h] = mix_h
            scores = split(decayed * mm(query, key, NT))
            eff_out[s, h] = jnp.exp(cum_col) * query.astype(F32) - mm(scores, split(mix_h))
            end_weight = jnp.exp(end - cum_col)
            small_row = lax.broadcasted_iota(jnp.int32, (key_dim, key_dim), 0)
            small_col = lax.broadcasted_iota(jnp.int32, (key_dim, key_dim), 1)
            moved = jnp.where(small_row == small_col, jnp.exp(end), 0.0)
            pair = s * heads + h
            maps_low[pair] = (moved - mm(split(mix_h * end_weight), key, TN)).astype(BF16)
            for i, piece in enumerate(units.pieces(mm(split(delta_h * end_weight), key, TN).astype(BF16))):
                shifts_low[pair * units.share + i] = piece

        leave(s, 0, 1, 2, 3, 4)
        for i in range(heads * units.share):
            unit = s * heads * units.share + i

            @pl.when(unit != me)
            def _(unit=unit):
                map_copy(unit).start()
                shift_copy(unit).start()

            @pl.when(unit == me)
            def _(unit=unit):
                maps_in[unit] = maps_low[unit // units.share]
                shifts_in[unit] = shifts_low[unit]

        return carry

    lax.fori_loop(0, slots, slot_terms, 0)

    def scan(place, state):
        low = state.astype(BF16)

        @pl.when(place != me)
        def _():
            state_send[place] = low
            back_copy(place).start()
            units.at_owner(maps_low.at[0], maps_in, map_send, map_recv, place).wait_recv()
            units.at_owner(shifts_low.at[0], shifts_in, shift_send, shift_recv, place).wait_recv()

        @pl.when(place == me)
        def _():
            states[place] = low

        return mm(split(state), maps_in[place]) + shifts_in[place].astype(F32)

    lax.fori_loop(0, parts, scan, jnp.zeros((value_dim // units.share, key_dim), F32))

    def emit(s, carry):
        for i in range(heads * units.share):
            unit = s * heads * units.share + i

            @pl.when(unit != me)
            def _(unit=unit):
                back_arrival(unit).wait_recv()

        log_cols, _ = gates_of(ab[s], lanes[0:1, :], lanes[1:2, :])
        log_rows, _ = gates_of(abt[s], cols[0:8, 0:1], cols[8:16, 0:1])
        for h in range(heads):
            query, key = query_out[s, h], key_out[s, h]
            cum_col, _, _, decayed = decay_of(log_cols[:, h : h + 1], log_rows[h : h + 1, :], row, col)
            scores = split(decayed * mm(query, key, NT))
            state = units.whole(states, s * heads + h)
            rows = delta[s, h] - mm(split(mix[s, h]), state, NT)
            rows_out[s, h] = rows
            mixer = mm(scores, split(rows)) + jnp.exp(cum_col) * mm(query, state, NT)
            mixer_out[s, h] = mixer
            scale = lax.rsqrt(jnp.sum(mixer * mixer, axis=1, keepdims=True) / value_dim + NORM_EPSILON)
            here = slice(h * value_dim, (h + 1) * value_dim)
            gate_h = gate[s, :, here]
            gated_out[s, :, here] = (mixer * scale * gain[0:1, :] * (gate_h * sigmoid(gate_h))).astype(BF16)
        leave(s, 5, 6, 7)
        return carry

    lax.fori_loop(0, slots, emit, 0)

    def drain(away, carry):
        unit = lax.rem(me + away, parts)
        map_copy(unit).wait_send()
        shift_copy(unit).wait_send()
        back_copy(unit).wait_send()
        return carry

    lax.fori_loop(1, parts, drain, 0)
    edge_copy().wait_send()


def forward_call(parts, head_parts, heads, *operands):
    hidden, query_weight, value_weight, gate_weight = operands[0], operands[2], operands[4], operands[5]
    slots, length, width = hidden.shape
    key_dim, value_dim = query_weight.shape[1] // heads, value_weight.shape[1] // heads
    channels = heads * (2 * key_dim + value_dim)
    share = parts // (slots * heads)
    sds = jax.ShapeDtypeStruct
    dma = pltpu.SemaphoreType.DMA
    per = lambda kind, *tail: sds((slots, heads) + tail, kind)
    each = lambda kind, *tail: sds((slots,) + tail, kind)
    unit = (parts, value_dim // share, key_dim)
    outs = (
        per(BF16, length, key_dim), per(BF16, length, key_dim), per(BF16, length, value_dim),
        per(F32, length, length), per(F32, length, key_dim), per(F32, length, value_dim),
        per(F32, length, value_dim), each(BF16, length, heads * value_dim),
        each(BF16, length, width), each(BF16, length, channels), each(F32, length, heads * value_dim),
        each(BF16, length, width // head_parts), each(F32, length, LANES), each(F32, RIM, channels),
        each(F32, length, LANES), each(F32, 8, length),
        sds(unit, BF16), sds((parts, key_dim, key_dim), BF16),
    )
    scratch = [
        pltpu.VMEM((length + RIM, channels), F32),
        pltpu.VMEM((slots, 2 * RIM, width), BF16),
        pltpu.VMEM((slots, heads, length, value_dim), F32),
        pltpu.VMEM((slots, heads, length, key_dim), F32),
        pltpu.VMEM((slots * heads, key_dim, key_dim), BF16),
        pltpu.VMEM(unit, BF16), pltpu.VMEM(unit, BF16), pltpu.VMEM(unit, BF16), dma((1,)), dma((1,)),
    ] + [dma((parts - 1,))] * 6
    return staged_call(
        functools.partial(forward_kernel, slots, heads, key_dim, value_dim, parts),
        operands, outs, scratch, 2, leaving=tuple(range(13)), slots=slots,
    )


def head_scratch(kinds, stats, slots, head_parts, length, shard):
    lines = head_parts // 2
    dma = pltpu.SemaphoreType.DMA
    return [
        pltpu.VMEM((head_parts, length, shard), F32),
        pltpu.VMEM((kinds, slots, lines, length, shard), F32),
        pltpu.VMEM((kinds, slots, lines, length, shard), BF16),
        pltpu.VMEM((kinds, slots, lines, length, shard), BF16),
        pltpu.VMEM((kinds, slots, lines - 1, length, shard), BF16),
        pltpu.VMEM((kinds, slots, lines - 1, length, shard), BF16),
        pltpu.VMEM((stats, slots, 8, length), F32),
        pltpu.VMEM((stats, slots, head_parts - 1, 8, length), F32),
        dma((kinds, slots, lines)), dma((kinds, slots, lines)),
        dma((kinds, slots, lines - 1)), dma((kinds, slots, lines - 1)),
        dma((stats, slots, head_parts - 1)), dma((stats, slots, head_parts - 1)),
    ]


def head_tools(head_parts, refs, stats):
    whole_part, part, low, from_core, to_line, from_line, stat_own, stat_in = refs[:8]
    core_send, core_recv, line_send, line_recv, stat_send, stat_recv = refs[8:]
    me = lax.axis_index("head")
    place = lax.axis_index("seq")
    lines = head_parts // 2
    core = lax.rem(me, 2)
    line = me // 2
    sibling = 2 * line + (1 - core)
    length, shard = whole_part.shape[1:]
    row, col = grid_masks(length)

    def greet(barrier):
        for away in range(1, head_parts):
            pl.semaphore_signal(
                barrier, inc=1, device_id=(place, lax.rem(me + away, head_parts)), device_id_type=MESH
            )

    def core_copy(kind, s, y):
        return remote(
            low.at[kind, s, y], from_core.at[kind, s, y],
            core_send.at[kind, s, y], core_recv.at[kind, s, y], (place, sibling),
        )

    def line_copy(kind, s, away):
        return remote(
            to_line.at[kind, s, away - 1], from_line.at[kind, s, away - 1],
            line_send.at[kind, s, away - 1], line_recv.at[kind, s, away - 1],
            (place, 2 * lax.rem(line + away, lines) + core),
        )

    def stat_copy(kind, s, away):
        return remote(
            stat_own.at[kind, s], stat_in.at[kind, s, away - 1],
            stat_send.at[kind, s, away - 1], stat_recv.at[kind, s, away - 1],
            (place, lax.rem(me + away, head_parts)),
        )

    def send_part(kind, s, value):
        for j in range(head_parts):
            whole_part[j] = value[:, j * shard : (j + 1) * shard]
        for y in range(lines):
            low[kind, s, y] = whole_part[2 * y + (1 - core)].astype(BF16)
            core_copy(kind, s, y).start()
            part[kind, s, y] = whole_part[2 * y + core]

    def join_core(kind, s):
        for y in range(lines):
            core_copy(kind, s, y).wait_recv()
        for away in range(1, lines):
            y = lax.rem(line + away, lines)
            joined = part[kind, s, y] + from_core[kind, s, y].astype(F32)
            to_line[kind, s, away - 1] = joined.astype(BF16)
            line_copy(kind, s, away).start()
        part[kind, s, line] = part[kind, s, line] + from_core[kind, s, line].astype(F32)

    def join_line(kind, s):
        total = part[kind, s, line]
        for away in range(1, lines):
            line_copy(kind, s, away).wait_recv()
            total = total + from_line[kind, s, away - 1].astype(F32)
        return total

    def send_stat(kind, s, column):
        stat_own[kind, s] = jnp.broadcast_to(turn_to_row(column, row, col), (8, length))
        for away in range(1, head_parts):
            stat_copy(kind, s, away).start()

    def join_stat(kind, s):
        total = stat_own[kind, s]
        for away in range(1, head_parts):
            stat_copy(kind, s, away).wait_recv()
            total = total + stat_in[kind, s, away - 1]
        return turn_to_column(total[0:1, :], row, col)

    def drain(s):
        for kind in range(part.shape[0]):
            for y in range(lines):
                core_copy(kind, s, y).wait_send()
            for away in range(1, lines):
                line_copy(kind, s, away).wait_send()
        for kind in range(stats):
            for away in range(1, head_parts):
                stat_copy(kind, s, away).wait_send()

    return types.SimpleNamespace(
        me=me, place=place, lines=lines, core=core, line=line, sibling=sibling, greet=greet,
        send_part=send_part, join_core=join_core, join_line=join_line, send_stat=send_stat,
        join_stat=join_stat, drain=drain,
    )


def weight_rows(left, right, store):
    wide = left.shape[2]
    step = min(wide, 256)
    steps = wide // step

    def one(j, carry):
        start = pl.multiple_of(j * step, step)
        block = left[:, :, pl.ds(start, step)]
        store(start, step, raw(block.reshape(-1, step), right, TN).astype(BF16))
        return carry

    lax.fori_loop(0, steps, one, 0)
    if wide % step:
        rest = wide % step
        block = left[:, :, steps * step :]
        store(steps * step, rest, raw(block.reshape(-1, rest), right, TN).astype(BF16))


def middle_kernel(
    slots, head_parts, parts, heads, arrive, leave,
    gated, x_shard, cotangent, mask, out_weight, gate_weight, up_weight,
    down_weight, gain, mixer, gate, gain_row, eff,
    residual, act_all, up_part, gate_part, down_part, residual_grad_out, mixer_rows_grad, mixer_grad, gate_grad_out,
    gain_grad_out, output_gain_grad, shifts_in,
    normed_all, up_grad_all, gate_grad_all, out_grad,
    inverse, spread, grad_shard, shifts_low, shift_send, shift_recv,
    spread_line_send, spread_line_recv, spread_core_send, spread_core_recv,
    *head_refs,
):
    tools = head_tools(head_parts, head_refs, 2)
    me, place, lines, core, line, sibling = (
        tools.me, tools.place, tools.lines, tools.core, tools.line, tools.sibling
    )
    send_part, join_core, join_line = tools.send_part, tools.join_core, tools.join_line
    send_stat, join_stat = tools.send_stat, tools.join_stat
    length, shard = x_shard.shape[1], x_shard.shape[2]
    width = shard * head_parts
    hidden = gate_weight.shape[0]
    value_dim = mixer.shape[3]
    units = Units(parts, slots * heads)

    barrier = pltpu.get_barrier_semaphore()
    tools.greet(barrier)
    units.greet(barrier)
    gain_grad_out[...] = jnp.zeros_like(gain_grad_out)
    output_gain_grad[...] = jnp.zeros_like(output_gain_grad)
    pl.semaphore_wait(barrier, head_parts - 1 + parts - 1)

    def shift_copy(unit):
        return units.to_owner(shifts_low.at[unit], shifts_in, shift_send, shift_recv, unit)

    def spread_line_copy(kind, s, away):
        return remote(
            spread.at[kind, s, me], spread.at[kind, s, me],
            spread_line_send.at[kind, s, away - 1], spread_line_recv.at[kind, s, away - 1],
            (place, 2 * lax.rem(line + away, lines) + core),
        )

    def spread_core_copy(kind, s, away):
        y = lax.rem(line + away, lines)
        return remote(
            spread.at[kind, s, 2 * y + core], spread.at[kind, s, 2 * y + core],
            spread_core_send.at[kind, s, away], spread_core_recv.at[kind, s, away], (place, sibling),
        )

    def spread_core_arrival(kind, s, away):
        y = lax.rem(line + away, lines)
        return remote(
            spread.at[kind, s, 2 * y + (1 - core)], spread.at[kind, s, 2 * y + (1 - core)],
            spread_core_send.at[kind, s, away], spread_core_recv.at[kind, s, away], (place, sibling),
        )

    def spread_line_arrival(kind, s, away):
        y = lax.rem(line + lines - away, lines)
        return remote(
            spread.at[kind, s, 2 * y + core], spread.at[kind, s, 2 * y + core],
            spread_line_send.at[kind, s, away - 1], spread_line_recv.at[kind, s, away - 1],
            (place, 2 * y + core),
        )

    def send_spread(kind, s, value):
        spread[kind, s, me] = value
        for away in range(1, lines):
            spread_line_copy(kind, s, away).start()
        spread_core_copy(kind, s, 0).start()

    def pass_spread(kind, s):
        for away in range(1, lines):
            spread_line_arrival(kind, s, lines - away).wait_recv()
            spread_core_copy(kind, s, away).start()

    def take_spread(kind, s):
        for away in range(lines):
            spread_core_arrival(kind, s, away).wait_recv()
        return jnp.concatenate([spread[kind, s, j] for j in range(head_parts)], axis=1)

    def attention(s):
        send_part(0, s, raw(gated[s], out_weight[...], NN))

    def rows_in(s):
        total = x_shard[s].astype(F32) + mask[s][:, 0:1] * join_line(0, s)
        residual[s] = total
        leave(s, 0)
        send_stat(0, s, jnp.sum(total * total, axis=1, keepdims=True))

    def norm_second(s):
        inv = lax.rsqrt(join_stat(0, s) / width + NORM_EPSILON)
        inverse[s] = jnp.broadcast_to(inv, (length, LANES))
        send_spread(0, s, (residual[s] * inv * gain[0:1, :]).astype(BF16))

    def swiglu(s):
        normed = take_spread(0, s)
        normed_all[s] = normed
        gate_values = raw(normed, gate_weight[...], NT)
        up_values = raw(normed, up_weight[...], NT)
        out_grad[s] = (cotangent[s].astype(F32) * mask[s][:, 0:1]).astype(BF16)
        act_grad = raw(out_grad[s], down_weight[...], NT)
        sig = sigmoid(gate_values)
        silu = gate_values * sig
        act_all[s] = (silu * up_values).astype(BF16)
        up_grad = (act_grad * silu).astype(BF16)
        gate_grad = (act_grad * up_values * sig * (1.0 + gate_values * (1.0 - sig))).astype(BF16)
        up_grad_all[s] = up_grad
        gate_grad_all[s] = gate_grad
        leave(s, 1)
        send_part(1, s, raw(up_grad, up_weight[...], NN) + raw(gate_grad, gate_weight[...], NN))

    def norm_back(s):
        grad = join_line(1, s)
        inv = inverse[s][:, 0:1]
        gain_grad_out[0:1, :] += jnp.sum(grad * residual[s] * inv, axis=0, keepdims=True)
        weighted = grad * gain[0:1, :]
        grad_shard[s] = weighted
        send_stat(1, s, jnp.sum(weighted * residual[s], axis=1, keepdims=True))

    def residual_back(s):
        stat = join_stat(1, s) / width
        inv = inverse[s][:, 0:1]
        cot = cotangent[s, :, pl.ds(pl.multiple_of(me * shard, shard), shard)].astype(F32)
        grad = cot + inv * (grad_shard[s] - residual[s] * (inv * inv * stat))
        residual_grad_out[s] = grad
        leave(s, 5)
        send_spread(1, s, (mask[s][:, 0:1] * grad).astype(BF16))

    def gate_back(s, gated_grad):
        out_gain = gain_row[0:1, :]
        for h in range(heads):
            here = slice(h * value_dim, (h + 1) * value_dim)
            grad = gated_grad[:, here]
            mixer_h = mixer[s, h]
            gate_h = gate[s, :, here]
            scale = lax.rsqrt(jnp.sum(mixer_h * mixer_h, axis=1, keepdims=True) / value_dim + NORM_EPSILON)
            sig = sigmoid(gate_h)
            unit_rows = mixer_h * scale
            gate_grad_out[s, :, here] = (
                grad * unit_rows * out_gain * (sig * (1.0 + gate_h * (1.0 - sig)))
            ).astype(BF16)
            scaled_grad = grad * (gate_h * sig)
            output_gain_grad[0:1, :] += jnp.sum(scaled_grad * unit_rows, axis=0, keepdims=True)
            unit_grad = scaled_grad * out_gain
            stat = jnp.sum(unit_grad * mixer_h, axis=1, keepdims=True) / value_dim
            mixer_grad_h = scale * (unit_grad - mixer_h * (scale * scale * stat))
            mixer_grad[s, h] = mixer_grad_h
            entering = mm(split(mixer_grad_h), split(eff[s, h]), TN).astype(BF16)
            for i, piece in enumerate(units.pieces(entering)):
                shifts_low[(s * heads + h) * units.share + i] = piece

        for i in range(heads * units.share):
            unit = s * heads * units.share + i

            @pl.when(unit != units.me)
            def _(unit=unit):
                shift_copy(unit).start()

            @pl.when(unit == units.me)
            def _(unit=unit):
                shifts_in[unit] = shifts_low[unit]

    def mixer_rows(s):
        grad = take_spread(1, s)
        mixer_rows_grad[s] = grad
        gate_back(s, raw(grad, out_weight[...], NT))
        leave(s, 6, 7, 8)

    stages = (
        (10, mixer_rows),
        (9, functools.partial(pass_spread, 1)),
        (8, residual_back),
        (7, norm_back),
        (6, functools.partial(join_core, 1)),
        (4, functools.partial(pass_spread, 0)),
        (3, norm_second),
        (2, rows_in),
        (1, functools.partial(join_core, 0)),
        (0, attention),
        (5, swiglu),
    )

    def step(t, carry):
        @pl.when(t == 5)
        def _():
            arrive(0)

        @pl.when(t == 10)
        def _():
            arrive(1)

        for offset, stage in stages:
            s = t - offset

            @pl.when((s >= 0) & (s < slots))
            def _(stage=stage, s=s):
                stage(s)

        for late, left, right, target, index in (
            (5, up_grad_all, normed_all, up_part, 2),
            (6, gate_grad_all, normed_all, gate_part, 3),
            (7, act_all, out_grad, down_part, 4),
        ):

            @pl.when(t == slots + late)
            def _(left=left, right=right, target=target, index=index):
                def store(start, size, block):
                    target[pl.ds(start, size), :] = block

                weight_rows(left, right[...].reshape(-1, width), store)
                if target.shape[0] > hidden:
                    target[hidden:, :] = jnp.zeros((target.shape[0] - hidden, width), BF16)
                leave(None, index)

        return carry

    lax.fori_loop(0, slots + 10, step, 0)

    def drain(s, carry):
        tools.drain(s)
        for kind in range(2):
            for away in range(1, lines):
                spread_line_copy(kind, s, away).wait_send()
            for away in range(lines):
                spread_core_copy(kind, s, away).wait_send()
        return carry

    lax.fori_loop(0, slots, drain, 0)

    def take_units(away, carry):
        unit = lax.rem(units.me + away, parts)
        units.at_owner(shifts_low.at[0], shifts_in, shift_send, shift_recv, unit).wait_recv()
        return carry

    lax.fori_loop(1, parts, take_units, 0)

    def drain_units(away, carry):
        shift_copy(lax.rem(units.me + away, parts)).wait_send()
        return carry

    lax.fori_loop(1, parts, drain_units, 0)


def padded_rows(count, parts):
    return count + -count % (32 * parts)


def middle_call(parts, head_parts, heads, *operands):
    gated, x_shard, gate_weight, mixer, eff = (operands[i] for i in (0, 1, 5, 9, 12))
    slots, length, shard = x_shard.shape
    width = shard * head_parts
    hidden = gate_weight.shape[0]
    lines = head_parts // 2
    value_dim, key_dim = mixer.shape[3], eff.shape[3]
    unit = (parts, value_dim * slots * heads // parts, key_dim)
    sds = jax.ShapeDtypeStruct
    dma = pltpu.SemaphoreType.DMA
    product = sds((padded_rows(hidden, parts), width), BF16)
    outs = (
        sds((slots, length, shard), F32), sds((slots, length, hidden), BF16), product, product, product,
        sds((slots, length, shard), F32), sds((slots, length, width), BF16), sds(mixer.shape, F32),
        sds(gated.shape, BF16), sds((8, shard), F32), sds((8, value_dim), F32), sds(unit, BF16),
    )
    scratch = [
        pltpu.VMEM((slots, length, width), BF16),
        pltpu.VMEM((slots, length, hidden), BF16),
        pltpu.VMEM((slots, length, hidden), BF16),
        pltpu.VMEM((slots, length, width), BF16),
        pltpu.VMEM((slots, length, LANES), F32),
        pltpu.VMEM((2, slots, head_parts, length, shard), BF16),
        pltpu.VMEM((slots, length, shard), F32),
        pltpu.VMEM(unit, BF16), dma((parts - 1,)), dma((parts - 1,)),
        dma((2, slots, lines - 1)), dma((2, slots, lines - 1)),
        dma((2, slots, lines)), dma((2, slots, lines)),
    ] + head_scratch(2, 2, slots, head_parts, length, shard)
    return staged_call(
        functools.partial(middle_kernel, slots, head_parts, parts, heads),
        operands, outs, scratch, 0, late=((5, 6, 7, 2), (9, 10, 12)), leaving=tuple(range(9)), slots=slots,
    )


def ring_scratch(parts, shapes):
    dma = pltpu.SemaphoreType.DMA
    count = len(shapes)
    return [
        pltpu.VMEM((2, parts, rows // (2 * parts), wide), BF16) for rows, wide in shapes
    ] + [dma((count, 2)), dma((count, 2, parts - 1)), dma((count, 2)), dma((count, 2, parts - 1)), dma((count, 2))]


def ring_tools(parts, ins, outs, held, send, recv, spread_send, spread_recv, own):
    count = len(ins)
    index = lax.axis_index("seq")
    other = lax.axis_index("head")
    side = lax.rem(index, 2)
    level = index // 2
    levels = parts // 2
    position = jnp.where(side == 1, level, parts - 1 - level)
    up = jnp.where(side == 1, jnp.where(level == levels - 1, index - 1, index + 2),
                   jnp.where(level == 0, index + 1, index - 2))
    down = jnp.where(side == 1, jnp.where(level == 0, index - 1, index - 2),
                     jnp.where(level == levels - 1, index + 1, index + 2))
    targets = (up, down)
    def greet(barrier):
        for target in targets:
            pl.semaphore_signal(barrier, inc=1, device_id=(target, other), device_id_type=MESH)

    def rows_of(a, way, chunk):
        size = ins[a].shape[0] // (2 * parts)
        return pl.ds(pl.multiple_of((chunk * 2 + way) * size, size), size)

    def chunk_at(way, step):
        if way == 0:
            return lax.rem(position - step + 2 * parts, parts)
        return lax.rem(position + step + 2 * parts, parts)

    def sum_copy(a, way, step):
        return remote(
            held[a].at[way, step], held[a].at[way, step + 1], send.at[a, way], recv.at[a, way, step],
            (targets[way], other),
        )

    def spread_copy(a, way, step):
        block = rows_of(a, way, chunk_at(way, step - 1))
        return remote(
            outs[a].at[block, :], outs[a].at[block, :], spread_send.at[a, way], spread_recv.at[a, way, step],
            (targets[way], other),
        )

    def spread_first(a, way):
        block = rows_of(a, way, chunk_at(way, parts - 1))
        return remote(
            held[a].at[way, parts - 1], outs[a].at[block, :], spread_send.at[a, way],
            spread_recv.at[a, way, 0], (targets[way], other),
        )

    def own_copy(a, way):
        block = rows_of(a, way, chunk_at(way, parts - 1))
        return pltpu.make_async_copy(held[a].at[way, parts - 1], outs[a].at[block, :], own.at[a, way])

    def spread_arrival(a, way, step):
        block = rows_of(a, way, chunk_at(way, step))
        return remote(
            outs[a].at[block, :], outs[a].at[block, :], spread_send.at[a, way], spread_recv.at[a, way, step],
            (targets[way], other),
        )

    lanes = [(a, way) for a in range(count) for way in range(2)]
    last = parts - 2

    def add(step, a, way):
        sum_copy(a, way, step).wait_recv()
        mine = ins[a][rows_of(a, way, chunk_at(way, step + 1)), :].astype(F32)
        return (held[a][way, step + 1].astype(F32) + mine).astype(BF16)

    def begin():
        for a, way in lanes:
            held[a][way, 0] = ins[a][rows_of(a, way, chunk_at(way, 0)), :]
            sum_copy(a, way, 0).start()

    def one(step):
        for a, way in lanes:
            held[a][way, step + 1] = add(step, a, way)
            sum_copy(a, way, step).wait_send()
            sum_copy(a, way, step + 1).start()

    def turn():
        for a, way in lanes:
            held[a][way, parts - 1] = add(last, a, way)
            sum_copy(a, way, last).wait_send()
            spread_first(a, way).start()
            own_copy(a, way).start()

    def pass_first():
        for a, way in lanes:
            spread_arrival(a, way, 0).wait_recv()
            spread_first(a, way).wait_send()
            spread_copy(a, way, 1).start()

    def pass_on(step):
        for a, way in lanes:
            spread_arrival(a, way, step).wait_recv()
            spread_copy(a, way, step).wait_send()
            spread_copy(a, way, step + 1).start()

    def finish():
        for a, way in lanes:
            spread_arrival(a, way, last).wait_recv()
            spread_copy(a, way, last).wait_send()
            own_copy(a, way).wait()

    def tick(k):
        @pl.when(k < last)
        def _():
            one(k)

        @pl.when(k == last)
        def _():
            turn()

        @pl.when(k == last + 1)
        def _():
            pass_first()

        @pl.when(k > last + 1)
        def _():
            pass_on(k - last - 1)

    return types.SimpleNamespace(
        greet=greet, begin=begin, tick=tick, finish=finish, ticks=2 * parts - 3, up=up, down=down
    )


def backward_kernel(
    slots, heads, key_dim, value_dim, parts, head_parts, arrive, leave,
    mixer_grad, shifts_in, gated, mixer_rows_grad, normed, gate_grad, act, down_weight, residual, mask,
    pre, rim, ab, abt, taps_ref, lanes, cols,
    queries, keys, value_rows, inverse_all, delta_rows, states, maps_in, up_part, gate_part, down_part,
    block_out, pre_grad_out, ab_grad_out, taps_grad_out, lane_grad_out,
    up_sum, gate_sum, down_sum, out_sum, first_sum,
    out_part, first_part, ext, conv_grad, tail, rim_own, rim_in, leavings, leaving_send,
    back_send, back_recv, rim_send, rim_recv, *refs,
):
    sides = (refs[:7], refs[7:15])
    length = pre.shape[1]
    taps = 4
    width = normed.shape[2]
    values = gated.shape[2]
    units = Units(parts, slots * heads)
    me = units.me
    tools = head_tools(head_parts, refs[15:], 0)
    rings = (
        ring_tools(parts, (up_part, gate_part), (up_sum, gate_sum), sides[0][:2], *sides[0][2:]),
        ring_tools(
            parts, (down_part, out_part, first_part), (down_sum, out_sum, first_sum), sides[1][:3], *sides[1][3:]
        ),
    )
    barrier = pltpu.get_barrier_semaphore()
    units.greet(barrier)
    tools.greet(barrier)
    row, col = grid_masks(length)
    taps_grad_out[...] = jnp.zeros_like(taps_grad_out)
    lane_grad_out[...] = jnp.zeros_like(lane_grad_out)
    pl.semaphore_wait(barrier, parts - 1 + head_parts - 1)
    rings[0].begin()

    def back_copy(place):
        ahead = units.ahead(place)
        return remote(
            leaving_send.at[place], leavings.at[me], back_send.at[ahead], back_recv.at[ahead],
            (place, units.other),
        )

    def back_arrival(unit):
        behind = units.behind(unit)
        return remote(
            leaving_send.at[unit], leavings.at[unit], back_send.at[behind], back_recv.at[behind],
            (unit, units.other),
        )

    def rim_copy():
        return remote(
            rim_own, rim_in, rim_send.at[0], rim_recv.at[0], (lax.rem(me + parts - 1, parts), units.other)
        )

    def scan(hop, leaving):
        place = parts - 1 - hop
        low = leaving.astype(BF16)

        @pl.when(place != me)
        def _():
            leaving_send[place] = low
            back_copy(place).start()

        @pl.when(place == me)
        def _():
            leavings[place] = low

        return mm(split(leaving), maps_in[place], NT) + shifts_in[place].astype(F32)

    lax.fori_loop(0, parts, scan, jnp.zeros((value_dim // units.share, key_dim), F32))
    arrive(0)

    def store_out(start, size, block):
        out_part[pl.ds(start, size), :] = block

    def store_first(start, size, block):
        first_part[pl.ds(start, size), :] = block

    weight_rows(gated, mixer_rows_grad[...].reshape(-1, width), store_out)
    weight_rows(normed, gate_grad[...].reshape(-1, values), store_first)
    rings[1].begin()
    arrive(1)

    def swiglu_out(s, carry):
        tools.send_part(0, s, raw(act[s], down_weight[...], NN))
        return carry

    lax.fori_loop(0, slots, swiglu_out, 0)
    rings[0].tick(0)

    def swiglu_core(s, carry):
        tools.join_core(0, s)
        return carry

    lax.fori_loop(0, slots, swiglu_core, 0)
    rings[1].tick(0)
    arrive(2)

    def delta_slot(s, carry):
        for i in range(heads * units.share):
            unit = s * heads * units.share + i

            @pl.when(unit != me)
            def _(unit=unit):
                back_arrival(unit).wait_recv()

        ext[0:RIM, :] = rim[s]
        ext[RIM : RIM + length, :] = pre[s].astype(F32)
        lane = lax.broadcasted_iota(jnp.int32, (length, LANES), 1)
        log_cols, strength_cols = gates_of(ab[s], lanes[0:1, :], lanes[1:2, :])
        log_rows, strength_rows = gates_of(abt[s], cols[0:8, 0:1], cols[8:16, 0:1])
        key_start = heads * key_dim
        value_start = 2 * heads * key_dim
        strict = row > col
        grads = jnp.zeros((length, LANES), F32)
        conv_grad[0:RIM, :] = jnp.zeros((RIM, conv_grad.shape[1]), F32)
        conv_grad[RIM + length : 2 * RIM + length, :] = jnp.zeros((RIM, conv_grad.shape[1]), F32)

        def activation(start, width):
            total = taps_ref[0:1, start : start + width] * ext[pl.ds(RIM - taps + 1, length), start : start + width]
            for tap in range(1, taps):
                total = total + (
                    taps_ref[tap : tap + 1, start : start + width]
                    * ext[pl.ds(RIM - taps + 1 + tap, length), start : start + width]
                )
            sig = sigmoid(total)
            return total * sig, sig * (1.0 + total * (1.0 - sig))

        def unit_back(grad, start, scale_by):
            act, slope = activation(start, key_dim)
            scale = lax.rsqrt(jnp.sum(act * act, axis=1, keepdims=True) + UNIT_EPSILON)
            inner = jnp.sum(act * grad, axis=1, keepdims=True)
            back = scale_by * scale * (grad - act * (scale * scale * inner))
            conv_grad[RIM : RIM + length, start : start + key_dim] = back * slope

        for h in range(heads):
            query, key, value = queries[s, h], keys[s, h], value_rows[s, h]
            query_f, key_f = query.astype(F32), key.astype(F32)
            strength = strength_cols[:, heads + h : heads + h + 1]
            cum_col, cum_row, end, decayed = decay_of(
                log_cols[:, h : h + 1], log_rows[h : h + 1, :], row, col
            )
            rise = jnp.exp(cum_col)
            end_weight = jnp.exp(end - cum_col)
            state = units.whole(states, s * heads + h)
            leaving = units.whole(leavings, s * heads + h)
            state_f, leaving_f = state.astype(F32), leaving.astype(F32)
            rows = split(delta_rows[s, h])
            out_grad = split(mixer_grad[s, h])
            products = mm(key, key, NT)
            scores = decayed * mm(query, key, NT)
            rows_grad = mm(split(scores), out_grad, TN) + end_weight * mm(key, leaving, NT)
            scores_grad = mm(out_grad, rows, NT)
            query_grad = rise * mm(out_grad, state)
            right_grad = mm(split(inverse_all[s, h]), split(rows_grad), TN)
            key_state = mm(key, state, NT)
            triangle_grad = -jnp.where(strict, mm(split(right_grad), rows, NT), 0.0)
            value_grad = strength * right_grad
            strength_grad = jnp.sum(right_grad * (value.astype(F32) - rise * key_state), axis=1, keepdims=True)
            read_grad = -rise * value_grad
            cum_grad = jnp.sum(read_grad * key_state, axis=1, keepdims=True)
            key_grad = mm(split(read_grad), state)
            decayed_grad = triangle_grad * decayed
            strength_grad = strength_grad + jnp.sum(decayed_grad * products, axis=1, keepdims=True)
            weighted = strength * decayed_grad
            both = weighted * products + scores_grad * scores
            products_grad = split(weighted)
            overlap_grad = split(scores_grad * decayed)
            cum_grad = cum_grad + jnp.sum(both, axis=1, keepdims=True) + jnp.sum(query_f * query_grad, axis=1, keepdims=True)
            query_grad = query_grad + mm(overlap_grad, key)
            key_grad = (
                key_grad + mm(overlap_grad, query, TN) + mm(products_grad, key) + mm(products_grad, key, TN)
            )
            moved = mm(rows, leaving)
            key_grad = key_grad + end_weight * moved
            end_part = jnp.sum(moved * key_f, axis=1, keepdims=True) * end_weight
            cum_grad = cum_grad - end_part
            last = jnp.sum(end_part, axis=0, keepdims=True) + jnp.exp(end) * jnp.sum(
                jnp.sum(leaving_f * state_f, axis=1, keepdims=True), axis=0, keepdims=True
            )
            turned = jnp.sum(jnp.where(row == col, cum_grad, 0.0), axis=0, keepdims=True)
            turned = turned - jnp.sum(both, axis=0, keepdims=True)
            log_grad = jnp.sum(jnp.where(row <= col, turned, 0.0), axis=1, keepdims=True) + last
            grads = jnp.where(lane == h, log_grad, grads)
            grads = jnp.where(lane == heads + h, strength_grad, grads)
            unit_back(query_grad, h * key_dim, key_dim ** (-0.5))
            unit_back(key_grad, key_start + h * key_dim, 1.0)
            if h == 0:
                rings[0].tick(s + 1)
            _, slope = activation(value_start + h * value_dim, value_dim)
            conv_grad[RIM : RIM + length, value_start + h * value_dim : value_start + (h + 1) * value_dim] = (
                value_grad * slope
            )

        softened = -lanes[0:1, :] * sigmoid(ab[s] + lanes[1:2, :])
        decay_part = grads * softened
        is_log = lane < heads
        ab_grad_out[s] = jnp.where(is_log, decay_part, grads * strength_cols * (1.0 - strength_cols))
        lane_grad_out[0:1, :] += jnp.sum(jnp.where(is_log, grads * log_cols, 0.0), axis=0, keepdims=True)
        lane_grad_out[1:2, :] += jnp.sum(jnp.where(is_log, decay_part, 0.0), axis=0, keepdims=True)
        main = conv_grad[RIM : RIM + length, :]
        pre_grad = jnp.zeros_like(main)
        rim_grad = jnp.zeros((RIM, conv_grad.shape[1]), F32)
        for tap in range(taps):
            weight = taps_ref[tap : tap + 1, :]
            taps_grad_out[tap : tap + 1, :] += jnp.sum(
                main * ext[pl.ds(RIM - taps + 1 + tap, length), :], axis=0, keepdims=True
            )
            pre_grad = pre_grad + weight * conv_grad[pl.ds(RIM + taps - 1 - tap, length), :]
            rim_grad = rim_grad + weight * conv_grad[pl.ds(taps - 1 - tap, RIM), :]
        pre_grad_out[s] = pre_grad.astype(BF16)
        tail[s] = pre_grad[length - 2 * RIM : length, :]
        rim_own[s] = rim_grad


        rings[1].tick(s + 1)
        block_out[s] = (residual[s] + mask[s][:, 0:1] * tools.join_line(0, s)).astype(BF16)
        return carry

    lax.fori_loop(0, slots, delta_slot, 0)
    rim_copy().start()

    def rest(k, carry):
        rings[0].tick(k)
        rings[1].tick(k)
        return carry

    lax.fori_loop(slots + 1, rings[0].ticks, rest, 0)
    rim_copy().wait_recv()
    inside = me < parts - 1
    for s in range(slots):
        late = jnp.where(inside, rim_in[s], 0.0)
        end = tail[s]
        shifted_in = jnp.concatenate([jnp.zeros_like(late), late], axis=0)
        pre_grad_out[s, length - 2 * RIM : length, :] = (end + shifted_in).astype(BF16)
    rim_copy().wait_send()

    def drain(away, carry):
        back_copy(lax.rem(me + away, parts)).wait_send()
        return carry

    lax.fori_loop(1, parts, drain, 0)

    def drain_head(s, carry):
        tools.drain(s)
        return carry

    lax.fori_loop(0, slots, drain_head, 0)
    rings[0].finish()
    rings[1].finish()


def backward_call(parts, head_parts, heads, *operands):
    (
        mixer_grad, shifts_in, gated, mixer_rows_grad, normed, gate_grad, act, down_weight, residual, mask,
        pre, rim, ab, abt, taps, lanes, cols,
        queries, keys, value_rows, inverse, delta_rows, states, maps_in, up_part, gate_part, down_part,
    ) = operands
    slots, length, channels = pre.shape
    value_dim, key_dim = value_rows.shape[3], keys.shape[3]
    width, shard = normed.shape[2], residual.shape[2]
    sds = jax.ShapeDtypeStruct
    dma = pltpu.SemaphoreType.DMA
    out_shape = (padded_rows(gated.shape[2], parts), width)
    first_shape = (width, gate_grad.shape[2])
    outs = (
        sds(residual.shape, BF16), sds(pre.shape, BF16), sds(ab.shape, F32), sds((8, channels), F32),
        sds((8, LANES), F32), sds(up_part.shape, BF16), sds(gate_part.shape, BF16), sds(down_part.shape, BF16),
        sds(out_shape, BF16), sds(first_shape, BF16),
    )
    unit = pltpu.VMEM(states.shape, BF16)
    edge = pltpu.VMEM((slots, RIM, channels), F32)
    scratch = ([
        pltpu.VMEM(out_shape, BF16), pltpu.VMEM(first_shape, BF16),
        pltpu.VMEM((length + RIM, channels), F32), pltpu.VMEM((length + 2 * RIM, channels), F32),
        pltpu.VMEM((slots, 2 * RIM, channels), F32), edge, edge, unit, unit,
        dma((parts - 1,)), dma((parts - 1,)), dma((1,)), dma((1,)),
    ]
    + ring_scratch(parts, [up_part.shape, gate_part.shape])
    + ring_scratch(parts, [down_part.shape, out_shape, first_shape])
    + head_scratch(1, 1, slots, head_parts, length, shard))
    return staged_call(
        functools.partial(backward_kernel, slots, heads, key_dim, value_dim, parts, head_parts),
        operands, outs, scratch, 3,
        late=((2, 3, 4, 5, 26), (6, 7), (0, 8, 9, 10, 11, 12, 13, 17, 18, 19, 20, 21, 22)),
        kept=(5, 6, 7, 8, 9), flops=5 * 10**10,
    )


def last_kernel(
    slots, head_parts, heads, parts, taps, arrive, leave,
    pre_grad, gate_grad, ab_grad, normed, query_weight, key_weight, value_weight, gate_weight, ab_weight, x_shard, inv_first,
    residual_grad, input_gain, gain_part, taps_grad, lane_grad, mixed_part,
    input_grad_out, unit_sum, value_sum, small_sum,
    unit_own, value_own, small_own, small_in, gain_own, gain_in, first_shard,
    small_send, small_recv, gain_send, gain_recv, *refs,
):
    head_refs = refs[12:]
    tools = head_tools(head_parts, head_refs, 1)
    rings = (
        ring_tools(parts, (unit_own,), (unit_sum,), refs[0:1], *refs[1:6]),
        ring_tools(parts, (value_own,), (value_sum,), refs[6:7], *refs[7:12]),
    )
    me, place = tools.me, tools.place
    length, shard = x_shard.shape[1], x_shard.shape[2]
    width = shard * head_parts
    channels = pre_grad.shape[2]
    unit_wide = unit_own.shape[1]
    barrier = pltpu.get_barrier_semaphore()
    tools.greet(barrier)

    def greet(away, carry):
        pl.semaphore_signal(
            barrier, inc=1, device_id=(lax.rem(place + away, parts), me), device_id_type=MESH
        )
        return carry

    lax.fori_loop(1, parts, greet, 0)

    def gain_copy(away):
        return remote(
            gain_own, gain_in.at[away - 1], gain_send.at[away - 1], gain_recv.at[away - 1],
            (place, lax.rem(me + away, head_parts)),
        )

    def small_copy(away):
        return remote(
            small_own, small_in.at[away - 1], small_send.at[away - 1], small_recv.at[away - 1],
            (lax.rem(place + away, parts), me),
        )

    def store_unit(start, size, block):
        unit_own[pl.ds(start, size), :] = block

    def store_value(start, size, block):
        value_own[pl.ds(start, size), :] = block

    weight_rows(normed, pre_grad[:, :, :unit_wide].reshape(-1, unit_wide), store_unit)
    pl.semaphore_wait(barrier, head_parts - 1 + parts - 1)
    rings[0].begin()
    weight_rows(normed, pre_grad[:, :, unit_wide:].reshape(-1, channels - unit_wide), store_value)
    rings[1].begin()
    def products(s, carry):
        low = ab_grad[s].astype(BF16)
        half = unit_wide // 2
        tools.send_part(
            0, s,
            raw(pre_grad[s, :, :half], query_weight[...], NT)
            + raw(pre_grad[s, :, half:unit_wide], key_weight[...], NT)
            + raw(pre_grad[s, :, unit_wide:], value_weight[...], NT)
            + raw(gate_grad[s], gate_weight[...], NT)
            + raw(low, ab_weight[...], NT),
        )
        rings[0].tick(s)
        rings[1].tick(s)
        return carry

    arrive(0)
    lax.fori_loop(0, slots, products, 0)
    arrive(1)

    def first_join(s, carry):
        tools.join_core(0, s)
        return carry

    lax.fori_loop(0, slots, first_join, 0)
    rings[0].tick(slots)
    rings[1].tick(slots)
    small_own[...] = jnp.zeros_like(small_own)
    gain_own[...] = gain_part[...]
    for away in range(1, head_parts):
        gain_copy(away).start()

    def second_join(s, carry):
        grad = tools.join_line(0, s)
        x = x_shard[s].astype(F32)
        inv = inv_first[s][:, 0:1]
        weighted = grad * input_gain[0:1, :]
        first_shard[s] = weighted
        tools.send_stat(0, s, jnp.sum(weighted * x, axis=1, keepdims=True))
        return carry + jnp.sum(grad * x * inv, axis=0, keepdims=True)

    gain_line = lax.fori_loop(0, slots, second_join, jnp.zeros((1, shard), F32))
    rings[0].tick(slots + 1)
    rings[1].tick(slots + 1)

    def input_rows(s, carry):
        stat = tools.join_stat(0, s) / width
        inv = inv_first[s][:, 0:1]
        input_grad_out[s] = residual_grad[s] + inv * (
            first_shard[s] - x_shard[s].astype(F32) * (inv * inv * stat)
        )
        return carry

    lax.fori_loop(0, slots, input_rows, 0)
    gain_total = gain_own[...]
    for away in range(1, head_parts):
        gain_copy(away).wait_recv()
        gain_total = gain_total + gain_in[away - 1]
    low = ab_grad[...].astype(BF16).reshape(-1, LANES)
    ab_lines = raw(low, normed[...].reshape(-1, width), TN)
    at = 0
    for lines in [taps_grad[t : t + 1, :] for t in range(taps)] + [
        ab_lines[t : t + 1, :] for t in range(2 * heads)
    ] + [gain_total[0:1, :], lane_grad[0:1, :], lane_grad[1:2, :], mixed_part[0:1, :], gain_line]:
        for j in range(lines.shape[1] // LANES):
            small_own[at : at + 1, :] = lines[:, j * LANES : (j + 1) * LANES]
            at += 1

    def small_start(away, carry):
        small_copy(away).start()
        return carry

    lax.fori_loop(1, parts, small_start, 0)

    def rest(k, carry):
        rings[0].tick(k)
        rings[1].tick(k)
        return carry

    lax.fori_loop(slots + 2, rings[0].ticks, rest, 0)
    small_sum[...] = small_own[...]

    def small_join(away, carry):
        small_copy(away).wait_recv()
        small_sum[...] += small_in[away - 1]
        small_copy(away).wait_send()
        return carry

    lax.fori_loop(1, parts, small_join, 0)
    for away in range(1, head_parts):
        gain_copy(away).wait_send()

    def drain(s, carry):
        tools.drain(s)
        return carry

    lax.fori_loop(0, slots, drain, 0)
    rings[0].finish()
    rings[1].finish()


def last_call(
    parts, head_parts, heads, taps, unit_wide, pre_grad, gate_grad, ab_grad, normed, query_weight, key_weight, value_weight, gate_weight, ab_weight,
    x_shard, inv_first, residual_grad, input_gain, gain_part, taps_grad, lane_grad, mixed_part,
):
    slots, length, shard = x_shard.shape
    width = shard * head_parts
    channels = pre_grad.shape[2]
    lines = (taps * channels + 2 * heads * width + gain_part.shape[1] + 2 * shard) // LANES + 2
    lines += -lines % 8
    sds = jax.ShapeDtypeStruct
    dma = pltpu.SemaphoreType.DMA
    operands = (
        pre_grad, gate_grad, ab_grad, normed, query_weight, key_weight, value_weight, gate_weight, ab_weight, x_shard, inv_first,
        residual_grad, input_gain, gain_part, taps_grad, lane_grad, mixed_part,
    )
    first, second = (width, unit_wide), (width, channels - unit_wide)
    outs = (sds((slots, length, shard), F32), sds(first, BF16), sds(second, BF16), sds((lines, LANES), F32))
    scratch = ([
        pltpu.VMEM(first, BF16), pltpu.VMEM(second, BF16), pltpu.VMEM((lines, LANES), F32), pltpu.VMEM((parts - 1, lines, LANES), F32),
        pltpu.VMEM(gain_part.shape, F32), pltpu.VMEM((head_parts - 1,) + gain_part.shape, F32),
        pltpu.VMEM((slots, length, shard), F32),
        dma((parts - 1,)), dma((parts - 1,)), dma((head_parts - 1,)), dma((head_parts - 1,)),
    ]
    + ring_scratch(parts, [first])
    + ring_scratch(parts, [second])
    + head_scratch(1, 1, slots, head_parts, length, shard))
    return staged_call(
        functools.partial(last_kernel, slots, head_parts, heads, parts, taps),
        operands, outs, scratch, 4, late=((4, 5, 6, 7, 8, 2, 1), (9, 10, 11, 12, 13, 14, 15, 16)),
        kept=(1, 2), flops=5 * 10**10,
    )


def per_device(
    hidden_in, lengths, input_gain, query_weight, key_weight, value_weight, alpha_weight, beta_weight,
    decay_log, decay_bias, query_kernel, key_kernel, value_kernel, gate_weight, output_gain,
    output_weight, mixed_gain, swiglu_gate, swiglu_up, swiglu_down, cotangent,
):
    slots, segment, width = hidden_in.shape
    heads = decay_log.shape[0]
    key_dim = query_kernel.shape[1] // heads
    value_dim = value_kernel.shape[1] // heads
    taps = query_kernel.shape[0]
    split_key = heads * key_dim
    channels = 2 * split_key + heads * value_dim
    head_parts = lax.axis_size("head")
    seq_parts = lax.axis_size("seq")
    shard = width // head_parts
    head_start = lax.axis_index("head") * shard

    position = lax.axis_index("seq") * segment + jnp.arange(segment)
    mask = (position[None, :] < lengths[:, None]).astype(F32)[:, :, None]
    lane_mask = jnp.broadcast_to(mask, (slots, segment, LANES))
    ab_weight = jnp.concatenate(
        [alpha_weight, beta_weight, jnp.zeros((width, LANES - 2 * heads), BF16)], axis=1
    )
    kernel = jnp.concatenate([query_kernel, key_kernel, value_kernel], axis=1).astype(F32)
    kernel = jnp.pad(kernel, ((0, 8 - taps), (0, 0)))
    rate = jnp.exp(decay_log)
    pad_heads = lambda v: jnp.pad(v, (0, LANES - heads))
    lane_gates = jnp.pad(jnp.stack([pad_heads(rate), pad_heads(decay_bias)]), ((0, 6), (0, 0)))
    pad_rows = lambda v: jnp.broadcast_to(jnp.pad(v, (0, 8 - heads))[:, None], (8, LANES))
    col_gates = jnp.concatenate([pad_rows(rate), pad_rows(decay_bias)], axis=0)
    gain_row = jnp.broadcast_to(output_gain[None, :], (8, value_dim))

    (
        query, key, value, inverse, eff, delta_rows, mixer, gated, normed_first, pre_all, gate_pre, x_low,
        inv_first, rim_pre, ab_pre, ab_rows, states, maps_in,
    ) = forward_call(
        seq_parts, head_parts, heads, hidden_in, jnp.broadcast_to(input_gain[None, :], (8, width)),
        query_weight, key_weight, value_weight, gate_weight, ab_weight, kernel, lane_gates, col_gates, gain_row,
    )
    (
        residual, activation, up_part, gate_part, down_part, residual_grad, mixer_rows_grad, mixer_grad,
        gate_grad, mixed_part, gain_part, shifts_in,
    ) = middle_call(
        seq_parts, head_parts, heads, gated, x_low, cotangent, lane_mask, output_weight, swiglu_gate.T,
        swiglu_up.T, swiglu_down, jnp.broadcast_to(mixed_gain[None, :], (8, shard)), mixer, gate_pre, gain_row, eff,
    )
    (
        block_out, pre_grad, ab_grad, taps_grad, lane_grad, up_sum, gate_sum, down_sum, out_sum, gate_first_sum
    ) = backward_call(
        seq_parts, head_parts, heads, mixer_grad, shifts_in, gated, mixer_rows_grad, normed_first, gate_grad,
        activation, swiglu_down, residual, lane_mask, pre_all, rim_pre, ab_pre, ab_rows, kernel, lane_gates,
        col_gates, query, key, value, inverse, delta_rows, states, maps_in, up_part, gate_part, down_part,
    )
    gain_shard = lax.dynamic_slice_in_dim(input_gain, head_start, shard, 0)
    input_grad, unit_sum, value_sum, small_sum = last_call(
        seq_parts, head_parts, heads, taps, 2 * split_key, pre_grad, gate_grad, ab_grad,
        normed_first, query_weight, key_weight, value_weight, gate_weight, ab_weight, x_low,
        inv_first, residual_grad,
        jnp.broadcast_to(gain_shard[None, :], (8, shard)), gain_part, taps_grad, lane_grad, mixed_part,
    )
    hidden = swiglu_gate.shape[1]
    flat_small = small_sum.reshape(-1)
    pieces, at = [], 0
    for size in (taps * channels, 2 * heads * width, value_dim, LANES, LANES, shard, shard):
        pieces.append(flat_small[at : at + size])
        at += size
    taps_sum = pieces[0].reshape(taps, channels)
    ab_sum = pieces[1].reshape(2 * heads, width).T
    value_share = value_dim // head_parts
    output_gain_grad = lax.dynamic_slice_in_dim(
        pieces[2], lax.axis_index("head") * value_share, value_share, 0
    )
    return (
        block_out,
        input_grad,
        pieces[6],
        unit_sum[:, :split_key].astype(F32),
        unit_sum[:, split_key:].astype(F32),
        value_sum.astype(F32),
        ab_sum[:, :heads],
        ab_sum[:, heads:],
        pieces[3][:heads],
        pieces[4][:heads],
        taps_sum[:, :split_key],
        taps_sum[:, split_key : 2 * split_key],
        taps_sum[:, 2 * split_key :],
        gate_first_sum.astype(F32),
        output_gain_grad,
        out_sum[: heads * value_dim].astype(F32),
        pieces[5],
        gate_sum[:hidden].astype(F32).T,
        up_sum[:hidden].astype(F32).T,
        down_sum[:hidden].astype(F32),
    )


def solution(mesh):
    seq, cols, lines = P(None, "seq", None), P(None, "head"), P("head", None)
    one = P("head")
    placed = (
        seq, P(), P(), cols, cols, cols, cols, cols, one, one, cols, cols, cols, cols, P(), lines, one,
        cols, cols, lines, seq,
    )
    both = P(None, "seq", "head")
    return jax.shard_map(
        per_device,
        mesh=mesh,
        in_specs=placed,
        out_specs=(
            both, both, one, cols, cols, cols, cols, cols, one, one, cols, cols, cols, cols, one, lines,
            one, cols, cols, lines,
        ),
        check_vma=False,
    )
```

```python
import functools
import types

import jax
import jax.numpy as jnp
from jax import lax
from jax.experimental import pallas as pl
from jax.experimental.pallas import tpu as pltpu
from jax.sharding import PartitionSpec as P

NORM_EPSILON = 1e-05
UNIT_EPSILON = 1e-06
RIM = 8
LANES = 128
F32 = jnp.float32
BF16 = jnp.bfloat16
VMEM_LIMIT = 58 * 1024 * 1024

NN = (((1,), (0,)), ((), ()))
NT = (((1,), (1,)), ((), ()))
TN = (((0,), (0,)), ((), ()))


def split(x):
    high = x.astype(BF16)
    return high, (x - high.astype(F32)).astype(BF16)


def raw(a, b, dims):
    return lax.dot_general(a, b, dims, preferred_element_type=F32)


def mm(a, b, dims=NN):
    a_high, a_low = a if isinstance(a, tuple) else (a, None)
    b_high, b_low = b if isinstance(b, tuple) else (b, None)
    total = raw(a_high, b_high, dims)
    if a_low is not None:
        total = total + raw(a_low, b_high, dims)
    if b_low is not None:
        total = total + raw(a_high, b_low, dims)
    return total


def sigmoid(x):
    return 1.0 / (1.0 + jnp.exp(-x))


def softplus(x):
    return jnp.maximum(x, 0.0) + jnp.log1p(jnp.exp(-jnp.abs(x)))


def grid_masks(size):
    row = lax.broadcasted_iota(jnp.int32, (size, size), 0)
    col = lax.broadcasted_iota(jnp.int32, (size, size), 1)
    return row, col


def rough_inverses(blocks):
    size = blocks[0].shape[0]
    row, col = grid_masks(size)
    apart = row ^ col
    base = 8
    starts = [jnp.where(apart < base, block, 0.0) for block in blocks]
    ones = [start.astype(BF16) for start in starts]
    squares = [raw(one, one, NN) for one in ones]
    lows = [square.astype(BF16) for square in squares]
    fourths = [raw(low, low, NN).astype(BF16) for low in lows]
    cubes = [raw(one, low, NN) for one, low in zip(ones, lows)]
    eye = jnp.where(row == col, 1.0, 0.0)
    found = [eye - start + square - cube for start, square, cube in zip(starts, squares, cubes)]
    found = [one + raw(one.astype(BF16), fourth, NN) for one, fourth in zip(found, fourths)]
    while base < size:
        ring = (apart >= base) & (apart < 2 * base)
        offs = [jnp.where(ring, block, 0.0).astype(BF16) for block in blocks]
        lows = [one.astype(BF16) for one in found]
        offs = [raw(low, off, NN).astype(BF16) for low, off in zip(lows, offs)]
        found = [one - raw(off, low, NN) for one, off, low in zip(found, offs, lows)]
        base *= 2
    return found


def unit_inverses(lowers, row, col):
    size = lowers[0].shape[0]
    half = size // 2
    count = len(lowers)
    found = rough_inverses([low[:half, :half] for low in lowers] + [low[half:, half:] for low in lowers])
    corners = [
        raw(second.astype(BF16), low[half:, :half].astype(BF16), NN).astype(BF16)
        for second, low in zip(found[count:], lowers)
    ]
    corners = [-raw(corner, first.astype(BF16), NN) for corner, first in zip(corners, found[:count])]
    zero = jnp.zeros((half, half), F32)
    roughs = [
        jnp.concatenate(
            [jnp.concatenate([first, zero], axis=1), jnp.concatenate([corner, second], axis=1)], axis=0
        )
        for first, corner, second in zip(found[:count], corners, found[count:])
    ]
    parts = [split(rough) for rough in roughs]
    eye = jnp.where(row == col, 1.0, 0.0)
    lefts = [
        (eye - rough - mm(split(low), part)).astype(BF16) for rough, low, part in zip(roughs, lowers, parts)
    ]
    return [rough + raw(part[0], left, NN) for rough, part, left in zip(roughs, parts, lefts)]


def gates_of(ab, rate, bias):
    return -rate * softplus(ab + bias), sigmoid(ab)


def decay_of(log_col, log_row, row, col):
    seen = row >= col
    cum_col = jnp.sum(jnp.where(seen, log_row, 0.0), axis=1, keepdims=True)
    cum_row = jnp.sum(jnp.where(row <= col, log_col, 0.0), axis=0, keepdims=True)
    end = jnp.sum(log_row, axis=1, keepdims=True)
    decayed = jnp.where(seen, jnp.exp(jnp.where(seen, cum_col - cum_row, 0.0)), 0.0)
    return cum_col, cum_row, end, decayed


def convolve(ext, taps_ref, length):
    taps = 4
    total = taps_ref[0:1, :] * ext[pl.ds(RIM - taps + 1, length), :]
    for tap in range(1, taps):
        total = total + taps_ref[tap : tap + 1, :] * ext[pl.ds(RIM - taps + 1 + tap, length), :]
    return total


MESH = pl.DeviceIdType.MESH


def remote(src, dst, send_sem, recv_sem, device):
    return pltpu.make_async_remote_copy(
        src_ref=src, dst_ref=dst, send_sem=send_sem, recv_sem=recv_sem, device_id=device, device_id_type=MESH
    )


def turn_to_row(column, row, col):
    return jnp.sum(jnp.where(row == col, column, 0.0), axis=0, keepdims=True)


def turn_to_column(line, row, col):
    return jnp.sum(jnp.where(row == col, line, 0.0), axis=1, keepdims=True)


def staged_call(kernel, operands, outs, scratch, collective_id, late=(), leaving=(), kept=(), slots=0, flops=10**10):
    dma = pltpu.SemaphoreType.DMA
    order = [i for group in late for i in group]
    vmem, free = pl.BlockSpec(memory_space=pltpu.VMEM), pl.BlockSpec(memory_space=pl.ANY)
    count, total = len(operands), len(operands) + len(outs)
    stages = [pltpu.VMEM(operands[i].shape, operands[i].dtype) for i in order]
    stages += [pltpu.VMEM(outs[i].shape, outs[i].dtype) for i in leaving]
    sems = [dma((max(1, len(order)),)), dma((max(1, len(leaving)), max(1, slots)))]

    def body(*refs):
        ins, results, rest = list(refs[:count]), list(refs[count:total]), refs[total:]
        held, (in_sem, out_sem), rest = rest[: len(stages)], rest[len(stages) : len(stages) + 2], rest[len(stages) + 2 :]
        copies = {}
        for j, i in enumerate(order):
            copies[i] = pltpu.make_async_copy(ins[i], held[j], in_sem.at[j])
            copies[i].start()
            ins[i] = held[j]
        targets = {}
        for j, i in enumerate(leaving):
            targets[i] = (results[i], held[len(order) + j], j)
            results[i] = held[len(order) + j]
        left = {}

        def arrive(group):
            for i in late[group]:
                copies[i].wait()

        def out_copy(i, slot):
            target, source, j = targets[i]
            if slot is None:
                return pltpu.make_async_copy(source, target, out_sem.at[j, 0])
            return pltpu.make_async_copy(source.at[slot], target.at[slot], out_sem.at[j, slot])

        def leave(slot, *indices):
            for i in indices:
                left[i] = slot is not None
                out_copy(i, slot).start()

        kernel(arrive, leave, *ins, *results, *rest)
        for i in leaving:
            for slot in range(slots) if left[i] else (None,):
                out_copy(i, slot).wait()

    late_set = set(order)
    return pl.pallas_call(
        body,
        in_specs=[free if i in late_set else vmem for i in range(count)],
        out_specs=[free if i in leaving or i in kept else vmem for i in range(len(outs))],
        out_shape=tuple(outs),
        scratch_shapes=stages + sems + list(scratch),
        compiler_params=pltpu.CompilerParams(
            collective_id=collective_id, has_side_effects=True, vmem_limit_bytes=VMEM_LIMIT
        ),
        cost_estimate=pl.CostEstimate(flops=flops, bytes_accessed=60 * 10**6, transcendentals=0),
    )(*operands)


class Units:
    def __init__(self, count, pairs):
        self.count, self.pairs, self.share = count, pairs, count // pairs
        self.me, self.other = lax.axis_index("seq"), lax.axis_index("head")

    def ahead(self, place):
        return lax.rem(place - self.me + self.count, self.count) - 1

    def behind(self, place):
        return lax.rem(self.me - place + self.count, self.count) - 1

    def to_owner(self, src, dst, send, recv, unit):
        return remote(src, dst.at[self.me], send.at[self.ahead(unit)], recv.at[self.ahead(unit)], (unit, self.other))

    def at_owner(self, src, dst, send, recv, place):
        return remote(src, dst.at[place], send.at[self.behind(place)], recv.at[self.behind(place)], (place, self.other))

    def pieces(self, value):
        size = value.shape[0] // self.share
        return [value[i * size : (i + 1) * size] for i in range(self.share)]

    def whole(self, ref, pair):
        return jnp.concatenate([ref[pair * self.share + i] for i in range(self.share)], axis=0)

    def greet(self, barrier):
        def one(away, carry):
            pl.semaphore_signal(
                barrier, inc=1, device_id=(lax.rem(self.me + away, self.count), self.other), device_id_type=MESH
            )
            return carry

        lax.fori_loop(1, self.count, one, 0)


def forward_kernel(
    slots, heads, key_dim, value_dim, parts, arrive, leave,
    hidden, input_gain, query_weight, key_weight, value_weight, gate_weight, ab_weight, taps_ref, lanes, cols, gain,
    query_out, key_out, value_out, inverse_out, eff_out, rows_out, mixer_out, gated_out,
    normed, pre, gate, x_out, inv_out, rim, ab, abt, states, maps_in,
    ext, rim_rows, delta, mix, maps_low, shifts_low, shifts_in, state_send, edge_send, edge_recv,
    map_send, map_recv, shift_send, shift_recv, back_send, back_recv,
):
    length = pre.shape[1]
    units = Units(parts, slots * heads)
    me = units.me
    barrier = pltpu.get_barrier_semaphore()
    units.greet(barrier)
    row, col = grid_masks(length)
    key_start = heads * key_dim
    value_start = 2 * heads * key_dim
    width = hidden.shape[2]
    shard = x_out.shape[2]
    edge = rim_rows.shape[1]
    shard_start = pl.multiple_of(units.other * shard, shard)

    def edge_copy():
        return remote(
            hidden.at[:, length - edge : length, :], rim_rows, edge_send.at[0], edge_recv.at[0],
            (lax.rem(me + 1, parts), units.other),
        )

    def norm_rows(x):
        inv = lax.rsqrt(jnp.sum(x * x, axis=1, keepdims=True) / width + NORM_EPSILON)
        return inv, (x * inv * input_gain[0:1, :]).astype(BF16)

    def project(s, carry):
        inv, low = norm_rows(hidden[s].astype(F32))
        normed[s] = low
        x_out[s] = hidden[s, :, pl.ds(shard_start, shard)]
        inv_out[s] = jnp.broadcast_to(inv, (length, LANES))
        pre[s, :, :key_start] = raw(low, query_weight[...], NN).astype(BF16)
        pre[s, :, key_start:value_start] = raw(low, key_weight[...], NN).astype(BF16)
        pre[s, :, value_start:] = raw(low, value_weight[...], NN).astype(BF16)
        gates = raw(low, ab_weight[...], NN)
        ab[s] = gates
        abt[s] = jnp.transpose(gates)[0:8, :]
        leave(s, 8, 9, 11, 12)

        @pl.when(s == 0)
        def _():
            pl.semaphore_wait(barrier, parts - 1)
            edge_copy().start()

        return carry

    lax.fori_loop(0, slots, project, 0)
    edge_copy().wait_recv()
    _, edge_low = norm_rows(rim_rows[...].reshape(slots * edge, width).astype(F32))
    edge_pre = jnp.concatenate(
        [raw(edge_low, weight[...], NN) for weight in (query_weight, key_weight, value_weight)], axis=1
    ).astype(BF16).astype(F32)
    for s in range(slots):
        rim[s] = jnp.where(me > 0, edge_pre[(s + 1) * edge - RIM : (s + 1) * edge, :], 0.0)

    def map_copy(unit):
        return units.to_owner(maps_low.at[unit // units.share], maps_in, map_send, map_recv, unit)

    def shift_copy(unit):
        return units.to_owner(shifts_low.at[unit], shifts_in, shift_send, shift_recv, unit)

    def back_copy(place):
        ahead = units.ahead(place)
        return remote(
            state_send.at[place], states.at[me], back_send.at[ahead], back_recv.at[ahead], (place, units.other)
        )

    def back_arrival(unit):
        behind = units.behind(unit)
        return remote(
            state_send.at[unit], states.at[unit], back_send.at[behind], back_recv.at[behind], (unit, units.other)
        )

    together = 2 if slots % 2 == 0 else 1

    def group_terms(group, carry):
        pairs = []
        for i in range(together):
            s = group * together + i
            ext[i, 0:RIM, :] = rim[s]
            ext[i, RIM : RIM + length, :] = pre[s].astype(F32)
            conv = convolve(ext.at[i], taps_ref, length)
            active = conv * sigmoid(conv)
            log_cols, strength_cols = gates_of(ab[s], lanes[0:1, :], lanes[1:2, :])
            log_rows, strength_rows = gates_of(abt[s], cols[0:8, 0:1], cols[8:16, 0:1])
            for h in range(heads):
                query_act = active[:, h * key_dim : (h + 1) * key_dim]
                key_act = active[:, key_start + h * key_dim : key_start + (h + 1) * key_dim]
                value_act = active[:, value_start + h * value_dim : value_start + (h + 1) * value_dim]
                query_scale = lax.rsqrt(jnp.sum(query_act * query_act, axis=1, keepdims=True) + UNIT_EPSILON)
                key_scale = lax.rsqrt(jnp.sum(key_act * key_act, axis=1, keepdims=True) + UNIT_EPSILON)
                query = (query_act * query_scale * key_dim ** (-0.5)).astype(BF16)
                key = (key_act * key_scale).astype(BF16)
                value = value_act.astype(BF16)
                query_out[s, h] = query
                key_out[s, h] = key
                value_out[s, h] = value
                cum_col, cum_row, end, decayed = decay_of(
                    log_cols[:, h : h + 1], log_rows[h : h + 1, :], row, col
                )
                pairs.append(
                    types.SimpleNamespace(
                        s=s, h=h, query=query, key=key, value=value, cum_col=cum_col, cum_row=cum_row, end=end,
                        decayed=decayed, strength=strength_cols[:, heads + h : heads + h + 1],
                        strength_row=strength_rows[heads + h : heads + h + 1, :],
                    )
                )
        lowers = [
            jnp.where(row > col, pair.strength * pair.decayed * mm(pair.key, pair.key, NT), 0.0) for pair in pairs
        ]
        for pair, inverse in zip(pairs, unit_inverses(lowers, row, col)):
            inverse_out[pair.s, pair.h] = inverse
            pair.scaled = inverse * pair.strength_row
        for pair in pairs:
            pair.delta = mm(split(pair.scaled), pair.value)
            pair.mix = mm(split(pair.scaled * jnp.exp(pair.cum_row)), pair.key)
            delta[pair.s, pair.h] = pair.delta
            mix[pair.s, pair.h] = pair.mix
        small_row, small_col = grid_masks(key_dim)
        for pair in pairs:
            end_weight = jnp.exp(pair.end - pair.cum_col)
            moved = jnp.where(small_row == small_col, jnp.exp(pair.end), 0.0)
            place = pair.s * heads + pair.h
            maps_low[place] = (moved - mm(split(pair.mix * end_weight), pair.key, TN)).astype(BF16)
            for i, piece in enumerate(units.pieces(mm(split(pair.delta * end_weight), pair.key, TN).astype(BF16))):
                shifts_low[place * units.share + i] = piece
        for i in range(together):
            leave(group * together + i, 0, 1, 2, 3)
        for i in range(together * heads * units.share):
            unit = group * together * heads * units.share + i

            @pl.when(unit != me)
            def _(unit=unit):
                map_copy(unit).start()
                shift_copy(unit).start()

            @pl.when(unit == me)
            def _(unit=unit):
                maps_in[unit] = maps_low[unit // units.share]
                shifts_in[unit] = shifts_low[unit]

        return carry

    lax.fori_loop(0, slots // together, group_terms, 0)

    def within(s):
        gate[s] = raw(normed[s], gate_weight[...], NN)
        log_cols, _ = gates_of(ab[s], lanes[0:1, :], lanes[1:2, :])
        log_rows, _ = gates_of(abt[s], cols[0:8, 0:1], cols[8:16, 0:1])
        for h in range(heads):
            query = query_out[s, h]
            cum_col, _, _, decayed = decay_of(log_cols[:, h : h + 1], log_rows[h : h + 1, :], row, col)
            scores = split(decayed * mm(query, key_out[s, h], NT))
            eff_out[s, h] = jnp.exp(cum_col) * query.astype(F32) - mm(scores, split(mix[s, h]))
            mixer_out[s, h] = mm(scores, split(delta[s, h]))
        leave(s, 4, 10)

    def within_group(group, carry):
        for i in range(together):
            within(group * together + i)
        return carry

    early = slots // together // 2
    lax.fori_loop(0, early, within_group, 0)

    def scan(place, state):
        low = state.astype(BF16)

        @pl.when(place != me)
        def _():
            state_send[place] = low
            back_copy(place).start()
            units.at_owner(maps_low.at[0], maps_in, map_send, map_recv, place).wait_recv()
            units.at_owner(shifts_low.at[0], shifts_in, shift_send, shift_recv, place).wait_recv()

        @pl.when(place == me)
        def _():
            states[place] = low

        return mm(split(state), maps_in[place]) + shifts_in[place].astype(F32)

    lax.fori_loop(0, parts, scan, jnp.zeros((value_dim // units.share, key_dim), F32))

    lax.fori_loop(early, slots // together, within_group, 0)

    def emit(s, carry):
        for i in range(heads * units.share):
            unit = s * heads * units.share + i

            @pl.when(unit != me)
            def _(unit=unit):
                back_arrival(unit).wait_recv()

        for h in range(heads):
            state = units.whole(states, s * heads + h)
            rows_out[s, h] = delta[s, h] - mm(split(mix[s, h]), state, NT)
            mixer = mixer_out[s, h] + mm(split(eff_out[s, h]), state, NT)
            mixer_out[s, h] = mixer
            scale = lax.rsqrt(jnp.sum(mixer * mixer, axis=1, keepdims=True) / value_dim + NORM_EPSILON)
            here = slice(h * value_dim, (h + 1) * value_dim)
            gate_h = gate[s, :, here]
            gated_out[s, :, here] = (mixer * scale * gain[0:1, :] * (gate_h * sigmoid(gate_h))).astype(BF16)
        leave(s, 5, 6, 7)
        return carry

    lax.fori_loop(0, slots, emit, 0)

    def drain(away, carry):
        unit = lax.rem(me + away, parts)
        map_copy(unit).wait_send()
        shift_copy(unit).wait_send()
        back_copy(unit).wait_send()
        return carry

    lax.fori_loop(1, parts, drain, 0)
    edge_copy().wait_send()


def forward_call(parts, head_parts, heads, *operands):
    hidden, query_weight, value_weight, gate_weight = operands[0], operands[2], operands[4], operands[5]
    slots, length, width = hidden.shape
    key_dim, value_dim = query_weight.shape[1] // heads, value_weight.shape[1] // heads
    channels = heads * (2 * key_dim + value_dim)
    share = parts // (slots * heads)
    sds = jax.ShapeDtypeStruct
    dma = pltpu.SemaphoreType.DMA
    per = lambda kind, *tail: sds((slots, heads) + tail, kind)
    each = lambda kind, *tail: sds((slots,) + tail, kind)
    unit = (parts, value_dim // share, key_dim)
    outs = (
        per(BF16, length, key_dim), per(BF16, length, key_dim), per(BF16, length, value_dim),
        per(F32, length, length), per(F32, length, key_dim), per(F32, length, value_dim),
        per(F32, length, value_dim), each(BF16, length, heads * value_dim),
        each(BF16, length, width), each(BF16, length, channels), each(F32, length, heads * value_dim),
        each(BF16, length, width // head_parts), each(F32, length, LANES), each(F32, RIM, channels),
        each(F32, length, LANES), each(F32, 8, length),
        sds(unit, BF16), sds((parts, key_dim, key_dim), BF16),
    )
    scratch = [
        pltpu.VMEM((2, length + RIM, channels), F32),
        pltpu.VMEM((slots, 2 * RIM, width), BF16),
        pltpu.VMEM((slots, heads, length, value_dim), F32),
        pltpu.VMEM((slots, heads, length, key_dim), F32),
        pltpu.VMEM((slots * heads, key_dim, key_dim), BF16),
        pltpu.VMEM(unit, BF16), pltpu.VMEM(unit, BF16), pltpu.VMEM(unit, BF16), dma((1,)), dma((1,)),
    ] + [dma((parts - 1,))] * 6
    return staged_call(
        functools.partial(forward_kernel, slots, heads, key_dim, value_dim, parts),
        operands, outs, scratch, 2, leaving=tuple(range(13)), slots=slots,
    )


def head_scratch(kinds, stats, slots, head_parts, length, shard):
    lines = head_parts // 2
    dma = pltpu.SemaphoreType.DMA
    return [
        pltpu.VMEM((head_parts, length, shard), F32),
        pltpu.VMEM((min(kinds, 2), slots, lines, length, shard), F32),
        pltpu.VMEM((kinds, slots, lines, length, shard), BF16),
        pltpu.VMEM((kinds, slots, lines, length, shard), BF16),
        pltpu.VMEM((kinds, slots, lines - 1, length, shard), BF16),
        pltpu.VMEM((kinds, slots, lines - 1, length, shard), BF16),
        pltpu.VMEM((stats, slots, 8, length), F32),
        pltpu.VMEM((stats, slots, head_parts - 1, 8, length), F32),
        dma((kinds, slots, lines)), dma((kinds, slots, lines)),
        dma((kinds, slots, lines - 1)), dma((kinds, slots, lines - 1)),
        dma((stats, slots, head_parts - 1)), dma((stats, slots, head_parts - 1)),
    ]


def head_tools(head_parts, refs, stats):
    whole_part, part, low, from_core, to_line, from_line, stat_own, stat_in = refs[:8]
    core_send, core_recv, line_send, line_recv, stat_send, stat_recv = refs[8:]
    me = lax.axis_index("head")
    place = lax.axis_index("seq")
    lines = head_parts // 2
    core = lax.rem(me, 2)
    line = me // 2
    sibling = 2 * line + (1 - core)
    length, shard = whole_part.shape[1:]
    row, col = grid_masks(length)

    def greet(barrier):
        for away in range(1, head_parts):
            pl.semaphore_signal(
                barrier, inc=1, device_id=(place, lax.rem(me + away, head_parts)), device_id_type=MESH
            )

    def core_copy(kind, s, y):
        return remote(
            low.at[kind, s, y], from_core.at[kind, s, y],
            core_send.at[kind, s, y], core_recv.at[kind, s, y], (place, sibling),
        )

    def line_copy(kind, s, away):
        return remote(
            to_line.at[kind, s, away - 1], from_line.at[kind, s, away - 1],
            line_send.at[kind, s, away - 1], line_recv.at[kind, s, away - 1],
            (place, 2 * lax.rem(line + away, lines) + core),
        )

    def stat_copy(kind, s, away):
        return remote(
            stat_own.at[kind, s], stat_in.at[kind, s, away - 1],
            stat_send.at[kind, s, away - 1], stat_recv.at[kind, s, away - 1],
            (place, lax.rem(me + away, head_parts)),
        )

    def send_part(kind, s, value):
        for j in range(head_parts):
            whole_part[j] = value[:, j * shard : (j + 1) * shard]
        for y in range(lines):
            low[kind, s, y] = whole_part[2 * y + (1 - core)].astype(BF16)
            core_copy(kind, s, y).start()
            part[kind % 2, s, y] = whole_part[2 * y + core]

    def join_core(kind, s):
        for y in range(lines):
            core_copy(kind, s, y).wait_recv()
        for away in range(1, lines):
            y = lax.rem(line + away, lines)
            joined = part[kind % 2, s, y] + from_core[kind, s, y].astype(F32)
            to_line[kind, s, away - 1] = joined.astype(BF16)
            line_copy(kind, s, away).start()
        part[kind % 2, s, line] = part[kind % 2, s, line] + from_core[kind, s, line].astype(F32)

    def join_line(kind, s):
        total = part[kind % 2, s, line]
        for away in range(1, lines):
            line_copy(kind, s, away).wait_recv()
            total = total + from_line[kind, s, away - 1].astype(F32)
        return total

    def send_stat(kind, s, column):
        stat_own[kind, s] = jnp.broadcast_to(turn_to_row(column, row, col), (8, length))
        for away in range(1, head_parts):
            stat_copy(kind, s, away).start()

    def join_stat(kind, s):
        total = stat_own[kind, s]
        for away in range(1, head_parts):
            stat_copy(kind, s, away).wait_recv()
            total = total + stat_in[kind, s, away - 1]
        return turn_to_column(total[0:1, :], row, col)

    def drain(s):
        for kind in range(low.shape[0]):
            for y in range(lines):
                core_copy(kind, s, y).wait_send()
            for away in range(1, lines):
                line_copy(kind, s, away).wait_send()
        for kind in range(stats):
            for away in range(1, head_parts):
                stat_copy(kind, s, away).wait_send()

    return types.SimpleNamespace(
        me=me, place=place, lines=lines, core=core, line=line, sibling=sibling, greet=greet,
        send_part=send_part, join_core=join_core, join_line=join_line, send_stat=send_stat,
        join_stat=join_stat, drain=drain,
    )


def weight_rows(left, right, store):
    wide = left.shape[2]
    step = min(wide, 256)
    steps = wide // step

    def one(j, carry):
        start = pl.multiple_of(j * step, step)
        block = left[:, :, pl.ds(start, step)]
        store(start, step, raw(block.reshape(-1, step), right, TN).astype(BF16))
        return carry

    lax.fori_loop(0, steps, one, 0)
    if wide % step:
        rest = wide % step
        block = left[:, :, steps * step :]
        store(steps * step, rest, raw(block.reshape(-1, rest), right, TN).astype(BF16))


def middle_kernel(
    slots, head_parts, parts, heads, arrive, leave,
    gated, x_shard, cotangent, mask, out_weight, gate_weight, up_weight,
    down_weight, gain, mixer, gate, gain_row, eff,
    block_out, gate_part, residual_grad_out, mixer_rows_grad, mixer_grad, gate_grad_out,
    gain_grad_out, output_gain_grad, shifts_in, down_part, up_part,
    residual, act_all, up_grad_all, gate_grad_all,
    inverse, spread, shifts_low, shift_send, shift_recv,
    spread_line_send, spread_line_recv, spread_core_send, spread_core_recv,
    *refs,
):
    tools = head_tools(head_parts, refs, 2)
    me, place, lines, core, line, sibling = (
        tools.me, tools.place, tools.lines, tools.core, tools.line, tools.sibling
    )
    send_part, join_core, join_line = tools.send_part, tools.join_core, tools.join_line
    send_stat, join_stat = tools.send_stat, tools.join_stat
    length, shard = x_shard.shape[1], x_shard.shape[2]
    width = shard * head_parts
    hidden = gate_weight.shape[0]
    value_dim = mixer.shape[3]
    units = Units(parts, slots * heads)

    barrier = pltpu.get_barrier_semaphore()
    tools.greet(barrier)
    units.greet(barrier)
    gain_grad_out[...] = jnp.zeros_like(gain_grad_out)
    output_gain_grad[...] = jnp.zeros_like(output_gain_grad)
    pl.semaphore_wait(barrier, head_parts - 1 + parts - 1)

    def shift_copy(unit):
        return units.to_owner(shifts_low.at[unit], shifts_in, shift_send, shift_recv, unit)

    def spread_line_copy(kind, s, away):
        return remote(
            spread.at[kind, s, me], spread.at[kind, s, me],
            spread_line_send.at[kind, s, away - 1], spread_line_recv.at[kind, s, away - 1],
            (place, 2 * lax.rem(line + away, lines) + core),
        )

    def spread_core_copy(kind, s, away):
        y = lax.rem(line + away, lines)
        return remote(
            spread.at[kind, s, 2 * y + core], spread.at[kind, s, 2 * y + core],
            spread_core_send.at[kind, s, away], spread_core_recv.at[kind, s, away], (place, sibling),
        )

    def spread_core_arrival(kind, s, away):
        y = lax.rem(line + away, lines)
        return remote(
            spread.at[kind, s, 2 * y + (1 - core)], spread.at[kind, s, 2 * y + (1 - core)],
            spread_core_send.at[kind, s, away], spread_core_recv.at[kind, s, away], (place, sibling),
        )

    def spread_line_arrival(kind, s, away):
        y = lax.rem(line + lines - away, lines)
        return remote(
            spread.at[kind, s, 2 * y + core], spread.at[kind, s, 2 * y + core],
            spread_line_send.at[kind, s, away - 1], spread_line_recv.at[kind, s, away - 1],
            (place, 2 * y + core),
        )

    def send_spread(kind, s, value):
        spread[kind, s, me] = value
        for away in range(1, lines):
            spread_line_copy(kind, s, away).start()
        spread_core_copy(kind, s, 0).start()

    def pass_spread(kind, s):
        for away in range(1, lines):
            spread_line_arrival(kind, s, lines - away).wait_recv()
            spread_core_copy(kind, s, away).start()

    def take_spread(kind, s):
        for away in range(lines):
            spread_core_arrival(kind, s, away).wait_recv()
        return jnp.concatenate([spread[kind, s, j] for j in range(head_parts)], axis=1)

    def attention(s):
        send_part(0, s, raw(gated[s], out_weight[...], NN))

    def rows_in(s):
        total = x_shard[s].astype(F32) + mask[s][:, 0:1] * join_line(0, s)
        residual[s] = total
        send_stat(0, s, jnp.sum(total * total, axis=1, keepdims=True))

    def norm_second(s):
        inv = lax.rsqrt(join_stat(0, s) / width + NORM_EPSILON)
        inverse[s] = jnp.broadcast_to(inv, (length, LANES))
        send_spread(0, s, (residual[s] * inv * gain[0:1, :]).astype(BF16))

    def swiglu(s):
        normed = take_spread(0, s)
        valid = mask[s][:, 0:1]
        gate_values = raw(normed, gate_weight[...], NT)
        up_values = raw(normed, up_weight[...], NT)
        act_grad = raw(cotangent[s], down_weight[...], NT) * valid
        sig = sigmoid(gate_values)
        silu = gate_values * sig
        act_all[s] = (silu * up_values * valid).astype(BF16)
        up_grad = (act_grad * silu).astype(BF16)
        gate_grad = (act_grad * up_values * sig * (1.0 + gate_values * (1.0 - sig))).astype(BF16)
        up_grad_all[s] = up_grad
        gate_grad_all[s] = gate_grad
        send_part(1, s, raw(up_grad, up_weight[...], NN) + raw(gate_grad, gate_weight[...], NN))

    def swiglu_out(s):
        send_part(2, s, raw(act_all[s], down_weight[...], NN))

    def block_rows(s):
        block_out[s] = (residual[s] + mask[s][:, 0:1] * join_line(2, s)).astype(BF16)
        leave(s, 0)

    def norm_back(s):
        grad = join_line(1, s)
        inv = inverse[s][:, 0:1]
        gain_grad_out[0:1, :] += jnp.sum(grad * residual[s] * inv, axis=0, keepdims=True)
        weighted = grad * gain[0:1, :]
        residual_grad_out[s] = weighted
        send_stat(1, s, jnp.sum(weighted * residual[s], axis=1, keepdims=True))

    def residual_back(s):
        stat = join_stat(1, s) / width
        inv = inverse[s][:, 0:1]
        cot = cotangent[s, :, pl.ds(pl.multiple_of(me * shard, shard), shard)].astype(F32)
        grad = cot + inv * (residual_grad_out[s] - residual[s] * (inv * inv * stat))
        residual_grad_out[s] = grad
        leave(s, 2)
        send_spread(1, s, (mask[s][:, 0:1] * grad).astype(BF16))

    def gate_back(s, gated_grad):
        out_gain = gain_row[0:1, :]
        for h in range(heads):
            here = slice(h * value_dim, (h + 1) * value_dim)
            grad = gated_grad[:, here]
            mixer_h = mixer[s, h]
            gate_h = gate[s, :, here]
            scale = lax.rsqrt(jnp.sum(mixer_h * mixer_h, axis=1, keepdims=True) / value_dim + NORM_EPSILON)
            sig = sigmoid(gate_h)
            unit_rows = mixer_h * scale
            gate_grad_out[s, :, here] = (
                grad * unit_rows * out_gain * (sig * (1.0 + gate_h * (1.0 - sig)))
            ).astype(BF16)
            scaled_grad = grad * (gate_h * sig)
            output_gain_grad[0:1, :] += jnp.sum(scaled_grad * unit_rows, axis=0, keepdims=True)
            unit_grad = scaled_grad * out_gain
            stat = jnp.sum(unit_grad * mixer_h, axis=1, keepdims=True) / value_dim
            mixer_grad_h = scale * (unit_grad - mixer_h * (scale * scale * stat))
            mixer_grad[s, h] = mixer_grad_h
            entering = mm(split(mixer_grad_h), split(eff[s, h]), TN).astype(BF16)
            for i, piece in enumerate(units.pieces(entering)):
                shifts_low[(s * heads + h) * units.share + i] = piece

        for i in range(heads * units.share):
            unit = s * heads * units.share + i

            @pl.when(unit != units.me)
            def _(unit=unit):
                shift_copy(unit).start()

            @pl.when(unit == units.me)
            def _(unit=unit):
                shifts_in[unit] = shifts_low[unit]

    def mixer_rows(s):
        grad = take_spread(1, s)
        mixer_rows_grad[s] = grad
        gate_back(s, raw(grad, out_weight[...], NT))
        leave(s, 3, 4, 5)

    stages = (
        (10, mixer_rows),
        (9, functools.partial(pass_spread, 1)),
        (8, residual_back),
        (7, norm_back),
        (6, functools.partial(join_core, 1)),
        (11, block_rows),
        (10, functools.partial(join_core, 2)),
        (4, functools.partial(pass_spread, 0)),
        (3, norm_second),
        (2, rows_in),
        (1, functools.partial(join_core, 0)),
        (0, attention),
        (5, swiglu),
        (9, swiglu_out),
    )

    def step(t, carry):
        @pl.when(t == 5)
        def _():
            arrive(0)

        @pl.when(t == 10)
        def _():
            arrive(1)

        for offset, stage in stages:
            s = t - offset

            @pl.when((s >= 0) & (s < slots))
            def _(stage=stage, s=s):
                stage(s)

        def normed_rows():
            return jnp.concatenate(
                [spread[0, :, j].reshape(slots * length, shard) for j in range(head_parts)], axis=1
            )

        def cotangent_rows():
            return cotangent[...].reshape(-1, width)

        for late, left, right, target, index in (
            (5, act_all, cotangent_rows, down_part, 9),
            (6, up_grad_all, normed_rows, up_part, 10),
            (7, gate_grad_all, normed_rows, gate_part, 1),
        ):

            @pl.when(t == slots + late)
            def _(left=left, right=right, target=target, index=index):
                def store(start, size, block):
                    target[pl.ds(start, size), :] = block

                weight_rows(left, right(), store)
                if target.shape[0] > hidden:
                    target[hidden:, :] = jnp.zeros((target.shape[0] - hidden, width), BF16)
                leave(None, index)

        return carry

    lax.fori_loop(0, slots + 11, step, 0)

    def drain(s, carry):
        tools.drain(s)
        for kind in range(2):
            for away in range(1, lines):
                spread_line_copy(kind, s, away).wait_send()
            for away in range(lines):
                spread_core_copy(kind, s, away).wait_send()
        return carry

    lax.fori_loop(0, slots, drain, 0)

    def take_units(away, carry):
        unit = lax.rem(units.me + away, parts)
        units.at_owner(shifts_low.at[0], shifts_in, shift_send, shift_recv, unit).wait_recv()
        return carry

    lax.fori_loop(1, parts, take_units, 0)

    def drain_units(away, carry):
        shift_copy(lax.rem(units.me + away, parts)).wait_send()
        return carry

    lax.fori_loop(1, parts, drain_units, 0)


def padded_rows(count, parts):
    return count + -count % (32 * parts)


def middle_call(parts, head_parts, heads, *operands):
    gated, x_shard, gate_weight, mixer, eff = (operands[i] for i in (0, 1, 5, 9, 12))
    slots, length, shard = x_shard.shape
    width = shard * head_parts
    hidden = gate_weight.shape[0]
    lines = head_parts // 2
    value_dim, key_dim = mixer.shape[3], eff.shape[3]
    unit = (parts, value_dim * slots * heads // parts, key_dim)
    sds = jax.ShapeDtypeStruct
    dma = pltpu.SemaphoreType.DMA
    product = sds((padded_rows(hidden, parts), width), BF16)
    rows = sds((slots, length, shard), F32)
    outs = (
        sds((slots, length, shard), BF16), product, rows,
        sds((slots, length, width), BF16), sds(mixer.shape, F32),
        sds(gated.shape, BF16), sds((8, shard), F32), sds((8, value_dim), F32), sds(unit, BF16), product, product,
    )
    scratch = (
        [
            pltpu.VMEM(rows.shape, F32),
            pltpu.VMEM((slots, length, hidden), BF16),
            pltpu.VMEM((slots, length, hidden), BF16),
            pltpu.VMEM((slots, length, hidden), BF16),
            pltpu.VMEM((slots, length, LANES), F32),
            pltpu.VMEM((2, slots, head_parts, length, shard), BF16),
            pltpu.VMEM(unit, BF16), dma((parts - 1,)), dma((parts - 1,)),
            dma((2, slots, lines - 1)), dma((2, slots, lines - 1)),
            dma((2, slots, lines)), dma((2, slots, lines)),
        ]
        + head_scratch(3, 2, slots, head_parts, length, shard)
    )
    return staged_call(
        functools.partial(middle_kernel, slots, head_parts, parts, heads),
        operands, outs, scratch, 0, late=((5, 6, 7, 2), (9, 10, 12)), leaving=(0, 1, 2, 3, 4, 5, 9, 10),
        slots=slots,
    )


def ring_scratch(parts, shapes):
    dma = pltpu.SemaphoreType.DMA
    count = len(shapes)
    return [
        pltpu.VMEM((2, parts, rows // (2 * parts), wide), BF16) for rows, wide in shapes
    ] + [dma((count, 2)), dma((count, 2, parts - 1)), dma((count, 2)), dma((count, 2, parts - 1)), dma((count, 2))]


def ring_tools(parts, ins, outs, held, send, recv, spread_send, spread_recv, own):
    count = len(ins)
    index = lax.axis_index("seq")
    other = lax.axis_index("head")
    side = lax.rem(index, 2)
    level = index // 2
    levels = parts // 2
    position = jnp.where(side == 1, level, parts - 1 - level)
    up = jnp.where(side == 1, jnp.where(level == levels - 1, index - 1, index + 2),
                   jnp.where(level == 0, index + 1, index - 2))
    down = jnp.where(side == 1, jnp.where(level == 0, index - 1, index - 2),
                     jnp.where(level == levels - 1, index + 1, index + 2))
    targets = (up, down)
    def greet(barrier):
        for target in targets:
            pl.semaphore_signal(barrier, inc=1, device_id=(target, other), device_id_type=MESH)

    def rows_of(a, way, chunk):
        size = ins[a].shape[0] // (2 * parts)
        return pl.ds(pl.multiple_of((chunk * 2 + way) * size, size), size)

    def chunk_at(way, step):
        if way == 0:
            return lax.rem(position - step + 2 * parts, parts)
        return lax.rem(position + step + 2 * parts, parts)

    def sum_copy(a, way, step):
        return remote(
            held[a].at[way, step], held[a].at[way, step + 1], send.at[a, way], recv.at[a, way, step],
            (targets[way], other),
        )

    def spread_copy(a, way, step):
        block = rows_of(a, way, chunk_at(way, step - 1))
        return remote(
            outs[a].at[block, :], outs[a].at[block, :], spread_send.at[a, way], spread_recv.at[a, way, step],
            (targets[way], other),
        )

    def spread_first(a, way):
        block = rows_of(a, way, chunk_at(way, parts - 1))
        return remote(
            held[a].at[way, parts - 1], outs[a].at[block, :], spread_send.at[a, way],
            spread_recv.at[a, way, 0], (targets[way], other),
        )

    def own_copy(a, way):
        block = rows_of(a, way, chunk_at(way, parts - 1))
        return pltpu.make_async_copy(held[a].at[way, parts - 1], outs[a].at[block, :], own.at[a, way])

    def spread_arrival(a, way, step):
        block = rows_of(a, way, chunk_at(way, step))
        return remote(
            outs[a].at[block, :], outs[a].at[block, :], spread_send.at[a, way], spread_recv.at[a, way, step],
            (targets[way], other),
        )

    lanes = [(a, way) for a in range(count) for way in range(2)]
    last = parts - 2

    def add(step, a, way):
        sum_copy(a, way, step).wait_recv()
        mine = ins[a][rows_of(a, way, chunk_at(way, step + 1)), :].astype(F32)
        return (held[a][way, step + 1].astype(F32) + mine).astype(BF16)

    def begin():
        for a, way in lanes:
            held[a][way, 0] = ins[a][rows_of(a, way, chunk_at(way, 0)), :]
            sum_copy(a, way, 0).start()

    def one(step):
        for a, way in lanes:
            held[a][way, step + 1] = add(step, a, way)
            sum_copy(a, way, step).wait_send()
            sum_copy(a, way, step + 1).start()

    def turn():
        for a, way in lanes:
            held[a][way, parts - 1] = add(last, a, way)
            sum_copy(a, way, last).wait_send()
            spread_first(a, way).start()
            own_copy(a, way).start()

    def pass_first():
        for a, way in lanes:
            spread_arrival(a, way, 0).wait_recv()
            spread_first(a, way).wait_send()
            spread_copy(a, way, 1).start()

    def pass_on(step):
        for a, way in lanes:
            spread_arrival(a, way, step).wait_recv()
            spread_copy(a, way, step).wait_send()
            spread_copy(a, way, step + 1).start()

    def finish():
        for a, way in lanes:
            spread_arrival(a, way, last).wait_recv()
            spread_copy(a, way, last).wait_send()
            own_copy(a, way).wait()

    def tick(k):
        @pl.when(k < last)
        def _():
            one(k)

        @pl.when(k == last)
        def _():
            turn()

        @pl.when(k == last + 1)
        def _():
            pass_first()

        @pl.when(k > last + 1)
        def _():
            pass_on(k - last - 1)

    return types.SimpleNamespace(
        greet=greet, begin=begin, tick=tick, finish=finish, ticks=2 * parts - 3, up=up, down=down
    )


def backward_kernel(
    slots, heads, key_dim, value_dim, parts, head_parts, arrive, leave,
    mixer_grad, shifts_in, gated, mixer_rows_grad, normed, gate_grad,
    pre, rim, ab, abt, taps_ref, lanes, cols,
    queries, keys, value_rows, inverse_all, delta_rows, states, maps_in, gate_part,
    query_weight, key_weight, value_weight, gate_weight, ab_weight, x_shard, inv_first, residual_grad, input_gain,
    gain_part, mixed_part, up_part, down_part,
    input_grad_out, small_sum, gate_sum, out_sum, first_sum, unit_sum, value_sum, up_sum, down_sum,
    ab_grad_out, taps_grad_out, lane_grad_out, out_part, first_part, unit_own, value_own,
    ext, conv_grad, tail, rim_own, rim_in, leavings, leaving_send,
    small_own, small_in, gain_own, gain_in,
    back_send, back_recv, rim_send, rim_recv, small_send, small_recv, gain_send, gain_recv, *refs,
):
    length = pre.shape[1]
    taps = 4
    width = normed.shape[2]
    values = gated.shape[2]
    units = Units(parts, slots * heads)
    me = units.me
    tools = head_tools(head_parts, refs[27:], 1)
    place, head = me, units.other
    pre_grad_out = pre
    shard = x_shard.shape[2]
    channels = pre.shape[2]
    unit_wide = unit_own.shape[1]
    rings = (
        ring_tools(parts, (gate_part, up_part), (gate_sum, up_sum), refs[0:2], *refs[2:7]),
        ring_tools(
            parts, (down_part, out_part, first_part), (down_sum, out_sum, first_sum), refs[7:10], *refs[10:15]
        ),
        ring_tools(parts, (unit_own,), (unit_sum,), refs[15:16], *refs[16:21]),
        ring_tools(parts, (value_own,), (value_sum,), refs[21:22], *refs[22:27]),
    )
    barrier = pltpu.get_barrier_semaphore()
    units.greet(barrier)
    tools.greet(barrier)
    row, col = grid_masks(length)
    taps_grad_out[...] = jnp.zeros_like(taps_grad_out)
    lane_grad_out[...] = jnp.zeros_like(lane_grad_out)
    pl.semaphore_wait(barrier, parts - 1 + head_parts - 1)
    rings[0].begin()

    def back_copy(place):
        ahead = units.ahead(place)
        return remote(
            leaving_send.at[place], leavings.at[me], back_send.at[ahead], back_recv.at[ahead],
            (place, units.other),
        )

    def back_arrival(unit):
        behind = units.behind(unit)
        return remote(
            leaving_send.at[unit], leavings.at[unit], back_send.at[behind], back_recv.at[behind],
            (unit, units.other),
        )

    def rim_copy():
        return remote(
            rim_own, rim_in, rim_send.at[0], rim_recv.at[0], (lax.rem(me + parts - 1, parts), units.other)
        )

    def scan(hop, leaving):
        place = parts - 1 - hop
        low = leaving.astype(BF16)

        @pl.when(place != me)
        def _():
            leaving_send[place] = low
            back_copy(place).start()

        @pl.when(place == me)
        def _():
            leavings[place] = low

        return mm(split(leaving), maps_in[place], NT) + shifts_in[place].astype(F32)

    lax.fori_loop(0, parts, scan, jnp.zeros((value_dim // units.share, key_dim), F32))
    arrive(0)

    def store_out(start, size, block):
        out_part[pl.ds(start, size), :] = block

    def store_first(start, size, block):
        first_part[pl.ds(start, size), :] = block

    weight_rows(gated, mixer_rows_grad[...].reshape(-1, width), store_out)
    weight_rows(normed, gate_grad[...].reshape(-1, values), store_first)
    rings[1].begin()
    arrive(1)
    rings[0].tick(0)

    def delta_slot(s, carry):
        for i in range(heads * units.share):
            unit = s * heads * units.share + i

            @pl.when(unit != me)
            def _(unit=unit):
                back_arrival(unit).wait_recv()

        ext[0:RIM, :] = rim[s]
        ext[RIM : RIM + length, :] = pre[s].astype(F32)
        lane = lax.broadcasted_iota(jnp.int32, (length, LANES), 1)
        log_cols, strength_cols = gates_of(ab[s], lanes[0:1, :], lanes[1:2, :])
        log_rows, strength_rows = gates_of(abt[s], cols[0:8, 0:1], cols[8:16, 0:1])
        key_start = heads * key_dim
        value_start = 2 * heads * key_dim
        strict = row > col
        grads = jnp.zeros((length, LANES), F32)
        conv_grad[0:RIM, :] = jnp.zeros((RIM, conv_grad.shape[1]), F32)
        conv_grad[RIM + length : 2 * RIM + length, :] = jnp.zeros((RIM, conv_grad.shape[1]), F32)

        def activation(start, width):
            total = taps_ref[0:1, start : start + width] * ext[pl.ds(RIM - taps + 1, length), start : start + width]
            for tap in range(1, taps):
                total = total + (
                    taps_ref[tap : tap + 1, start : start + width]
                    * ext[pl.ds(RIM - taps + 1 + tap, length), start : start + width]
                )
            sig = sigmoid(total)
            return total * sig, sig * (1.0 + total * (1.0 - sig))

        def unit_back(grad, start, scale_by):
            act, slope = activation(start, key_dim)
            scale = lax.rsqrt(jnp.sum(act * act, axis=1, keepdims=True) + UNIT_EPSILON)
            inner = jnp.sum(act * grad, axis=1, keepdims=True)
            back = scale_by * scale * (grad - act * (scale * scale * inner))
            conv_grad[RIM : RIM + length, start : start + key_dim] = back * slope

        for h in range(heads):
            query, key, value = queries[s, h], keys[s, h], value_rows[s, h]
            query_f, key_f = query.astype(F32), key.astype(F32)
            strength = strength_cols[:, heads + h : heads + h + 1]
            cum_col, cum_row, end, decayed = decay_of(
                log_cols[:, h : h + 1], log_rows[h : h + 1, :], row, col
            )
            rise = jnp.exp(cum_col)
            end_weight = jnp.exp(end - cum_col)
            state = units.whole(states, s * heads + h)
            leaving = units.whole(leavings, s * heads + h)
            state_f, leaving_f = state.astype(F32), leaving.astype(F32)
            rows = split(delta_rows[s, h])
            out_grad = split(mixer_grad[s, h])
            products = mm(key, key, NT)
            scores = decayed * mm(query, key, NT)
            rows_grad = mm(split(scores), out_grad, TN) + end_weight * mm(key, leaving, NT)
            scores_grad = mm(out_grad, rows, NT)
            query_grad = rise * mm(out_grad, state)
            right_grad = mm(split(inverse_all[s, h]), split(rows_grad), TN)
            key_state = mm(key, state, NT)
            triangle_grad = -jnp.where(strict, mm(split(right_grad), rows, NT), 0.0)
            value_grad = strength * right_grad
            strength_grad = jnp.sum(right_grad * (value.astype(F32) - rise * key_state), axis=1, keepdims=True)
            read_grad = -rise * value_grad
            cum_grad = jnp.sum(read_grad * key_state, axis=1, keepdims=True)
            key_grad = mm(split(read_grad), state)
            decayed_grad = triangle_grad * decayed
            strength_grad = strength_grad + jnp.sum(decayed_grad * products, axis=1, keepdims=True)
            weighted = strength * decayed_grad
            both = weighted * products + scores_grad * scores
            products_grad = split(weighted)
            overlap_grad = split(scores_grad * decayed)
            cum_grad = cum_grad + jnp.sum(both, axis=1, keepdims=True) + jnp.sum(query_f * query_grad, axis=1, keepdims=True)
            query_grad = query_grad + mm(overlap_grad, key)
            key_grad = (
                key_grad + mm(overlap_grad, query, TN) + mm(products_grad, key) + mm(products_grad, key, TN)
            )
            moved = mm(rows, leaving)
            key_grad = key_grad + end_weight * moved
            end_part = jnp.sum(moved * key_f, axis=1, keepdims=True) * end_weight
            cum_grad = cum_grad - end_part
            last = jnp.sum(end_part, axis=0, keepdims=True) + jnp.exp(end) * jnp.sum(
                jnp.sum(leaving_f * state_f, axis=1, keepdims=True), axis=0, keepdims=True
            )
            turned = jnp.sum(jnp.where(row == col, cum_grad, 0.0), axis=0, keepdims=True)
            turned = turned - jnp.sum(both, axis=0, keepdims=True)
            log_grad = jnp.sum(jnp.where(row <= col, turned, 0.0), axis=1, keepdims=True) + last
            grads = jnp.where(lane == h, log_grad, grads)
            grads = jnp.where(lane == heads + h, strength_grad, grads)
            unit_back(query_grad, h * key_dim, key_dim ** (-0.5))
            unit_back(key_grad, key_start + h * key_dim, 1.0)
            if h == 0:
                rings[0].tick(s + 1)
            _, slope = activation(value_start + h * value_dim, value_dim)
            conv_grad[RIM : RIM + length, value_start + h * value_dim : value_start + (h + 1) * value_dim] = (
                value_grad * slope
            )

        softened = -lanes[0:1, :] * sigmoid(ab[s] + lanes[1:2, :])
        decay_part = grads * softened
        is_log = lane < heads
        ab_grad_out[s] = jnp.where(is_log, decay_part, grads * strength_cols * (1.0 - strength_cols))
        lane_grad_out[0:1, :] += jnp.sum(jnp.where(is_log, grads * log_cols, 0.0), axis=0, keepdims=True)
        lane_grad_out[1:2, :] += jnp.sum(jnp.where(is_log, decay_part, 0.0), axis=0, keepdims=True)
        main = conv_grad[RIM : RIM + length, :]
        pre_grad = jnp.zeros_like(main)
        rim_grad = jnp.zeros((RIM, conv_grad.shape[1]), F32)
        for tap in range(taps):
            weight = taps_ref[tap : tap + 1, :]
            taps_grad_out[tap : tap + 1, :] += jnp.sum(
                main * ext[pl.ds(RIM - taps + 1 + tap, length), :], axis=0, keepdims=True
            )
            pre_grad = pre_grad + weight * conv_grad[pl.ds(RIM + taps - 1 - tap, length), :]
            rim_grad = rim_grad + weight * conv_grad[pl.ds(taps - 1 - tap, RIM), :]
        pre_grad_out[s] = pre_grad.astype(BF16)
        tail[s] = pre_grad[length - 2 * RIM : length, :]
        rim_own[s] = rim_grad
        rings[1].tick(s)
        return carry

    lax.fori_loop(0, slots, delta_slot, 0)
    rim_copy().start()

    rings[0].tick(slots + 1)
    rings[1].tick(slots)
    rim_copy().wait_recv()
    inside = me < parts - 1
    for s in range(slots):
        late = jnp.where(inside, rim_in[s], 0.0)
        end = tail[s]
        shifted_in = jnp.concatenate([jnp.zeros_like(late), late], axis=0)
        pre_grad_out[s, length - 2 * RIM : length, :] = (end + shifted_in).astype(BF16)
    rim_copy().wait_send()

    def gain_copy(away):
        return remote(
            gain_own, gain_in.at[away - 1], gain_send.at[away - 1], gain_recv.at[away - 1],
            (place, lax.rem(head + away, head_parts)),
        )

    def small_copy(away):
        return remote(
            small_own, small_in.at[away - 1], small_send.at[away - 1], small_recv.at[away - 1],
            (lax.rem(place + away, parts), head),
        )

    def store_unit(start, size, block):
        unit_own[pl.ds(start, size), :] = block

    def store_value(start, size, block):
        value_own[pl.ds(start, size), :] = block

    weight_rows(normed, pre_grad_out[:, :, :unit_wide].reshape(-1, unit_wide), store_unit)
    rings[2].begin()
    weight_rows(normed, pre_grad_out[:, :, unit_wide:].reshape(-1, channels - unit_wide), store_value)
    rings[3].begin()

    def products(s, carry):
        low = ab_grad_out[s].astype(BF16)
        half = unit_wide // 2
        tools.send_part(
            0, s,
            raw(pre_grad_out[s, :, :half], query_weight[...], NT)
            + raw(pre_grad_out[s, :, half:unit_wide], key_weight[...], NT)
            + raw(pre_grad_out[s, :, unit_wide:], value_weight[...], NT)
            + raw(gate_grad[s], gate_weight[...], NT)
            + raw(low, ab_weight[...], NT),
        )
        rings[0].tick(s + slots + 2)
        rings[2].tick(s)
        rings[1].tick(s + slots + 1)
        rings[3].tick(s)
        return carry

    arrive(2)
    lax.fori_loop(0, slots, products, 0)
    arrive(3)

    def tick_all(first, second):
        rings[0].tick(first)
        rings[2].tick(second)
        rings[1].tick(first - 1)
        rings[3].tick(second)


    def first_join(s, carry):
        tools.join_core(0, s)
        return carry

    lax.fori_loop(0, slots, first_join, 0)
    tick_all(2 * slots + 2, slots)
    small_own[...] = jnp.zeros_like(small_own)
    gain_own[...] = gain_part[...]
    for away in range(1, head_parts):
        gain_copy(away).start()

    def second_join(s, carry):
        grad = tools.join_line(0, s)
        x = x_shard[s].astype(F32)
        inv = inv_first[s][:, 0:1]
        weighted = grad * input_gain[0:1, :]
        input_grad_out[s] = weighted
        tools.send_stat(0, s, jnp.sum(weighted * x, axis=1, keepdims=True))
        return carry + jnp.sum(grad * x * inv, axis=0, keepdims=True)

    gain_line = lax.fori_loop(0, slots, second_join, jnp.zeros((1, shard), F32))
    tick_all(2 * slots + 3, slots + 1)

    def input_rows(s, carry):
        stat = tools.join_stat(0, s) / width
        inv = inv_first[s][:, 0:1]
        input_grad_out[s] = residual_grad[s] + inv * (
            input_grad_out[s] - x_shard[s].astype(F32) * (inv * inv * stat)
        )
        return carry

    lax.fori_loop(0, slots, input_rows, 0)
    gain_total = gain_own[...]
    for away in range(1, head_parts):
        gain_copy(away).wait_recv()
        gain_total = gain_total + gain_in[away - 1]
    low = ab_grad_out[...].astype(BF16).reshape(-1, LANES)
    ab_lines = raw(low, normed[...].reshape(-1, width), TN)
    at = 0
    for lines in [taps_grad_out[t : t + 1, :] for t in range(taps)] + [
        ab_lines[t : t + 1, :] for t in range(2 * heads)
    ] + [gain_total[0:1, :], lane_grad_out[0:1, :], lane_grad_out[1:2, :], mixed_part[0:1, :], gain_line]:
        for j in range(lines.shape[1] // LANES):
            small_own[at : at + 1, :] = lines[:, j * LANES : (j + 1) * LANES]
            at += 1

    def small_start(away, carry):
        small_copy(away).start()
        return carry

    lax.fori_loop(1, parts, small_start, 0)

    ticks = rings[0].ticks
    shift = slots + 2

    def rest(k, carry):
        @pl.when(k + shift < ticks)
        def _():
            rings[0].tick(k + shift)

        @pl.when(k + shift - 1 < ticks)
        def _():
            rings[1].tick(k + shift - 1)

        @pl.when(k < ticks)
        def _():
            rings[2].tick(k)
            rings[3].tick(k)

        return carry

    lax.fori_loop(slots + 2, max(ticks, ticks - shift + 1), rest, 0)
    small_sum[...] = small_own[...]

    def small_join(away, carry):
        small_copy(away).wait_recv()
        small_sum[...] += small_in[away - 1]
        small_copy(away).wait_send()
        return carry

    lax.fori_loop(1, parts, small_join, 0)
    for away in range(1, head_parts):
        gain_copy(away).wait_send()

    def drain(s, carry):
        tools.drain(s)
        return carry

    lax.fori_loop(0, slots, drain, 0)
    def drain_units(away, carry):
        back_copy(lax.rem(me + away, parts)).wait_send()
        return carry

    lax.fori_loop(1, parts, drain_units, 0)
    for ring in rings:
        ring.finish()


def backward_call(parts, head_parts, heads, taps, *operands):
    gated, normed, gate_grad, pre, ab, keys, value_rows, states, gate_part, x_shard, gain_part, down_part = (
        operands[i] for i in (2, 4, 5, 6, 8, 14, 15, 18, 20, 26, 30, 33)
    )
    slots, length, channels = pre.shape
    value_dim, key_dim = value_rows.shape[3], keys.shape[3]
    width, shard = normed.shape[2], x_shard.shape[2]
    lines = (taps * channels + 2 * heads * width + gain_part.shape[1] + 2 * shard) // LANES + 2
    lines += -lines % 8
    sds = jax.ShapeDtypeStruct
    dma = pltpu.SemaphoreType.DMA
    out_shape = (padded_rows(gated.shape[2], parts), width)
    first_shape = (width, gate_grad.shape[2])
    unit_shape = (width, 2 * heads * key_dim)
    value_shape = (width, heads * value_dim)
    sums = (gate_part.shape, out_shape, first_shape, unit_shape, value_shape, gate_part.shape, down_part.shape)
    outs = (sds(x_shard.shape, F32), sds((lines, LANES), F32)) + tuple(sds(a, BF16) for a in sums)
    unit = pltpu.VMEM(states.shape, BF16)
    edge = pltpu.VMEM((slots, RIM, channels), F32)
    scratch = (
        [
            pltpu.VMEM(ab.shape, F32), pltpu.VMEM((8, channels), F32),
            pltpu.VMEM((8, LANES), F32),
        ]
        + [pltpu.VMEM(a, BF16) for a in sums[1:5]]
        + [
            pltpu.VMEM((length + RIM, channels), F32), pltpu.VMEM((length + 2 * RIM, channels), F32),
            pltpu.VMEM((slots, 2 * RIM, channels), F32), edge, edge, unit, unit,
            pltpu.VMEM((lines, LANES), F32), pltpu.VMEM((parts - 1, lines, LANES), F32),
            pltpu.VMEM(gain_part.shape, F32), pltpu.VMEM((head_parts - 1,) + gain_part.shape, F32),
            dma((parts - 1,)), dma((parts - 1,)), dma((1,)), dma((1,)),
            dma((parts - 1,)), dma((parts - 1,)), dma((head_parts - 1,)), dma((head_parts - 1,)),
        ]
        + ring_scratch(parts, [gate_part.shape, gate_part.shape])
        + ring_scratch(parts, [down_part.shape, out_shape, first_shape])
        + ring_scratch(parts, [unit_shape])
        + ring_scratch(parts, [value_shape])
        + head_scratch(1, 1, slots, head_parts, length, shard)
    )
    return staged_call(
        functools.partial(backward_kernel, slots, heads, key_dim, value_dim, parts, head_parts),
        operands, outs, scratch, 3,
        late=(
            (2, 3, 4, 5, 33), (0, 6, 7, 8, 9, 13, 14, 15, 16, 17, 18), (21, 22, 23, 24, 25),
            (26, 27, 28, 29, 30, 31),
        ),
        kept=(2, 3, 4, 5, 6, 7, 8), flops=5 * 10**10,
    )


def per_device(
    hidden_in, lengths, input_gain, query_weight, key_weight, value_weight, alpha_weight, beta_weight,
    decay_log, decay_bias, query_kernel, key_kernel, value_kernel, gate_weight, output_gain,
    output_weight, mixed_gain, swiglu_gate, swiglu_up, swiglu_down, cotangent,
):
    slots, segment, width = hidden_in.shape
    heads = decay_log.shape[0]
    key_dim = query_kernel.shape[1] // heads
    value_dim = value_kernel.shape[1] // heads
    taps = query_kernel.shape[0]
    split_key = heads * key_dim
    channels = 2 * split_key + heads * value_dim
    head_parts = lax.axis_size("head")
    seq_parts = lax.axis_size("seq")
    shard = width // head_parts
    head_start = lax.axis_index("head") * shard

    position = lax.axis_index("seq") * segment + jnp.arange(segment)
    mask = (position[None, :] < lengths[:, None]).astype(F32)[:, :, None]
    lane_mask = jnp.broadcast_to(mask, (slots, segment, LANES))
    ab_weight = jnp.concatenate(
        [alpha_weight, beta_weight, jnp.zeros((width, LANES - 2 * heads), BF16)], axis=1
    )
    kernel = jnp.concatenate([query_kernel, key_kernel, value_kernel], axis=1).astype(F32)
    kernel = jnp.pad(kernel, ((0, 8 - taps), (0, 0)))
    rate = jnp.exp(decay_log)
    pad_heads = lambda v: jnp.pad(v, (0, LANES - heads))
    lane_gates = jnp.pad(jnp.stack([pad_heads(rate), pad_heads(decay_bias)]), ((0, 6), (0, 0)))
    pad_rows = lambda v: jnp.broadcast_to(jnp.pad(v, (0, 8 - heads))[:, None], (8, LANES))
    col_gates = jnp.concatenate([pad_rows(rate), pad_rows(decay_bias)], axis=0)
    gain_row = jnp.broadcast_to(output_gain[None, :], (8, value_dim))

    (
        query, key, value, inverse, eff, delta_rows, mixer, gated, normed_first, pre_all, gate_pre, x_low,
        inv_first, rim_pre, ab_pre, ab_rows, states, maps_in,
    ) = forward_call(
        seq_parts, head_parts, heads, hidden_in, jnp.broadcast_to(input_gain[None, :], (8, width)),
        query_weight, key_weight, value_weight, gate_weight, ab_weight, kernel, lane_gates, col_gates, gain_row,
    )
    (
        block_out, gate_part, residual_grad, mixer_rows_grad, mixer_grad, gate_grad, mixed_part, gain_part,
        shifts_in, down_part, up_part,
    ) = middle_call(
        seq_parts, head_parts, heads, gated, x_low, cotangent, lane_mask, output_weight, swiglu_gate.T,
        swiglu_up.T, swiglu_down, jnp.broadcast_to(mixed_gain[None, :], (8, shard)), mixer, gate_pre, gain_row, eff,
    )
    gain_shard = lax.dynamic_slice_in_dim(input_gain, head_start, shard, 0)
    (
        input_grad, small_sum, gate_sum, out_sum, gate_first_sum, unit_sum, value_sum, up_sum, down_sum
    ) = backward_call(
        seq_parts, head_parts, heads, taps, mixer_grad, shifts_in, gated, mixer_rows_grad, normed_first, gate_grad,
        pre_all, rim_pre, ab_pre, ab_rows, kernel, lane_gates, col_gates, query, key, value, inverse, delta_rows,
        states, maps_in, gate_part, query_weight, key_weight, value_weight, gate_weight, ab_weight, x_low,
        inv_first, residual_grad, jnp.broadcast_to(gain_shard[None, :], (8, shard)), gain_part, mixed_part,
        up_part, down_part,
    )
    hidden = swiglu_gate.shape[1]
    flat_small = small_sum.reshape(-1)
    pieces, at = [], 0
    for size in (taps * channels, 2 * heads * width, value_dim, LANES, LANES, shard, shard):
        pieces.append(flat_small[at : at + size])
        at += size
    taps_sum = pieces[0].reshape(taps, channels)
    ab_sum = pieces[1].reshape(2 * heads, width).T
    value_share = value_dim // head_parts
    output_gain_grad = lax.dynamic_slice_in_dim(
        pieces[2], lax.axis_index("head") * value_share, value_share, 0
    )
    return (
        block_out,
        input_grad,
        pieces[6],
        unit_sum[:, :split_key].astype(F32),
        unit_sum[:, split_key:].astype(F32),
        value_sum.astype(F32),
        ab_sum[:, :heads],
        ab_sum[:, heads:],
        pieces[3][:heads],
        pieces[4][:heads],
        taps_sum[:, :split_key],
        taps_sum[:, split_key : 2 * split_key],
        taps_sum[:, 2 * split_key :],
        gate_first_sum.astype(F32),
        output_gain_grad,
        out_sum[: heads * value_dim].astype(F32),
        pieces[5],
        gate_sum[:hidden].astype(F32).T,
        up_sum[:hidden].astype(F32).T,
        down_sum[:hidden].astype(F32),
    )


def solution(mesh):
    seq, cols, lines = P(None, "seq", None), P(None, "head"), P("head", None)
    one = P("head")
    placed = (
        seq, P(), P(), cols, cols, cols, cols, cols, one, one, cols, cols, cols, cols, P(), lines, one,
        cols, cols, lines, seq,
    )
    both = P(None, "seq", "head")
    return jax.shard_map(
        per_device,
        mesh=mesh,
        in_specs=placed,
        out_specs=(
            both, both, one, cols, cols, cols, cols, cols, one, one, cols, cols, cols, cols, one, lines,
            one, cols, cols, lines,
        ),
        check_vma=False,
    )
```

```python
import functools
import types

import jax
import jax.numpy as jnp
from jax import lax
from jax.experimental import pallas as pl
from jax.experimental.pallas import tpu as pltpu
from jax.sharding import PartitionSpec as P

NORM_EPSILON = 1e-05
UNIT_EPSILON = 1e-06
RIM = 8
LANES = 128
F32 = jnp.float32
BF16 = jnp.bfloat16
VMEM_LIMIT = 58 * 1024 * 1024

NN = (((1,), (0,)), ((), ()))
NT = (((1,), (1,)), ((), ()))
TN = (((0,), (0,)), ((), ()))


def split(x):
    high = x.astype(BF16)
    return high, (x - high.astype(F32)).astype(BF16)


def raw(a, b, dims):
    return lax.dot_general(a, b, dims, preferred_element_type=F32)


def mm(a, b, dims=NN):
    a_high, a_low = a if isinstance(a, tuple) else (a, None)
    b_high, b_low = b if isinstance(b, tuple) else (b, None)
    total = raw(a_high, b_high, dims)
    if a_low is not None:
        total = total + raw(a_low, b_high, dims)
    if b_low is not None:
        total = total + raw(a_high, b_low, dims)
    return total


def sigmoid(x):
    return 1.0 / (1.0 + jnp.exp(-x))


def softplus(x):
    return jnp.maximum(x, 0.0) + jnp.log1p(jnp.exp(-jnp.abs(x)))


def grid_masks(size):
    row = lax.broadcasted_iota(jnp.int32, (size, size), 0)
    col = lax.broadcasted_iota(jnp.int32, (size, size), 1)
    return row, col


def rough_inverses(blocks):
    size = blocks[0].shape[0]
    row, col = grid_masks(size)
    apart = row ^ col
    base = 8
    starts = [jnp.where(apart < base, block, 0.0) for block in blocks]
    ones = [start.astype(BF16) for start in starts]
    squares = [raw(one, one, NN) for one in ones]
    lows = [square.astype(BF16) for square in squares]
    fourths = [raw(low, low, NN).astype(BF16) for low in lows]
    cubes = [raw(one, low, NN) for one, low in zip(ones, lows)]
    eye = jnp.where(row == col, 1.0, 0.0)
    found = [eye - start + square - cube for start, square, cube in zip(starts, squares, cubes)]
    found = [one + raw(one.astype(BF16), fourth, NN) for one, fourth in zip(found, fourths)]
    while base < size:
        ring = (apart >= base) & (apart < 2 * base)
        offs = [jnp.where(ring, block, 0.0).astype(BF16) for block in blocks]
        lows = [one.astype(BF16) for one in found]
        offs = [raw(low, off, NN).astype(BF16) for low, off in zip(lows, offs)]
        found = [one - raw(off, low, NN) for one, off, low in zip(found, offs, lows)]
        base *= 2
    return found


def unit_inverses(lowers, row, col):
    size = lowers[0].shape[0]
    half = size // 2
    count = len(lowers)
    found = rough_inverses([low[:half, :half] for low in lowers] + [low[half:, half:] for low in lowers])
    corners = [
        raw(second.astype(BF16), low[half:, :half].astype(BF16), NN).astype(BF16)
        for second, low in zip(found[count:], lowers)
    ]
    corners = [-raw(corner, first.astype(BF16), NN) for corner, first in zip(corners, found[:count])]
    zero = jnp.zeros((half, half), F32)
    roughs = [
        jnp.concatenate(
            [jnp.concatenate([first, zero], axis=1), jnp.concatenate([corner, second], axis=1)], axis=0
        )
        for first, corner, second in zip(found[:count], corners, found[count:])
    ]
    parts = [split(rough) for rough in roughs]
    eye = jnp.where(row == col, 1.0, 0.0)
    lefts = [
        (eye - rough - mm(split(low), part)).astype(BF16) for rough, low, part in zip(roughs, lowers, parts)
    ]
    return [rough + raw(part[0], left, NN) for rough, part, left in zip(roughs, parts, lefts)]


def gates_of(ab, rate, bias):
    return -rate * softplus(ab + bias), sigmoid(ab)


def decay_of(log_col, log_row, row, col):
    seen = row >= col
    cum_col = jnp.sum(jnp.where(seen, log_row, 0.0), axis=1, keepdims=True)
    cum_row = jnp.sum(jnp.where(row <= col, log_col, 0.0), axis=0, keepdims=True)
    end = jnp.sum(log_row, axis=1, keepdims=True)
    decayed = jnp.where(seen, jnp.exp(jnp.where(seen, cum_col - cum_row, 0.0)), 0.0)
    return cum_col, cum_row, end, decayed


def convolve(ext, taps_ref, length):
    taps = 4
    total = taps_ref[0:1, :] * ext[pl.ds(RIM - taps + 1, length), :]
    for tap in range(1, taps):
        total = total + taps_ref[tap : tap + 1, :] * ext[pl.ds(RIM - taps + 1 + tap, length), :]
    return total


MESH = pl.DeviceIdType.MESH


def remote(src, dst, send_sem, recv_sem, device):
    return pltpu.make_async_remote_copy(
        src_ref=src, dst_ref=dst, send_sem=send_sem, recv_sem=recv_sem, device_id=device, device_id_type=MESH
    )


def turn_to_row(column, row, col):
    return jnp.sum(jnp.where(row == col, column, 0.0), axis=0, keepdims=True)


def turn_to_column(line, row, col):
    return jnp.sum(jnp.where(row == col, line, 0.0), axis=1, keepdims=True)


def staged_call(kernel, operands, outs, scratch, collective_id, late=(), leaving=(), kept=(), slots=0, flops=10**10):
    dma = pltpu.SemaphoreType.DMA
    order = [i for group in late for i in group]
    vmem, free = pl.BlockSpec(memory_space=pltpu.VMEM), pl.BlockSpec(memory_space=pl.ANY)
    count, total = len(operands), len(operands) + len(outs)
    stages = [pltpu.VMEM(operands[i].shape, operands[i].dtype) for i in order]
    stages += [pltpu.VMEM(outs[i].shape, outs[i].dtype) for i in leaving]
    sems = [dma((max(1, len(order)),)), dma((max(1, len(leaving)), max(1, slots)))]

    def body(*refs):
        ins, results, rest = list(refs[:count]), list(refs[count:total]), refs[total:]
        held, (in_sem, out_sem), rest = rest[: len(stages)], rest[len(stages) : len(stages) + 2], rest[len(stages) + 2 :]
        copies = {}
        for j, i in enumerate(order):
            copies[i] = pltpu.make_async_copy(ins[i], held[j], in_sem.at[j])
            copies[i].start()
            ins[i] = held[j]
        targets = {}
        for j, i in enumerate(leaving):
            targets[i] = (results[i], held[len(order) + j], j)
            results[i] = held[len(order) + j]
        left = {}

        def arrive(group):
            for i in late[group]:
                copies[i].wait()

        def out_copy(i, slot):
            target, source, j = targets[i]
            if slot is None:
                return pltpu.make_async_copy(source, target, out_sem.at[j, 0])
            return pltpu.make_async_copy(source.at[slot], target.at[slot], out_sem.at[j, slot])

        def leave(slot, *indices):
            for i in indices:
                left[i] = slot is not None
                out_copy(i, slot).start()

        kernel(arrive, leave, *ins, *results, *rest)
        for i in leaving:
            for slot in range(slots) if left[i] else (None,):
                out_copy(i, slot).wait()

    late_set = set(order)
    return pl.pallas_call(
        body,
        in_specs=[free if i in late_set else vmem for i in range(count)],
        out_specs=[free if i in leaving or i in kept else vmem for i in range(len(outs))],
        out_shape=tuple(outs),
        scratch_shapes=stages + sems + list(scratch),
        compiler_params=pltpu.CompilerParams(
            collective_id=collective_id, has_side_effects=True, vmem_limit_bytes=VMEM_LIMIT
        ),
        cost_estimate=pl.CostEstimate(flops=flops, bytes_accessed=60 * 10**6, transcendentals=0),
    )(*operands)


class Units:
    def __init__(self, count, pairs):
        self.count, self.pairs, self.share = count, pairs, count // pairs
        self.me, self.other = lax.axis_index("seq"), lax.axis_index("head")

    def ahead(self, place):
        return lax.rem(place - self.me + self.count, self.count) - 1

    def behind(self, place):
        return lax.rem(self.me - place + self.count, self.count) - 1

    def to_owner(self, src, dst, send, recv, unit):
        return remote(src, dst.at[self.me], send.at[self.ahead(unit)], recv.at[self.ahead(unit)], (unit, self.other))

    def at_owner(self, src, dst, send, recv, place):
        return remote(src, dst.at[place], send.at[self.behind(place)], recv.at[self.behind(place)], (place, self.other))

    def pieces(self, value):
        size = value.shape[0] // self.share
        return [value[i * size : (i + 1) * size] for i in range(self.share)]

    def whole(self, ref, pair):
        return jnp.concatenate([ref[pair * self.share + i] for i in range(self.share)], axis=0)

    def greet(self, barrier):
        def one(away, carry):
            pl.semaphore_signal(
                barrier, inc=1, device_id=(lax.rem(self.me + away, self.count), self.other), device_id_type=MESH
            )
            return carry

        lax.fori_loop(1, self.count, one, 0)


def forward_kernel(
    slots, heads, key_dim, value_dim, parts, arrive, leave,
    hidden, input_gain, query_weight, key_weight, value_weight, gate_weight, ab_weight,
    query_kernel, key_kernel, value_kernel, decay_log, decay_bias, gain,
    query_out, key_out, value_out, inverse_out, eff_out, rows_out, mixer_out, gated_out,
    normed, pre, gate, x_out, inv_out, rim, ab, abt, states, maps_in, taps_ref, lanes, cols,
    ext, rim_rows, delta, mix, maps_low, shifts_low, shifts_in, state_send, edge_send, edge_recv,
    map_send, map_recv, shift_send, shift_recv, back_send, back_recv,
):
    length = pre.shape[1]
    units = Units(parts, slots * heads)
    me = units.me
    barrier = pltpu.get_barrier_semaphore()
    units.greet(barrier)
    row, col = grid_masks(length)
    key_start = heads * key_dim
    value_start = 2 * heads * key_dim
    width = hidden.shape[2]
    shard = x_out.shape[2]
    edge = rim_rows.shape[1]
    shard_start = pl.multiple_of(units.other * shard, shard)
    taps = query_kernel.shape[0]
    taps_ref[...] = jnp.zeros_like(taps_ref)
    taps_ref[0:taps, 0:key_start] = query_kernel[...].astype(F32)
    taps_ref[0:taps, key_start:value_start] = key_kernel[...].astype(F32)
    taps_ref[0:taps, value_start:] = value_kernel[...].astype(F32)
    lanes[...] = jnp.zeros_like(lanes)
    lane = lax.broadcasted_iota(jnp.int32, (1, LANES), 1)
    line = lax.broadcasted_iota(jnp.int32, (8, LANES), 0)
    for first, values in ((0, jnp.exp(decay_log[...])), (1, decay_bias[...])):
        by_lane = jnp.zeros((1, LANES), F32)
        by_line = jnp.zeros((8, LANES), F32)
        for h in range(heads):
            by_lane = jnp.where(lane == h, values[0:1, h : h + 1], by_lane)
            by_line = jnp.where(line == h, values[0:1, h : h + 1], by_line)
        lanes[first : first + 1, :] = by_lane
        cols[8 * first : 8 * first + 8, :] = by_line

    def edge_copy():
        return remote(
            hidden.at[:, length - edge : length, :], rim_rows, edge_send.at[0], edge_recv.at[0],
            (lax.rem(me + 1, parts), units.other),
        )

    def norm_rows(x):
        inv = lax.rsqrt(jnp.sum(x * x, axis=1, keepdims=True) / width + NORM_EPSILON)
        return inv, (x * inv * input_gain[0:1, :]).astype(BF16)

    def project(s, carry):
        inv, low = norm_rows(hidden[s].astype(F32))
        normed[s] = low
        x_out[s] = hidden[s, :, pl.ds(shard_start, shard)]
        inv_out[s] = jnp.broadcast_to(inv, (length, LANES))
        pre[s, :, :key_start] = raw(low, query_weight[...], NN).astype(BF16)
        pre[s, :, key_start:value_start] = raw(low, key_weight[...], NN).astype(BF16)
        pre[s, :, value_start:] = raw(low, value_weight[...], NN).astype(BF16)
        gates = raw(low, ab_weight[...], NT)
        ab[s] = gates
        abt[s] = jnp.transpose(gates)[0:8, :]
        leave(s, 8, 9, 11, 12)

        @pl.when(s == 0)
        def _():
            pl.semaphore_wait(barrier, parts - 1)
            edge_copy().start()

        return carry

    lax.fori_loop(0, slots, project, 0)
    edge_copy().wait_recv()
    _, edge_low = norm_rows(rim_rows[...].reshape(slots * edge, width).astype(F32))
    edge_pre = jnp.concatenate(
        [raw(edge_low, weight[...], NN) for weight in (query_weight, key_weight, value_weight)], axis=1
    ).astype(BF16).astype(F32)
    for s in range(slots):
        rim[s] = jnp.where(me > 0, edge_pre[(s + 1) * edge - RIM : (s + 1) * edge, :], 0.0)

    def map_copy(unit):
        return units.to_owner(maps_low.at[unit // units.share], maps_in, map_send, map_recv, unit)

    def shift_copy(unit):
        return units.to_owner(shifts_low.at[unit], shifts_in, shift_send, shift_recv, unit)

    def back_copy(place):
        ahead = units.ahead(place)
        return remote(
            state_send.at[place], states.at[me], back_send.at[ahead], back_recv.at[ahead], (place, units.other)
        )

    def back_arrival(unit):
        behind = units.behind(unit)
        return remote(
            state_send.at[unit], states.at[unit], back_send.at[behind], back_recv.at[behind], (unit, units.other)
        )

    together = 2 if slots % 2 == 0 else 1

    def group_terms(group, carry):
        pairs = []
        for i in range(together):
            s = group * together + i
            ext[i, 0:RIM, :] = rim[s]
            ext[i, RIM : RIM + length, :] = pre[s].astype(F32)
            conv = convolve(ext.at[i], taps_ref, length)
            active = conv * sigmoid(conv)
            log_cols, strength_cols = gates_of(ab[s], lanes[0:1, :], lanes[1:2, :])
            log_rows, strength_rows = gates_of(abt[s], cols[0:8, 0:1], cols[8:16, 0:1])
            for h in range(heads):
                query_act = active[:, h * key_dim : (h + 1) * key_dim]
                key_act = active[:, key_start + h * key_dim : key_start + (h + 1) * key_dim]
                value_act = active[:, value_start + h * value_dim : value_start + (h + 1) * value_dim]
                query_scale = lax.rsqrt(jnp.sum(query_act * query_act, axis=1, keepdims=True) + UNIT_EPSILON)
                key_scale = lax.rsqrt(jnp.sum(key_act * key_act, axis=1, keepdims=True) + UNIT_EPSILON)
                query = (query_act * query_scale * key_dim ** (-0.5)).astype(BF16)
                key = (key_act * key_scale).astype(BF16)
                value = value_act.astype(BF16)
                query_out[s, h] = query
                key_out[s, h] = key
                value_out[s, h] = value
                cum_col, cum_row, end, decayed = decay_of(
                    log_cols[:, h : h + 1], log_rows[h : h + 1, :], row, col
                )
                pairs.append(
                    types.SimpleNamespace(
                        s=s, h=h, query=query, key=key, value=value, cum_col=cum_col, cum_row=cum_row, end=end,
                        decayed=decayed, strength=strength_cols[:, heads + h : heads + h + 1],
                        strength_row=strength_rows[heads + h : heads + h + 1, :],
                    )
                )
        lowers = [
            jnp.where(row > col, pair.strength * pair.decayed * mm(pair.key, pair.key, NT), 0.0) for pair in pairs
        ]
        for pair, inverse in zip(pairs, unit_inverses(lowers, row, col)):
            inverse_out[pair.s, pair.h] = inverse
            pair.scaled = inverse * pair.strength_row
        for pair in pairs:
            pair.delta = mm(split(pair.scaled), pair.value)
            pair.mix = mm(split(pair.scaled * jnp.exp(pair.cum_row)), pair.key)
            delta[pair.s, pair.h] = pair.delta
            mix[pair.s, pair.h] = pair.mix
        small_row, small_col = grid_masks(key_dim)
        for pair in pairs:
            end_weight = jnp.exp(pair.end - pair.cum_col)
            moved = jnp.where(small_row == small_col, jnp.exp(pair.end), 0.0)
            place = pair.s * heads + pair.h
            maps_low[place] = (moved - mm(split(pair.mix * end_weight), pair.key, TN)).astype(BF16)
            for i, piece in enumerate(units.pieces(mm(split(pair.delta * end_weight), pair.key, TN).astype(BF16))):
                shifts_low[place * units.share + i] = piece
        for i in range(together):
            leave(group * together + i, 0, 1, 2, 3)
        for i in range(together * heads * units.share):
            unit = group * together * heads * units.share + i

            @pl.when(unit != me)
            def _(unit=unit):
                map_copy(unit).start()
                shift_copy(unit).start()

            @pl.when(unit == me)
            def _(unit=unit):
                maps_in[unit] = maps_low[unit // units.share]
                shifts_in[unit] = shifts_low[unit]

        return carry

    lax.fori_loop(0, slots // together, group_terms, 0)

    def within(s):
        gate[s] = raw(normed[s], gate_weight[...], NN)
        log_cols, _ = gates_of(ab[s], lanes[0:1, :], lanes[1:2, :])
        log_rows, _ = gates_of(abt[s], cols[0:8, 0:1], cols[8:16, 0:1])
        for h in range(heads):
            query = query_out[s, h]
            cum_col, _, _, decayed = decay_of(log_cols[:, h : h + 1], log_rows[h : h + 1, :], row, col)
            scores = split(decayed * mm(query, key_out[s, h], NT))
            eff_out[s, h] = jnp.exp(cum_col) * query.astype(F32) - mm(scores, split(mix[s, h]))
            mixer_out[s, h] = mm(scores, split(delta[s, h]))
        leave(s, 4, 10)

    def within_group(group, carry):
        for i in range(together):
            within(group * together + i)
        return carry

    early = slots // together // 2
    lax.fori_loop(0, early, within_group, 0)

    def scan(place, state):
        low = state.astype(BF16)

        @pl.when(place != me)
        def _():
            state_send[place] = low
            back_copy(place).start()
            units.at_owner(maps_low.at[0], maps_in, map_send, map_recv, place).wait_recv()
            units.at_owner(shifts_low.at[0], shifts_in, shift_send, shift_recv, place).wait_recv()

        @pl.when(place == me)
        def _():
            states[place] = low

        return mm(split(state), maps_in[place]) + shifts_in[place].astype(F32)

    lax.fori_loop(0, parts, scan, jnp.zeros((value_dim // units.share, key_dim), F32))

    lax.fori_loop(early, slots // together, within_group, 0)

    def emit(s, carry):
        for i in range(heads * units.share):
            unit = s * heads * units.share + i

            @pl.when(unit != me)
            def _(unit=unit):
                back_arrival(unit).wait_recv()

        for h in range(heads):
            state = units.whole(states, s * heads + h)
            rows_out[s, h] = delta[s, h] - mm(split(mix[s, h]), state, NT)
            mixer = mixer_out[s, h] + mm(split(eff_out[s, h]), state, NT)
            mixer_out[s, h] = mixer
            scale = lax.rsqrt(jnp.sum(mixer * mixer, axis=1, keepdims=True) / value_dim + NORM_EPSILON)
            here = slice(h * value_dim, (h + 1) * value_dim)
            gate_h = gate[s, :, here]
            gated_out[s, :, here] = (mixer * scale * gain[0:1, :] * (gate_h * sigmoid(gate_h))).astype(BF16)
        leave(s, 5, 6, 7)
        return carry

    lax.fori_loop(0, slots, emit, 0)

    def drain(away, carry):
        unit = lax.rem(me + away, parts)
        map_copy(unit).wait_send()
        shift_copy(unit).wait_send()
        back_copy(unit).wait_send()
        return carry

    lax.fori_loop(1, parts, drain, 0)
    edge_copy().wait_send()


def forward_call(parts, head_parts, heads, *operands):
    hidden, query_weight, value_weight, gate_weight = operands[0], operands[2], operands[4], operands[5]
    slots, length, width = hidden.shape
    key_dim, value_dim = query_weight.shape[1] // heads, value_weight.shape[1] // heads
    channels = heads * (2 * key_dim + value_dim)
    share = parts // (slots * heads)
    sds = jax.ShapeDtypeStruct
    dma = pltpu.SemaphoreType.DMA
    per = lambda kind, *tail: sds((slots, heads) + tail, kind)
    each = lambda kind, *tail: sds((slots,) + tail, kind)
    unit = (parts, value_dim // share, key_dim)
    outs = (
        per(BF16, length, key_dim), per(BF16, length, key_dim), per(BF16, length, value_dim),
        per(F32, length, length), per(F32, length, key_dim), per(F32, length, value_dim),
        per(F32, length, value_dim), each(BF16, length, heads * value_dim),
        each(BF16, length, width), each(BF16, length, channels), each(F32, length, heads * value_dim),
        each(BF16, length, width // head_parts), each(F32, length, LANES), each(F32, RIM, channels),
        each(F32, length, LANES), each(F32, 8, length),
        sds(unit, BF16), sds((parts, key_dim, key_dim), BF16), sds((8, channels), F32), sds((8, LANES), F32),
        sds((16, LANES), F32),
    )
    scratch = [
        pltpu.VMEM((2, length + RIM, channels), F32),
        pltpu.VMEM((slots, 2 * RIM, width), BF16),
        pltpu.VMEM((slots, heads, length, value_dim), F32),
        pltpu.VMEM((slots, heads, length, key_dim), F32),
        pltpu.VMEM((slots * heads, key_dim, key_dim), BF16),
        pltpu.VMEM(unit, BF16), pltpu.VMEM(unit, BF16), pltpu.VMEM(unit, BF16), dma((1,)), dma((1,)),
    ] + [dma((parts - 1,))] * 6
    return staged_call(
        functools.partial(forward_kernel, slots, heads, key_dim, value_dim, parts),
        operands, outs, scratch, 2, leaving=tuple(range(13)), slots=slots,
    )


def head_scratch(kinds, stats, slots, head_parts, length, shard):
    lines = head_parts // 2
    dma = pltpu.SemaphoreType.DMA
    return [
        pltpu.VMEM((head_parts, length, shard), F32),
        pltpu.VMEM((min(kinds, 2), slots, lines, length, shard), F32),
        pltpu.VMEM((kinds, slots, lines, length, shard), BF16),
        pltpu.VMEM((kinds, slots, lines, length, shard), BF16),
        pltpu.VMEM((min(kinds, 2), slots, lines - 1, length, shard), BF16),
        pltpu.VMEM((min(kinds, 2), slots, lines - 1, length, shard), BF16),
        pltpu.VMEM((stats, slots, 8, length), F32),
        pltpu.VMEM((stats, slots, head_parts - 1, 8, length), F32),
        dma((kinds, slots, lines)), dma((kinds, slots, lines)),
        dma((kinds, slots, lines - 1)), dma((kinds, slots, lines - 1)),
        dma((stats, slots, head_parts - 1)), dma((stats, slots, head_parts - 1)),
    ]


def head_tools(head_parts, refs, stats):
    whole_part, part, low, from_core, to_line, from_line, stat_own, stat_in = refs[:8]
    core_send, core_recv, line_send, line_recv, stat_send, stat_recv = refs[8:]
    me = lax.axis_index("head")
    place = lax.axis_index("seq")
    lines = head_parts // 2
    core = lax.rem(me, 2)
    line = me // 2
    sibling = 2 * line + (1 - core)
    length, shard = whole_part.shape[1:]
    row, col = grid_masks(length)

    def greet(barrier):
        for away in range(1, head_parts):
            pl.semaphore_signal(
                barrier, inc=1, device_id=(place, lax.rem(me + away, head_parts)), device_id_type=MESH
            )

    def core_copy(kind, s, y):
        return remote(
            low.at[kind, s, y], from_core.at[kind, s, y],
            core_send.at[kind, s, y], core_recv.at[kind, s, y], (place, sibling),
        )

    def line_copy(kind, s, away):
        return remote(
            to_line.at[kind, s, away - 1], from_line.at[kind, s, away - 1],
            line_send.at[kind, s, away - 1], line_recv.at[kind, s, away - 1],
            (place, 2 * lax.rem(line + away, lines) + core),
        )

    def stat_copy(kind, s, away):
        return remote(
            stat_own.at[kind, s], stat_in.at[kind, s, away - 1],
            stat_send.at[kind, s, away - 1], stat_recv.at[kind, s, away - 1],
            (place, lax.rem(me + away, head_parts)),
        )

    def send_part(kind, s, value):
        for j in range(head_parts):
            whole_part[j] = value[:, j * shard : (j + 1) * shard]
        for y in range(lines):
            low[kind, s, y] = whole_part[2 * y + (1 - core)].astype(BF16)
            core_copy(kind, s, y).start()
            part[kind % 2, s, y] = whole_part[2 * y + core]

    def join_core(kind, s):
        for y in range(lines):
            core_copy(kind, s, y).wait_recv()
        for away in range(1, lines):
            y = lax.rem(line + away, lines)
            joined = part[kind % 2, s, y] + from_core[kind, s, y].astype(F32)
            to_line[kind, s, away - 1] = joined.astype(BF16)
            line_copy(kind, s, away).start()
        part[kind % 2, s, line] = part[kind % 2, s, line] + from_core[kind, s, line].astype(F32)

    def joined_core(kind, s):
        for y in range(lines):
            core_copy(kind, s, y).wait_recv()
        others = [lax.rem(line + away, lines) for away in range(1, lines)]
        joined = [part[kind % 2, s, y] + from_core[kind, s, y].astype(F32) for y in [line] + others]
        return joined[0], joined[1:]

    def join_line(kind, s):
        total = part[kind % 2, s, line]
        for away in range(1, lines):
            line_copy(kind, s, away).wait_recv()
            total = total + from_line[kind, s, away - 1].astype(F32)
        return total

    def send_stat(kind, s, column):
        stat_own[kind, s] = jnp.broadcast_to(turn_to_row(column, row, col), (8, length))
        for away in range(1, head_parts):
            stat_copy(kind, s, away).start()

    def join_stat(kind, s):
        total = stat_own[kind, s]
        for away in range(1, head_parts):
            stat_copy(kind, s, away).wait_recv()
            total = total + stat_in[kind, s, away - 1]
        return turn_to_column(total[0:1, :], row, col)

    def drain(s):
        for kind in range(low.shape[0]):
            for y in range(lines):
                core_copy(kind, s, y).wait_send()
        for kind in range(to_line.shape[0]):
            for away in range(1, lines):
                line_copy(kind, s, away).wait_send()
        for kind in range(stats):
            for away in range(1, head_parts):
                stat_copy(kind, s, away).wait_send()

    return types.SimpleNamespace(
        me=me, place=place, lines=lines, core=core, line=line, sibling=sibling, greet=greet,
        send_part=send_part, join_core=join_core, join_line=join_line, send_stat=send_stat,
        join_stat=join_stat, drain=drain, joined_core=joined_core,
    )


def weight_rows(left, right, store):
    wide = left.shape[2]
    step = min(wide, 256)
    steps = wide // step

    def one(j, carry):
        start = pl.multiple_of(j * step, step)
        block = left[:, :, pl.ds(start, step)]
        store(start, step, raw(block.reshape(-1, step), right, TN).astype(BF16))
        return carry

    lax.fori_loop(0, steps, one, 0)
    if wide % step:
        rest = wide % step
        block = left[:, :, steps * step :]
        store(steps * step, rest, raw(block.reshape(-1, rest), right, TN).astype(BF16))


def middle_kernel(
    slots, head_parts, parts, heads, arrive, leave,
    gated, x_shard, cotangent, mask, out_weight, gate_weight, up_weight,
    down_weight, gain, mixer, gate, gain_row, eff,
    block_base, gate_part, residual_grad_out, mixer_rows_grad, mixer_grad, gate_grad_out,
    gain_grad_out, output_gain_grad, shifts_in, down_part, up_part, block_line,
    residual, act_all, up_grad_all, gate_grad_all,
    inverse, spread, shifts_low, shift_send, shift_recv,
    spread_line_send, spread_line_recv, spread_core_send, spread_core_recv,
    *refs,
):
    tools = head_tools(head_parts, refs, 2)
    me, place, lines, core, line, sibling = (
        tools.me, tools.place, tools.lines, tools.core, tools.line, tools.sibling
    )
    send_part, join_core, join_line = tools.send_part, tools.join_core, tools.join_line
    send_stat, join_stat = tools.send_stat, tools.join_stat
    length, shard = x_shard.shape[1], x_shard.shape[2]
    width = shard * head_parts
    hidden = gate_weight.shape[0]
    value_dim = mixer.shape[3]
    units = Units(parts, slots * heads)

    barrier = pltpu.get_barrier_semaphore()
    tools.greet(barrier)
    units.greet(barrier)
    gain_grad_out[...] = jnp.zeros_like(gain_grad_out)
    output_gain_grad[...] = jnp.zeros_like(output_gain_grad)
    pl.semaphore_wait(barrier, head_parts - 1 + parts - 1)

    def shift_copy(unit):
        return units.to_owner(shifts_low.at[unit], shifts_in, shift_send, shift_recv, unit)

    def spread_line_copy(kind, s, away):
        return remote(
            spread.at[kind, s, me], spread.at[kind, s, me],
            spread_line_send.at[kind, s, away - 1], spread_line_recv.at[kind, s, away - 1],
            (place, 2 * lax.rem(line + away, lines) + core),
        )

    def spread_core_copy(kind, s, away):
        y = lax.rem(line + away, lines)
        return remote(
            spread.at[kind, s, 2 * y + core], spread.at[kind, s, 2 * y + core],
            spread_core_send.at[kind, s, away], spread_core_recv.at[kind, s, away], (place, sibling),
        )

    def spread_core_arrival(kind, s, away):
        y = lax.rem(line + away, lines)
        return remote(
            spread.at[kind, s, 2 * y + (1 - core)], spread.at[kind, s, 2 * y + (1 - core)],
            spread_core_send.at[kind, s, away], spread_core_recv.at[kind, s, away], (place, sibling),
        )

    def spread_line_arrival(kind, s, away):
        y = lax.rem(line + lines - away, lines)
        return remote(
            spread.at[kind, s, 2 * y + core], spread.at[kind, s, 2 * y + core],
            spread_line_send.at[kind, s, away - 1], spread_line_recv.at[kind, s, away - 1],
            (place, 2 * y + core),
        )

    def send_spread(kind, s, value):
        spread[kind, s, me] = value
        for away in range(1, lines):
            spread_line_copy(kind, s, away).start()
        spread_core_copy(kind, s, 0).start()

    def pass_spread(kind, s):
        for away in range(1, lines):
            spread_line_arrival(kind, s, lines - away).wait_recv()
            spread_core_copy(kind, s, away).start()

    def take_spread(kind, s):
        for away in range(lines):
            spread_core_arrival(kind, s, away).wait_recv()
        return jnp.concatenate([spread[kind, s, j] for j in range(head_parts)], axis=1)

    def attention(s):
        send_part(0, s, raw(gated[s], out_weight[...], NN))

    def rows_in(s):
        total = x_shard[s].astype(F32) + mask[s][:, 0:1] * join_line(0, s)
        residual[s] = total
        send_stat(0, s, jnp.sum(total * total, axis=1, keepdims=True))

    def norm_second(s):
        inv = lax.rsqrt(join_stat(0, s) / width + NORM_EPSILON)
        inverse[s] = jnp.broadcast_to(inv, (length, LANES))
        send_spread(0, s, (residual[s] * inv * gain[0:1, :]).astype(BF16))

    def swiglu(s):
        normed = take_spread(0, s)
        valid = mask[s][:, 0:1]
        gate_values = raw(normed, gate_weight[...], NT)
        up_values = raw(normed, up_weight[...], NT)
        act_grad = raw(cotangent[s], down_weight[...], NT) * valid
        sig = sigmoid(gate_values)
        silu = gate_values * sig
        act_all[s] = (silu * up_values * valid).astype(BF16)
        up_grad = (act_grad * silu).astype(BF16)
        gate_grad = (act_grad * up_values * sig * (1.0 + gate_values * (1.0 - sig))).astype(BF16)
        up_grad_all[s] = up_grad
        gate_grad_all[s] = gate_grad
        send_part(1, s, raw(up_grad, up_weight[...], NN) + raw(gate_grad, gate_weight[...], NN))

    def swiglu_out(s):
        send_part(2, s, raw(act_all[s], down_weight[...], NN))

    def block_rows(s):
        valid = mask[s][:, 0:1]
        own, others = tools.joined_core(2, s)
        block_base[s] = residual[s] + valid * own
        for i, other in enumerate(others):
            block_line[s, i] = (valid * other).astype(BF16)
        leave(s, 0, 11)

    def norm_back(s):
        grad = join_line(1, s)
        inv = inverse[s][:, 0:1]
        gain_grad_out[0:1, :] += jnp.sum(grad * residual[s] * inv, axis=0, keepdims=True)
        weighted = grad * gain[0:1, :]
        residual_grad_out[s] = weighted
        send_stat(1, s, jnp.sum(weighted * residual[s], axis=1, keepdims=True))

    def residual_back(s):
        stat = join_stat(1, s) / width
        inv = inverse[s][:, 0:1]
        cot = cotangent[s, :, pl.ds(pl.multiple_of(me * shard, shard), shard)].astype(F32)
        grad = cot + inv * (residual_grad_out[s] - residual[s] * (inv * inv * stat))
        residual_grad_out[s] = grad
        leave(s, 2)
        send_spread(1, s, (mask[s][:, 0:1] * grad).astype(BF16))

    def gate_back(s, gated_grad):
        out_gain = gain_row[0:1, :]
        for h in range(heads):
            here = slice(h * value_dim, (h + 1) * value_dim)
            grad = gated_grad[:, here]
            mixer_h = mixer[s, h]
            gate_h = gate[s, :, here]
            scale = lax.rsqrt(jnp.sum(mixer_h * mixer_h, axis=1, keepdims=True) / value_dim + NORM_EPSILON)
            sig = sigmoid(gate_h)
            unit_rows = mixer_h * scale
            gate_grad_out[s, :, here] = (
                grad * unit_rows * out_gain * (sig * (1.0 + gate_h * (1.0 - sig)))
            ).astype(BF16)
            scaled_grad = grad * (gate_h * sig)
            output_gain_grad[0:1, :] += jnp.sum(scaled_grad * unit_rows, axis=0, keepdims=True)
            unit_grad = scaled_grad * out_gain
            stat = jnp.sum(unit_grad * mixer_h, axis=1, keepdims=True) / value_dim
            mixer_grad_h = scale * (unit_grad - mixer_h * (scale * scale * stat))
            mixer_grad[s, h] = mixer_grad_h
            entering = mm(split(mixer_grad_h), split(eff[s, h]), TN).astype(BF16)
            for i, piece in enumerate(units.pieces(entering)):
                shifts_low[(s * heads + h) * units.share + i] = piece

        for i in range(heads * units.share):
            unit = s * heads * units.share + i

            @pl.when(unit != units.me)
            def _(unit=unit):
                shift_copy(unit).start()

            @pl.when(unit == units.me)
            def _(unit=unit):
                shifts_in[unit] = shifts_low[unit]

    def mixer_rows(s):
        grad = take_spread(1, s)
        mixer_rows_grad[s] = grad
        gate_back(s, raw(grad, out_weight[...], NT))
        leave(s, 3, 4, 5)

    stages = (
        (10, mixer_rows),
        (9, functools.partial(pass_spread, 1)),
        (8, residual_back),
        (7, norm_back),
        (6, functools.partial(join_core, 1)),
        (10, block_rows),
        (4, functools.partial(pass_spread, 0)),
        (3, norm_second),
        (2, rows_in),
        (1, functools.partial(join_core, 0)),
        (0, attention),
        (5, swiglu),
        (9, swiglu_out),
    )

    def step(t, carry):
        @pl.when(t == 5)
        def _():
            arrive(0)

        @pl.when(t == 10)
        def _():
            arrive(1)

        for offset, stage in stages:
            s = t - offset

            @pl.when((s >= 0) & (s < slots))
            def _(stage=stage, s=s):
                stage(s)

        def normed_rows():
            return jnp.concatenate(
                [spread[0, :, j].reshape(slots * length, shard) for j in range(head_parts)], axis=1
            )

        def cotangent_rows():
            return cotangent[...].reshape(-1, width)

        for late, left, right, target, index in (
            (5, act_all, cotangent_rows, down_part, 9),
            (6, up_grad_all, normed_rows, up_part, 10),
            (7, gate_grad_all, normed_rows, gate_part, 1),
        ):

            @pl.when(t == slots + late)
            def _(left=left, right=right, target=target, index=index):
                def store(start, size, block):
                    target[pl.ds(start, size), :] = block

                weight_rows(left, right(), store)
                if target.shape[0] > hidden:
                    target[hidden:, :] = jnp.zeros((target.shape[0] - hidden, width), BF16)
                leave(None, index)

        return carry

    lax.fori_loop(0, slots + 10, step, 0)

    def drain(s, carry):
        tools.drain(s)
        for kind in range(2):
            for away in range(1, lines):
                spread_line_copy(kind, s, away).wait_send()
            for away in range(lines):
                spread_core_copy(kind, s, away).wait_send()
        return carry

    lax.fori_loop(0, slots, drain, 0)

    def take_units(away, carry):
        unit = lax.rem(units.me + away, parts)
        units.at_owner(shifts_low.at[0], shifts_in, shift_send, shift_recv, unit).wait_recv()
        return carry

    lax.fori_loop(1, parts, take_units, 0)

    def drain_units(away, carry):
        shift_copy(lax.rem(units.me + away, parts)).wait_send()
        return carry

    lax.fori_loop(1, parts, drain_units, 0)


def padded_rows(count, parts):
    return count + -count % (32 * parts)


def middle_call(parts, head_parts, heads, *operands):
    gated, x_shard, gate_weight, mixer, eff = (operands[i] for i in (0, 1, 5, 9, 12))
    slots, length, shard = x_shard.shape
    width = shard * head_parts
    hidden = gate_weight.shape[0]
    lines = head_parts // 2
    value_dim, key_dim = mixer.shape[3], eff.shape[3]
    unit = (parts, value_dim * slots * heads // parts, key_dim)
    sds = jax.ShapeDtypeStruct
    dma = pltpu.SemaphoreType.DMA
    product = sds((padded_rows(hidden, parts), width), BF16)
    rows = sds((slots, length, shard), F32)
    outs = (
        rows, product, rows,
        sds((slots, length, width), BF16), sds(mixer.shape, F32),
        sds(gated.shape, BF16), sds((8, shard), F32), sds((8, value_dim), F32), sds(unit, BF16), product, product,
        sds((slots, lines - 1, length, shard), BF16),
    )
    scratch = (
        [
            pltpu.VMEM(rows.shape, F32),
            pltpu.VMEM((slots, length, hidden), BF16),
            pltpu.VMEM((slots, length, hidden), BF16),
            pltpu.VMEM((slots, length, hidden), BF16),
            pltpu.VMEM((slots, length, LANES), F32),
            pltpu.VMEM((2, slots, head_parts, length, shard), BF16),
            pltpu.VMEM(unit, BF16), dma((parts - 1,)), dma((parts - 1,)),
            dma((2, slots, lines - 1)), dma((2, slots, lines - 1)),
            dma((2, slots, lines)), dma((2, slots, lines)),
        ]
        + head_scratch(3, 2, slots, head_parts, length, shard)
    )
    return staged_call(
        functools.partial(middle_kernel, slots, head_parts, parts, heads),
        operands, outs, scratch, 0, late=((5, 6, 7, 2), (9, 10, 12)), leaving=(0, 1, 2, 3, 4, 5, 9, 10, 11),
        slots=slots,
    )


def ring_scratch(parts, shapes):
    dma = pltpu.SemaphoreType.DMA
    count = len(shapes)
    return [
        pltpu.VMEM((2, parts, rows // (2 * parts), wide), BF16) for rows, wide in shapes
    ] + [dma((count, 2)), dma((count, 2, parts - 1)), dma((count, 2)), dma((count, 2, parts - 1)), dma((count, 2))]


def ring_tools(parts, ins, outs, held, send, recv, spread_send, spread_recv, own):
    count = len(ins)
    index = lax.axis_index("seq")
    other = lax.axis_index("head")
    side = lax.rem(index, 2)
    level = index // 2
    levels = parts // 2
    position = jnp.where(side == 1, level, parts - 1 - level)
    up = jnp.where(side == 1, jnp.where(level == levels - 1, index - 1, index + 2),
                   jnp.where(level == 0, index + 1, index - 2))
    down = jnp.where(side == 1, jnp.where(level == 0, index - 1, index - 2),
                     jnp.where(level == levels - 1, index + 1, index + 2))
    targets = (up, down)
    def greet(barrier):
        for target in targets:
            pl.semaphore_signal(barrier, inc=1, device_id=(target, other), device_id_type=MESH)

    def rows_of(a, way, chunk):
        size = ins[a].shape[0] // (2 * parts)
        return pl.ds(pl.multiple_of((chunk * 2 + way) * size, size), size)

    def chunk_at(way, step):
        if way == 0:
            return lax.rem(position - step + 2 * parts, parts)
        return lax.rem(position + step + 2 * parts, parts)

    def sum_copy(a, way, step):
        return remote(
            held[a].at[way, step], held[a].at[way, step + 1], send.at[a, way], recv.at[a, way, step],
            (targets[way], other),
        )

    def spread_copy(a, way, step):
        block = rows_of(a, way, chunk_at(way, step - 1))
        return remote(
            outs[a].at[block, :], outs[a].at[block, :], spread_send.at[a, way], spread_recv.at[a, way, step],
            (targets[way], other),
        )

    def spread_first(a, way):
        block = rows_of(a, way, chunk_at(way, parts - 1))
        return remote(
            held[a].at[way, parts - 1], outs[a].at[block, :], spread_send.at[a, way],
            spread_recv.at[a, way, 0], (targets[way], other),
        )

    def own_copy(a, way):
        block = rows_of(a, way, chunk_at(way, parts - 1))
        return pltpu.make_async_copy(held[a].at[way, parts - 1], outs[a].at[block, :], own.at[a, way])

    def spread_arrival(a, way, step):
        block = rows_of(a, way, chunk_at(way, step))
        return remote(
            outs[a].at[block, :], outs[a].at[block, :], spread_send.at[a, way], spread_recv.at[a, way, step],
            (targets[way], other),
        )

    lanes = [(a, way) for a in range(count) for way in range(2)]
    last = parts - 2

    def add(step, a, way):
        sum_copy(a, way, step).wait_recv()
        mine = ins[a][rows_of(a, way, chunk_at(way, step + 1)), :].astype(F32)
        return (held[a][way, step + 1].astype(F32) + mine).astype(BF16)

    def begin():
        for a, way in lanes:
            held[a][way, 0] = ins[a][rows_of(a, way, chunk_at(way, 0)), :]
            sum_copy(a, way, 0).start()

    def one(step):
        for a, way in lanes:
            held[a][way, step + 1] = add(step, a, way)
            sum_copy(a, way, step).wait_send()
            sum_copy(a, way, step + 1).start()

    def turn():
        for a, way in lanes:
            held[a][way, parts - 1] = add(last, a, way)
            sum_copy(a, way, last).wait_send()
            spread_first(a, way).start()
            own_copy(a, way).start()

    def pass_first():
        for a, way in lanes:
            spread_arrival(a, way, 0).wait_recv()
            spread_first(a, way).wait_send()
            spread_copy(a, way, 1).start()

    def pass_on(step):
        for a, way in lanes:
            spread_arrival(a, way, step).wait_recv()
            spread_copy(a, way, step).wait_send()
            spread_copy(a, way, step + 1).start()

    def finish():
        for a, way in lanes:
            spread_arrival(a, way, last).wait_recv()
            spread_copy(a, way, last).wait_send()
            own_copy(a, way).wait()

    def tick(k):
        @pl.when(k < last)
        def _():
            one(k)

        @pl.when(k == last)
        def _():
            turn()

        @pl.when(k == last + 1)
        def _():
            pass_first()

        @pl.when(k > last + 1)
        def _():
            pass_on(k - last - 1)

    return types.SimpleNamespace(
        greet=greet, begin=begin, tick=tick, finish=finish, ticks=2 * parts - 3, up=up, down=down
    )


def backward_kernel(
    slots, heads, key_dim, value_dim, parts, head_parts, arrive, leave,
    mixer_grad, shifts_in, gated, mixer_rows_grad, normed, gate_grad,
    pre, rim, ab, abt, taps_ref, lanes, cols,
    queries, keys, value_rows, inverse_all, delta_rows, states, maps_in, gate_part,
    query_weight, key_weight, value_weight, gate_weight, ab_weight, x_shard, inv_first, residual_grad, input_gain,
    gain_part, mixed_part, up_part, down_part, block_base, block_line,
    input_grad_out, small_sum, gate_sum, out_sum, first_sum, unit_sum, value_sum, up_sum, down_sum, block_out,
    ab_grad_out, taps_grad_out, lane_grad_out, out_part, first_part,
    ext, conv_grad, tail, rim_own, rim_in, leavings, leaving_send,
    small_lines, small_own, small_in, gain_own, gain_in, block_in, block_send, block_recv,
    back_send, back_recv, rim_send, rim_recv, small_send, small_recv, gain_send, gain_recv, *refs,
):
    length = pre.shape[1]
    taps = 4
    width = normed.shape[2]
    values = gated.shape[2]
    units = Units(parts, slots * heads)
    me = units.me
    tools = head_tools(head_parts, refs[27:], 1)
    place, head = me, units.other
    pre_grad_out = pre
    shard = x_shard.shape[2]
    channels = pre.shape[2]
    unit_wide = 2 * heads * key_dim
    unit_own = mixer_rows_grad.at[:, 0:unit_wide]
    value_own = mixer_rows_grad.at[:, unit_wide:channels]
    rings = (
        ring_tools(parts, (gate_part, up_part), (gate_sum, up_sum), refs[0:2], *refs[2:7]),
        ring_tools(
            parts, (down_part, out_part, first_part), (down_sum, out_sum, first_sum), refs[7:10], *refs[10:15]
        ),
        ring_tools(parts, (unit_own,), (unit_sum,), refs[15:16], *refs[16:21]),
        ring_tools(parts, (value_own,), (value_sum,), refs[21:22], *refs[22:27]),
    )
    barrier = pltpu.get_barrier_semaphore()
    units.greet(barrier)
    tools.greet(barrier)
    row, col = grid_masks(length)
    taps_grad_out[...] = jnp.zeros_like(taps_grad_out)
    lane_grad_out[...] = jnp.zeros_like(lane_grad_out)
    pl.semaphore_wait(barrier, parts - 1 + head_parts - 1)
    rings[0].begin()

    def back_copy(place):
        ahead = units.ahead(place)
        return remote(
            leaving_send.at[place], leavings.at[me], back_send.at[ahead], back_recv.at[ahead],
            (place, units.other),
        )

    def back_arrival(unit):
        behind = units.behind(unit)
        return remote(
            leaving_send.at[unit], leavings.at[unit], back_send.at[behind], back_recv.at[behind],
            (unit, units.other),
        )

    def rim_copy():
        return remote(
            rim_own, rim_in, rim_send.at[0], rim_recv.at[0], (lax.rem(me + parts - 1, parts), units.other)
        )

    def scan(hop, leaving):
        place = parts - 1 - hop
        low = leaving.astype(BF16)

        @pl.when(place != me)
        def _():
            leaving_send[place] = low
            back_copy(place).start()

        @pl.when(place == me)
        def _():
            leavings[place] = low

        return mm(split(leaving), maps_in[place], NT) + shifts_in[place].astype(F32)

    lax.fori_loop(0, parts, scan, jnp.zeros((value_dim // units.share, key_dim), F32))
    arrive(0)

    def store_out(start, size, block):
        out_part[pl.ds(start, size), :] = block

    def store_first(start, size, block):
        first_part[pl.ds(start, size), :] = block

    weight_rows(gated, mixer_rows_grad[...], store_out)
    weight_rows(normed, gate_grad[...].reshape(-1, values), store_first)
    rings[1].begin()
    arrive(1)

    def block_copy(s, away):
        target = 2 * lax.rem(tools.line + away, tools.lines) + tools.core
        return remote(
            block_line.at[s, away - 1], block_in.at[s, away - 1], block_send.at[s, away - 1],
            block_recv.at[s, away - 1], (place, target),
        )

    for s in range(slots):
        for away in range(1, tools.lines):
            block_copy(s, away).start()
    rings[0].tick(0)

    def delta_slot(s, carry):
        for i in range(heads * units.share):
            unit = s * heads * units.share + i

            @pl.when(unit != me)
            def _(unit=unit):
                back_arrival(unit).wait_recv()

        ext[0:RIM, :] = rim[s]
        ext[RIM : RIM + length, :] = pre[s].astype(F32)
        lane = lax.broadcasted_iota(jnp.int32, (length, LANES), 1)
        log_cols, strength_cols = gates_of(ab[s], lanes[0:1, :], lanes[1:2, :])
        log_rows, strength_rows = gates_of(abt[s], cols[0:8, 0:1], cols[8:16, 0:1])
        key_start = heads * key_dim
        value_start = 2 * heads * key_dim
        strict = row > col
        grads = jnp.zeros((length, LANES), F32)
        conv_grad[0:RIM, :] = jnp.zeros((RIM, conv_grad.shape[1]), F32)
        conv_grad[RIM + length : 2 * RIM + length, :] = jnp.zeros((RIM, conv_grad.shape[1]), F32)

        def activation(start, width):
            total = taps_ref[0:1, start : start + width] * ext[pl.ds(RIM - taps + 1, length), start : start + width]
            for tap in range(1, taps):
                total = total + (
                    taps_ref[tap : tap + 1, start : start + width]
                    * ext[pl.ds(RIM - taps + 1 + tap, length), start : start + width]
                )
            sig = sigmoid(total)
            return total * sig, sig * (1.0 + total * (1.0 - sig))

        def unit_back(grad, start, scale_by):
            act, slope = activation(start, key_dim)
            scale = lax.rsqrt(jnp.sum(act * act, axis=1, keepdims=True) + UNIT_EPSILON)
            inner = jnp.sum(act * grad, axis=1, keepdims=True)
            back = scale_by * scale * (grad - act * (scale * scale * inner))
            conv_grad[RIM : RIM + length, start : start + key_dim] = back * slope

        for h in range(heads):
            query, key, value = queries[s, h], keys[s, h], value_rows[s, h]
            query_f, key_f = query.astype(F32), key.astype(F32)
            strength = strength_cols[:, heads + h : heads + h + 1]
            cum_col, cum_row, end, decayed = decay_of(
                log_cols[:, h : h + 1], log_rows[h : h + 1, :], row, col
            )
            rise = jnp.exp(cum_col)
            end_weight = jnp.exp(end - cum_col)
            state = units.whole(states, s * heads + h)
            leaving = units.whole(leavings, s * heads + h)
            state_f, leaving_f = state.astype(F32), leaving.astype(F32)
            rows = split(delta_rows[s, h])
            out_grad = split(mixer_grad[s, h])
            products = mm(key, key, NT)
            scores = decayed * mm(query, key, NT)
            rows_grad = mm(split(scores), out_grad, TN) + end_weight * mm(key, leaving, NT)
            scores_grad = mm(out_grad, rows, NT)
            query_grad = rise * mm(out_grad, state)
            right_grad = mm(split(inverse_all[s, h]), split(rows_grad), TN)
            key_state = mm(key, state, NT)
            triangle_grad = -jnp.where(strict, mm(split(right_grad), rows, NT), 0.0)
            value_grad = strength * right_grad
            strength_grad = jnp.sum(right_grad * (value.astype(F32) - rise * key_state), axis=1, keepdims=True)
            read_grad = -rise * value_grad
            cum_grad = jnp.sum(read_grad * key_state, axis=1, keepdims=True)
            key_grad = mm(split(read_grad), state)
            decayed_grad = triangle_grad * decayed
            strength_grad = strength_grad + jnp.sum(decayed_grad * products, axis=1, keepdims=True)
            weighted = strength * decayed_grad
            both = weighted * products + scores_grad * scores
            products_grad = split(weighted)
            overlap_grad = split(scores_grad * decayed)
            cum_grad = cum_grad + jnp.sum(both, axis=1, keepdims=True) + jnp.sum(query_f * query_grad, axis=1, keepdims=True)
            query_grad = query_grad + mm(overlap_grad, key)
            key_grad = (
                key_grad + mm(overlap_grad, query, TN) + mm(products_grad, key) + mm(products_grad, key, TN)
            )
            moved = mm(rows, leaving)
            key_grad = key_grad + end_weight * moved
            end_part = jnp.sum(moved * key_f, axis=1, keepdims=True) * end_weight
            cum_grad = cum_grad - end_part
            last = jnp.sum(end_part, axis=0, keepdims=True) + jnp.exp(end) * jnp.sum(
                jnp.sum(leaving_f * state_f, axis=1, keepdims=True), axis=0, keepdims=True
            )
            turned = jnp.sum(jnp.where(row == col, cum_grad, 0.0), axis=0, keepdims=True)
            turned = turned - jnp.sum(both, axis=0, keepdims=True)
            log_grad = jnp.sum(jnp.where(row <= col, turned, 0.0), axis=1, keepdims=True) + last
            grads = jnp.where(lane == h, log_grad, grads)
            grads = jnp.where(lane == heads + h, strength_grad, grads)
            unit_back(query_grad, h * key_dim, key_dim ** (-0.5))
            unit_back(key_grad, key_start + h * key_dim, 1.0)
            if h == 0:
                rings[0].tick(s + 1)
            _, slope = activation(value_start + h * value_dim, value_dim)
            conv_grad[RIM : RIM + length, value_start + h * value_dim : value_start + (h + 1) * value_dim] = (
                value_grad * slope
            )

        softened = -lanes[0:1, :] * sigmoid(ab[s] + lanes[1:2, :])
        decay_part = grads * softened
        is_log = lane < heads
        ab_grad_out[s] = jnp.where(is_log, decay_part, grads * strength_cols * (1.0 - strength_cols))
        lane_grad_out[0:1, :] += jnp.sum(jnp.where(is_log, grads * log_cols, 0.0), axis=0, keepdims=True)
        lane_grad_out[1:2, :] += jnp.sum(jnp.where(is_log, decay_part, 0.0), axis=0, keepdims=True)
        main = conv_grad[RIM : RIM + length, :]
        pre_grad = jnp.zeros_like(main)
        rim_grad = jnp.zeros((RIM, conv_grad.shape[1]), F32)
        for tap in range(taps):
            weight = taps_ref[tap : tap + 1, :]
            taps_grad_out[tap : tap + 1, :] += jnp.sum(
                main * ext[pl.ds(RIM - taps + 1 + tap, length), :], axis=0, keepdims=True
            )
            pre_grad = pre_grad + weight * conv_grad[pl.ds(RIM + taps - 1 - tap, length), :]
            rim_grad = rim_grad + weight * conv_grad[pl.ds(taps - 1 - tap, RIM), :]
        pre_grad_out[s] = pre_grad.astype(BF16)
        tail[s] = pre_grad[length - 2 * RIM : length, :]
        rim_own[s] = rim_grad
        rings[1].tick(s)
        return carry

    lax.fori_loop(0, slots, delta_slot, 0)
    rim_copy().start()

    rings[0].tick(slots + 1)
    rings[1].tick(slots)
    rim_copy().wait_recv()
    inside = me < parts - 1
    for s in range(slots):
        late = jnp.where(inside, rim_in[s], 0.0)
        end = tail[s]
        shifted_in = jnp.concatenate([jnp.zeros_like(late), late], axis=0)
        pre_grad_out[s, length - 2 * RIM : length, :] = (end + shifted_in).astype(BF16)
    rim_copy().wait_send()

    def gain_copy(away):
        return remote(
            gain_own, gain_in.at[away - 1], gain_send.at[away - 1], gain_recv.at[away - 1],
            (place, lax.rem(head + away, head_parts)),
        )

    def small_copy(away):
        return remote(
            small_own, small_in.at[away - 1], small_send.at[away - 1], small_recv.at[away - 1],
            (lax.rem(place + away, parts), head),
        )

    def store_unit(start, size, block):
        unit_own[pl.ds(start, size), :] = block

    def store_value(start, size, block):
        value_own[pl.ds(start, size), :] = block

    weight_rows(normed, pre_grad_out[:, :, :unit_wide].reshape(-1, unit_wide), store_unit)
    rings[2].begin()
    weight_rows(normed, pre_grad_out[:, :, unit_wide:].reshape(-1, channels - unit_wide), store_value)
    rings[3].begin()

    def products(s, carry):
        low = ab_grad_out[s].astype(BF16)
        half = unit_wide // 2
        tools.send_part(
            0, s,
            raw(pre_grad_out[s, :, :half], query_weight[...], NT)
            + raw(pre_grad_out[s, :, half:unit_wide], key_weight[...], NT)
            + raw(pre_grad_out[s, :, unit_wide:], value_weight[...], NT)
            + raw(gate_grad[s], gate_weight[...], NT)
            + raw(low, ab_weight[...], NN),
        )
        ring_round(s)
        return carry

    ticks = rings[0].ticks

    def ring_round(j):
        for ring, step in (
            (rings[0], slots + 2 + j), (rings[2], 2 * j), (rings[3], 2 * j),
            (rings[1], slots + 1 + j), (rings[2], 2 * j + 1), (rings[3], 2 * j + 1),
        ):

            @pl.when(step < ticks)
            def _(ring=ring, step=step):
                ring.tick(step)

    arrive(2)
    lax.fori_loop(0, slots, products, 0)
    arrive(3)


    def first_join(s, carry):
        tools.join_core(0, s)
        return carry

    lax.fori_loop(0, slots, first_join, 0)
    ring_round(jnp.int32(slots))
    small_lines[...] = jnp.zeros_like(small_lines)
    gain_own[...] = gain_part[...]
    for away in range(1, head_parts):
        gain_copy(away).start()

    def second_join(s, carry):
        grad = tools.join_line(0, s)
        x = x_shard[s].astype(F32)
        inv = inv_first[s][:, 0:1]
        weighted = grad * input_gain[:, pl.ds(pl.multiple_of(head * shard, shard), shard)]
        input_grad_out[s] = weighted
        tools.send_stat(0, s, jnp.sum(weighted * x, axis=1, keepdims=True))
        return carry + jnp.sum(grad * x * inv, axis=0, keepdims=True)

    gain_line = lax.fori_loop(0, slots, second_join, jnp.zeros((1, shard), F32))
    ring_round(jnp.int32(slots + 1))

    def input_rows(s, carry):
        stat = tools.join_stat(0, s) / width
        inv = inv_first[s][:, 0:1]
        input_grad_out[s] = residual_grad[s] + inv * (
            input_grad_out[s] - x_shard[s].astype(F32) * (inv * inv * stat)
        )
        return carry

    lax.fori_loop(0, slots, input_rows, 0)
    gain_total = gain_own[...]
    for away in range(1, head_parts):
        gain_copy(away).wait_recv()
        gain_total = gain_total + gain_in[away - 1]
    low = ab_grad_out[...].astype(BF16).reshape(-1, LANES)
    ab_lines = raw(low, normed[...].reshape(-1, width), TN)
    at = 0
    for lines in [taps_grad_out[t : t + 1, :] for t in range(taps)] + [
        ab_lines[t : t + 1, :] for t in range(2 * heads)
    ] + [gain_total[0:1, :], lane_grad_out[0:1, :], lane_grad_out[1:2, :], mixed_part[0:1, :], gain_line]:
        for j in range(lines.shape[1] // LANES):
            small_lines[at : at + 1, :] = lines[:, j * LANES : (j + 1) * LANES]
            at += 1
    small_own[...] = small_lines[...].astype(BF16)

    def small_start(away, carry):
        small_copy(away).start()
        return carry

    lax.fori_loop(1, parts, small_start, 0)

    def rest(j, carry):
        ring_round(j)
        return carry

    lax.fori_loop(slots + 2, ticks - slots - 1, rest, 0)
    small_sum[...] = small_lines[...]

    def small_join(away, carry):
        small_copy(away).wait_recv()
        small_sum[...] += small_in[away - 1].astype(F32)
        small_copy(away).wait_send()
        return carry

    lax.fori_loop(1, parts, small_join, 0)
    for s in range(slots):
        total = block_base[s]
        for away in range(1, tools.lines):
            block_copy(s, away).wait_recv()
            total = total + block_in[s, away - 1].astype(F32)
            block_copy(s, away).wait_send()
        block_out[s] = total.astype(BF16)
    for away in range(1, head_parts):
        gain_copy(away).wait_send()

    def drain(s, carry):
        tools.drain(s)
        return carry

    lax.fori_loop(0, slots, drain, 0)
    def drain_units(away, carry):
        back_copy(lax.rem(me + away, parts)).wait_send()
        return carry

    lax.fori_loop(1, parts, drain_units, 0)
    for ring in rings:
        ring.finish()


def backward_call(parts, head_parts, heads, taps, *operands):
    gated, normed, gate_grad, pre, ab, keys, value_rows, states, gate_part, x_shard, gain_part, down_part = (
        operands[i] for i in (2, 4, 5, 6, 8, 14, 15, 18, 20, 26, 30, 33)
    )
    slots, length, channels = pre.shape
    value_dim, key_dim = value_rows.shape[3], keys.shape[3]
    width, shard = normed.shape[2], x_shard.shape[2]
    lines = (taps * channels + 2 * heads * width + gain_part.shape[1] + 2 * shard) // LANES + 2
    lines += -lines % 16
    sds = jax.ShapeDtypeStruct
    dma = pltpu.SemaphoreType.DMA
    out_shape = (padded_rows(gated.shape[2], parts), width)
    first_shape = (width, gate_grad.shape[2])
    unit_shape = (width, 2 * heads * key_dim)
    value_shape = (width, heads * value_dim)
    sums = (gate_part.shape, out_shape, first_shape, unit_shape, value_shape, gate_part.shape, down_part.shape)
    outs = (sds(x_shard.shape, F32), sds((lines, LANES), F32)) + tuple(sds(a, BF16) for a in sums + (x_shard.shape,))
    away = head_parts // 2 - 1
    unit = pltpu.VMEM(states.shape, BF16)
    edge = pltpu.VMEM((slots, RIM, channels), F32)
    scratch = (
        [
            pltpu.VMEM(ab.shape, F32), pltpu.VMEM((8, channels), F32),
            pltpu.VMEM((8, LANES), F32),
        ]
        + [pltpu.VMEM(a, BF16) for a in sums[1:3]]
        + [
            pltpu.VMEM((length + RIM, channels), F32), pltpu.VMEM((length + 2 * RIM, channels), F32),
            pltpu.VMEM((slots, 2 * RIM, channels), F32), edge, edge, unit, unit,
            pltpu.VMEM((lines, LANES), F32), pltpu.VMEM((lines, LANES), BF16),
            pltpu.VMEM((parts - 1, lines, LANES), BF16),
            pltpu.VMEM(gain_part.shape, F32), pltpu.VMEM((head_parts - 1,) + gain_part.shape, F32),
            pltpu.VMEM((slots, away, length, shard), BF16), dma((slots, away)), dma((slots, away)),
            dma((parts - 1,)), dma((parts - 1,)), dma((1,)), dma((1,)),
            dma((parts - 1,)), dma((parts - 1,)), dma((head_parts - 1,)), dma((head_parts - 1,)),
        ]
        + ring_scratch(parts, [gate_part.shape, gate_part.shape])
        + ring_scratch(parts, [down_part.shape, out_shape, first_shape])
        + ring_scratch(parts, [unit_shape])
        + ring_scratch(parts, [value_shape])
        + head_scratch(1, 1, slots, head_parts, length, shard)
    )
    return staged_call(
        functools.partial(backward_kernel, slots, heads, key_dim, value_dim, parts, head_parts),
        operands, outs, scratch, 3,
        late=(
            (2, 3, 4, 5, 33), (0, 6, 7, 8, 9, 13, 14, 15, 16, 17, 18, 35), (21, 22, 23, 24, 25),
            (26, 27, 28, 29, 30, 31, 34),
        ),
        kept=(2, 3, 4, 5, 6, 7, 8), flops=5 * 10**10,
    )


def per_device(
    hidden_in, lengths, input_gain, query_weight, key_weight, value_weight, alpha_weight, beta_weight,
    decay_log, decay_bias, query_kernel, key_kernel, value_kernel, gate_weight, output_gain,
    output_weight, mixed_gain, swiglu_gate, swiglu_up, swiglu_down, cotangent,
):
    slots, segment, width = hidden_in.shape
    heads = decay_log.shape[0]
    key_dim = query_kernel.shape[1] // heads
    value_dim = value_kernel.shape[1] // heads
    taps = query_kernel.shape[0]
    split_key = heads * key_dim
    channels = 2 * split_key + heads * value_dim
    head_parts = lax.axis_size("head")
    seq_parts = lax.axis_size("seq")
    shard = width // head_parts

    position = lax.axis_index("seq") * segment + jnp.arange(segment)
    mask = (position[None, :] < lengths[:, None]).astype(F32)[:, :, None]
    lane_mask = jnp.broadcast_to(mask, (slots, segment, LANES))
    ab_weight = jnp.concatenate(
        [alpha_weight.T, beta_weight.T, jnp.zeros((LANES - 2 * heads, width), BF16)], axis=0
    )
    gain_row = output_gain[None, :]

    (
        query, key, value, inverse, eff, delta_rows, mixer, gated, normed_first, pre_all, gate_pre, x_low,
        inv_first, rim_pre, ab_pre, ab_rows, states, maps_in, kernel, lane_gates, col_gates,
    ) = forward_call(
        seq_parts, head_parts, heads, hidden_in, input_gain[None, :],
        query_weight, key_weight, value_weight, gate_weight, ab_weight, query_kernel, key_kernel, value_kernel,
        decay_log[None, :], decay_bias[None, :], gain_row,
    )
    (
        block_base, gate_part, residual_grad, mixer_rows_grad, mixer_grad, gate_grad, mixed_part, gain_part,
        shifts_in, down_part, up_part, block_line,
    ) = middle_call(
        seq_parts, head_parts, heads, gated, x_low, cotangent, lane_mask, output_weight, swiglu_gate.T,
        swiglu_up.T, swiglu_down, mixed_gain[None, :], mixer, gate_pre, gain_row, eff,
    )
    (
        input_grad, small_sum, gate_sum, out_sum, gate_first_sum, unit_sum, value_sum, up_sum, down_sum,
        block_out,
    ) = backward_call(
        seq_parts, head_parts, heads, taps, mixer_grad, shifts_in, gated,
        mixer_rows_grad.reshape(slots * segment, width), normed_first, gate_grad,
        pre_all, rim_pre, ab_pre, ab_rows, kernel, lane_gates, col_gates, query, key, value, inverse, delta_rows,
        states, maps_in, gate_part, query_weight, key_weight, value_weight, gate_weight, ab_weight, x_low,
        inv_first, residual_grad, input_gain[None, :], gain_part, mixed_part,
        up_part, down_part, block_base, block_line,
    )
    hidden = swiglu_gate.shape[1]
    flat_small = small_sum.reshape(-1)
    pieces, at = [], 0
    for size in (taps * channels, 2 * heads * width, value_dim, LANES, LANES, shard, shard):
        pieces.append(flat_small[at : at + size])
        at += size
    taps_sum = pieces[0].reshape(taps, channels)
    ab_sum = pieces[1].reshape(2 * heads, width).T
    value_share = value_dim // head_parts
    output_gain_grad = lax.dynamic_slice_in_dim(
        pieces[2], lax.axis_index("head") * value_share, value_share, 0
    )
    return (
        block_out,
        input_grad,
        pieces[6],
        unit_sum[:, :split_key].astype(F32),
        unit_sum[:, split_key:].astype(F32),
        value_sum.astype(F32),
        ab_sum[:, :heads],
        ab_sum[:, heads:],
        pieces[3][:heads],
        pieces[4][:heads],
        taps_sum[:, :split_key],
        taps_sum[:, split_key : 2 * split_key],
        taps_sum[:, 2 * split_key :],
        gate_first_sum.astype(F32),
        output_gain_grad,
        out_sum[: heads * value_dim].astype(F32),
        pieces[5],
        gate_sum[:hidden].astype(F32).T,
        up_sum[:hidden].astype(F32).T,
        down_sum[:hidden].astype(F32),
    )


def solution(mesh):
    seq, cols, lines = P(None, "seq", None), P(None, "head"), P("head", None)
    one = P("head")
    placed = (
        seq, P(), P(), cols, cols, cols, cols, cols, one, one, cols, cols, cols, cols, P(), lines, one,
        cols, cols, lines, seq,
    )
    both = P(None, "seq", "head")
    return jax.shard_map(
        per_device,
        mesh=mesh,
        in_specs=placed,
        out_specs=(
            both, both, one, cols, cols, cols, cols, cols, one, one, cols, cols, cols, cols, one, lines,
            one, cols, cols, lines,
        ),
        check_vma=False,
    )
```

```python
import functools
import types

import jax
import jax.numpy as jnp
from jax import lax
from jax.experimental import pallas as pl
from jax.experimental.pallas import tpu as pltpu
from jax.sharding import PartitionSpec as P

NORM_EPSILON = 1e-05
UNIT_EPSILON = 1e-06
RIM = 8
LANES = 128
F32 = jnp.float32
BF16 = jnp.bfloat16
VMEM_LIMIT = 58 * 1024 * 1024

NN = (((1,), (0,)), ((), ()))
NT = (((1,), (1,)), ((), ()))
TN = (((0,), (0,)), ((), ()))


def split(x):
    high = x.astype(BF16)
    return high, (x - high.astype(F32)).astype(BF16)


def raw(a, b, dims):
    return lax.dot_general(a, b, dims, preferred_element_type=F32)


def mm(a, b, dims=NN):
    a_high, a_low = a if isinstance(a, tuple) else (a, None)
    b_high, b_low = b if isinstance(b, tuple) else (b, None)
    total = raw(a_high, b_high, dims)
    if a_low is not None:
        total = total + raw(a_low, b_high, dims)
    if b_low is not None:
        total = total + raw(a_high, b_low, dims)
    return total


def sigmoid(x):
    return 1.0 / (1.0 + jnp.exp(-x))


def softplus(x):
    return jnp.maximum(x, 0.0) + jnp.log1p(jnp.exp(-jnp.abs(x)))


def grid_masks(size):
    row = lax.broadcasted_iota(jnp.int32, (size, size), 0)
    col = lax.broadcasted_iota(jnp.int32, (size, size), 1)
    return row, col


def rough_inverses(blocks):
    size = blocks[0].shape[0]
    row, col = grid_masks(size)
    apart = row ^ col
    base = 8
    starts = [jnp.where(apart < base, block, 0.0) for block in blocks]
    ones = [start.astype(BF16) for start in starts]
    squares = [raw(one, one, NN) for one in ones]
    lows = [square.astype(BF16) for square in squares]
    fourths = [raw(low, low, NN).astype(BF16) for low in lows]
    cubes = [raw(one, low, NN) for one, low in zip(ones, lows)]
    eye = jnp.where(row == col, 1.0, 0.0)
    found = [eye - start + square - cube for start, square, cube in zip(starts, squares, cubes)]
    found = [one + raw(one.astype(BF16), fourth, NN) for one, fourth in zip(found, fourths)]
    while base < size:
        ring = (apart >= base) & (apart < 2 * base)
        offs = [jnp.where(ring, block, 0.0).astype(BF16) for block in blocks]
        lows = [one.astype(BF16) for one in found]
        offs = [raw(low, off, NN).astype(BF16) for low, off in zip(lows, offs)]
        found = [one - raw(off, low, NN) for one, off, low in zip(found, offs, lows)]
        base *= 2
    return found


def unit_inverses(lowers, row, col):
    size = lowers[0].shape[0]
    half = size // 2
    count = len(lowers)
    found = rough_inverses([low[:half, :half] for low in lowers] + [low[half:, half:] for low in lowers])
    corners = [
        raw(second.astype(BF16), low[half:, :half].astype(BF16), NN).astype(BF16)
        for second, low in zip(found[count:], lowers)
    ]
    corners = [-raw(corner, first.astype(BF16), NN) for corner, first in zip(corners, found[:count])]
    zero = jnp.zeros((half, half), F32)
    roughs = [
        jnp.concatenate(
            [jnp.concatenate([first, zero], axis=1), jnp.concatenate([corner, second], axis=1)], axis=0
        )
        for first, corner, second in zip(found[:count], corners, found[count:])
    ]
    parts = [split(rough) for rough in roughs]
    eye = jnp.where(row == col, 1.0, 0.0)
    lefts = [
        (eye - rough - mm(split(low), part)).astype(BF16) for rough, low, part in zip(roughs, lowers, parts)
    ]
    return [rough + raw(part[0], left, NN) for rough, part, left in zip(roughs, parts, lefts)]


def gates_of(ab, rate, bias):
    return -rate * softplus(ab + bias), sigmoid(ab)


def decay_of(log_col, log_row, row, col):
    seen = row >= col
    cum_col = jnp.sum(jnp.where(seen, log_row, 0.0), axis=1, keepdims=True)
    cum_row = jnp.sum(jnp.where(row <= col, log_col, 0.0), axis=0, keepdims=True)
    end = jnp.sum(log_row, axis=1, keepdims=True)
    decayed = jnp.where(seen, jnp.exp(jnp.where(seen, cum_col - cum_row, 0.0)), 0.0)
    return cum_col, cum_row, end, decayed


def convolve(ext, taps_ref, length):
    taps = 4
    total = taps_ref[0:1, :] * ext[pl.ds(RIM - taps + 1, length), :]
    for tap in range(1, taps):
        total = total + taps_ref[tap : tap + 1, :] * ext[pl.ds(RIM - taps + 1 + tap, length), :]
    return total


MESH = pl.DeviceIdType.MESH


def remote(src, dst, send_sem, recv_sem, device):
    return pltpu.make_async_remote_copy(
        src_ref=src, dst_ref=dst, send_sem=send_sem, recv_sem=recv_sem, device_id=device, device_id_type=MESH
    )


def turn_to_row(column, row, col):
    return jnp.sum(jnp.where(row == col, column, 0.0), axis=0, keepdims=True)


def turn_to_column(line, row, col):
    return jnp.sum(jnp.where(row == col, line, 0.0), axis=1, keepdims=True)


def staged_call(kernel, operands, outs, scratch, collective_id, late=(), leaving=(), kept=(), slots=0, flops=10**10):
    dma = pltpu.SemaphoreType.DMA
    order = [i for group in late for i in group]
    vmem, free = pl.BlockSpec(memory_space=pltpu.VMEM), pl.BlockSpec(memory_space=pl.ANY)
    count, total = len(operands), len(operands) + len(outs)
    stages = [pltpu.VMEM(operands[i].shape, operands[i].dtype) for i in order]
    stages += [pltpu.VMEM(outs[i].shape, outs[i].dtype) for i in leaving]
    sems = [dma((max(1, len(order)),)), dma((max(1, len(leaving)), max(1, slots)))]

    def body(*refs):
        ins, results, rest = list(refs[:count]), list(refs[count:total]), refs[total:]
        held, (in_sem, out_sem), rest = rest[: len(stages)], rest[len(stages) : len(stages) + 2], rest[len(stages) + 2 :]
        copies = {}
        for j, i in enumerate(order):
            copies[i] = pltpu.make_async_copy(ins[i], held[j], in_sem.at[j])
            copies[i].start()
            ins[i] = held[j]
        targets = {}
        for j, i in enumerate(leaving):
            targets[i] = (results[i], held[len(order) + j], j)
            results[i] = held[len(order) + j]
        left = {}

        def arrive(group):
            for i in late[group]:
                copies[i].wait()

        def out_copy(i, slot):
            target, source, j = targets[i]
            if slot is None:
                return pltpu.make_async_copy(source, target, out_sem.at[j, 0])
            return pltpu.make_async_copy(source.at[slot], target.at[slot], out_sem.at[j, slot])

        def leave(slot, *indices):
            for i in indices:
                left[i] = slot is not None
                out_copy(i, slot).start()

        kernel(arrive, leave, *ins, *results, *rest)
        for i in leaving:
            for slot in range(slots) if left[i] else (None,):
                out_copy(i, slot).wait()

    late_set = set(order)
    return pl.pallas_call(
        body,
        in_specs=[free if i in late_set else vmem for i in range(count)],
        out_specs=[free if i in leaving or i in kept else vmem for i in range(len(outs))],
        out_shape=tuple(outs),
        scratch_shapes=stages + sems + list(scratch),
        compiler_params=pltpu.CompilerParams(
            collective_id=collective_id, has_side_effects=True, vmem_limit_bytes=VMEM_LIMIT
        ),
        cost_estimate=pl.CostEstimate(flops=flops, bytes_accessed=60 * 10**6, transcendentals=0),
    )(*operands)


class Units:
    def __init__(self, count, pairs):
        self.count, self.pairs, self.share = count, pairs, count // pairs
        self.me, self.other = lax.axis_index("seq"), lax.axis_index("head")

    def ahead(self, place):
        return lax.rem(place - self.me + self.count, self.count) - 1

    def behind(self, place):
        return lax.rem(self.me - place + self.count, self.count) - 1

    def to_owner(self, src, dst, send, recv, unit):
        return remote(src, dst.at[self.me], send.at[self.ahead(unit)], recv.at[self.ahead(unit)], (unit, self.other))

    def at_owner(self, src, dst, send, recv, place):
        return remote(src, dst.at[place], send.at[self.behind(place)], recv.at[self.behind(place)], (place, self.other))

    def pieces(self, value):
        size = value.shape[0] // self.share
        return [value[i * size : (i + 1) * size] for i in range(self.share)]

    def whole(self, ref, pair):
        return jnp.concatenate([ref[pair * self.share + i] for i in range(self.share)], axis=0)

    def greet(self, barrier):
        def one(away, carry):
            pl.semaphore_signal(
                barrier, inc=1, device_id=(lax.rem(self.me + away, self.count), self.other), device_id_type=MESH
            )
            return carry

        lax.fori_loop(1, self.count, one, 0)


def forward_kernel(
    slots, heads, key_dim, value_dim, parts, arrive, leave,
    hidden, input_gain, query_weight, key_weight, value_weight, gate_weight, ab_weight,
    query_kernel, key_kernel, value_kernel, decay_log, decay_bias, gain,
    query_out, key_out, value_out, inverse_out, eff_out, rows_out, mixer_out, gated_out,
    normed, pre, gate, x_out, inv_out, rim, ab, abt, states, maps_in, taps_ref, lanes, cols,
    ext, rim_rows, delta, mix, maps_low, shifts_low, shifts_in, state_send, edge_send, edge_recv,
    map_send, map_recv, shift_send, shift_recv, back_send, back_recv,
):
    length = pre.shape[1]
    units = Units(parts, slots * heads)
    me = units.me
    barrier = pltpu.get_barrier_semaphore()
    units.greet(barrier)
    row, col = grid_masks(length)
    key_start = heads * key_dim
    value_start = 2 * heads * key_dim
    width = hidden.shape[2]
    shard = x_out.shape[2]
    edge = rim_rows.shape[1]
    shard_start = pl.multiple_of(units.other * shard, shard)
    taps = query_kernel.shape[0]
    taps_ref[...] = jnp.zeros_like(taps_ref)
    taps_ref[0:taps, 0:key_start] = query_kernel[...].astype(F32)
    taps_ref[0:taps, key_start:value_start] = key_kernel[...].astype(F32)
    taps_ref[0:taps, value_start:] = value_kernel[...].astype(F32)
    lanes[...] = jnp.zeros_like(lanes)
    lane = lax.broadcasted_iota(jnp.int32, (1, LANES), 1)
    line = lax.broadcasted_iota(jnp.int32, (8, LANES), 0)
    for first, values in ((0, jnp.exp(decay_log[...])), (1, decay_bias[...])):
        by_lane = jnp.zeros((1, LANES), F32)
        by_line = jnp.zeros((8, LANES), F32)
        for h in range(heads):
            by_lane = jnp.where(lane == h, values[0:1, h : h + 1], by_lane)
            by_line = jnp.where(line == h, values[0:1, h : h + 1], by_line)
        lanes[first : first + 1, :] = by_lane
        cols[8 * first : 8 * first + 8, :] = by_line

    def edge_copy():
        return remote(
            hidden.at[:, length - edge : length, :], rim_rows, edge_send.at[0], edge_recv.at[0],
            (lax.rem(me + 1, parts), units.other),
        )

    def norm_rows(x):
        inv = lax.rsqrt(jnp.sum(x * x, axis=1, keepdims=True) / width + NORM_EPSILON)
        return inv, (x * inv * input_gain[0:1, :]).astype(BF16)

    def project(s, carry):
        inv, low = norm_rows(hidden[s].astype(F32))
        normed[s] = low
        x_out[s] = hidden[s, :, pl.ds(shard_start, shard)]
        inv_out[s] = jnp.broadcast_to(inv, (length, LANES))
        pre[s, :, :key_start] = raw(low, query_weight[...], NN).astype(BF16)
        pre[s, :, key_start:value_start] = raw(low, key_weight[...], NN).astype(BF16)
        pre[s, :, value_start:] = raw(low, value_weight[...], NN).astype(BF16)
        gates = raw(low, ab_weight[...], NT)
        ab[s] = gates
        abt[s] = jnp.transpose(gates)[0:8, :]
        leave(s, 8, 9, 11, 12)

        @pl.when(s == 0)
        def _():
            pl.semaphore_wait(barrier, parts - 1)
            edge_copy().start()

        return carry

    lax.fori_loop(0, slots, project, 0)
    edge_copy().wait_recv()
    _, edge_low = norm_rows(rim_rows[...].reshape(slots * edge, width).astype(F32))
    edge_pre = jnp.concatenate(
        [raw(edge_low, weight[...], NN) for weight in (query_weight, key_weight, value_weight)], axis=1
    ).astype(BF16).astype(F32)
    for s in range(slots):
        rim[s] = jnp.where(me > 0, edge_pre[(s + 1) * edge - RIM : (s + 1) * edge, :], 0.0)

    def map_copy(unit):
        return units.to_owner(maps_low.at[unit // units.share], maps_in, map_send, map_recv, unit)

    def shift_copy(unit):
        return units.to_owner(shifts_low.at[unit], shifts_in, shift_send, shift_recv, unit)

    def back_copy(place):
        ahead = units.ahead(place)
        return remote(
            state_send.at[place], states.at[me], back_send.at[ahead], back_recv.at[ahead], (place, units.other)
        )

    def back_arrival(unit):
        behind = units.behind(unit)
        return remote(
            state_send.at[unit], states.at[unit], back_send.at[behind], back_recv.at[behind], (unit, units.other)
        )

    together = 2 if slots % 2 == 0 else 1

    def group_terms(group, carry):
        pairs = []
        for i in range(together):
            s = group * together + i
            ext[i, 0:RIM, :] = rim[s]
            ext[i, RIM : RIM + length, :] = pre[s].astype(F32)
            conv = convolve(ext.at[i], taps_ref, length)
            active = conv * sigmoid(conv)
            log_cols, strength_cols = gates_of(ab[s], lanes[0:1, :], lanes[1:2, :])
            log_rows, strength_rows = gates_of(abt[s], cols[0:8, 0:1], cols[8:16, 0:1])
            for h in range(heads):
                query_act = active[:, h * key_dim : (h + 1) * key_dim]
                key_act = active[:, key_start + h * key_dim : key_start + (h + 1) * key_dim]
                value_act = active[:, value_start + h * value_dim : value_start + (h + 1) * value_dim]
                query_scale = lax.rsqrt(jnp.sum(query_act * query_act, axis=1, keepdims=True) + UNIT_EPSILON)
                key_scale = lax.rsqrt(jnp.sum(key_act * key_act, axis=1, keepdims=True) + UNIT_EPSILON)
                query = (query_act * query_scale * key_dim ** (-0.5)).astype(BF16)
                key = (key_act * key_scale).astype(BF16)
                value = value_act.astype(BF16)
                query_out[s, h] = query
                key_out[s, h] = key
                value_out[s, h] = value
                cum_col, cum_row, end, decayed = decay_of(
                    log_cols[:, h : h + 1], log_rows[h : h + 1, :], row, col
                )
                pairs.append(
                    types.SimpleNamespace(
                        s=s, h=h, query=query, key=key, value=value, cum_col=cum_col, cum_row=cum_row, end=end,
                        decayed=decayed, strength=strength_cols[:, heads + h : heads + h + 1],
                        strength_row=strength_rows[heads + h : heads + h + 1, :],
                    )
                )
        lowers = [
            jnp.where(row > col, pair.strength * pair.decayed * mm(pair.key, pair.key, NT), 0.0) for pair in pairs
        ]
        for pair, inverse in zip(pairs, unit_inverses(lowers, row, col)):
            inverse_out[pair.s, pair.h] = inverse
            pair.scaled = inverse * pair.strength_row
        for pair in pairs:
            pair.delta = mm(split(pair.scaled), pair.value)
            pair.mix = mm(split(pair.scaled * jnp.exp(pair.cum_row)), pair.key)
            delta[pair.s, pair.h] = pair.delta
            mix[pair.s, pair.h] = pair.mix
        small_row, small_col = grid_masks(key_dim)
        for pair in pairs:
            end_weight = jnp.exp(pair.end - pair.cum_col)
            moved = jnp.where(small_row == small_col, jnp.exp(pair.end), 0.0)
            place = pair.s * heads + pair.h
            maps_low[place] = (moved - mm(split(pair.mix * end_weight), pair.key, TN)).astype(BF16)
            for i, piece in enumerate(units.pieces(mm(split(pair.delta * end_weight), pair.key, TN).astype(BF16))):
                shifts_low[place * units.share + i] = piece
        for i in range(together):
            leave(group * together + i, 0, 1, 2, 3)
        for i in range(together * heads * units.share):
            unit = group * together * heads * units.share + i

            @pl.when(unit != me)
            def _(unit=unit):
                map_copy(unit).start()
                shift_copy(unit).start()

            @pl.when(unit == me)
            def _(unit=unit):
                maps_in[unit] = maps_low[unit // units.share]
                shifts_in[unit] = shifts_low[unit]

        return carry

    lax.fori_loop(0, slots // together, group_terms, 0)

    def within(s):
        gate[s] = raw(normed[s], gate_weight[...], NN)
        log_cols, _ = gates_of(ab[s], lanes[0:1, :], lanes[1:2, :])
        log_rows, _ = gates_of(abt[s], cols[0:8, 0:1], cols[8:16, 0:1])
        for h in range(heads):
            query = query_out[s, h]
            cum_col, _, _, decayed = decay_of(log_cols[:, h : h + 1], log_rows[h : h + 1, :], row, col)
            scores = split(decayed * mm(query, key_out[s, h], NT))
            eff_out[s, h] = jnp.exp(cum_col) * query.astype(F32) - mm(scores, split(mix[s, h]))
            mixer_out[s, h] = mm(scores, split(delta[s, h]))
        leave(s, 4, 10)

    def within_group(group, carry):
        for i in range(together):
            within(group * together + i)
        return carry

    early = slots // together // 2
    lax.fori_loop(0, early, within_group, 0)

    def scan(place, state):
        low = state.astype(BF16)

        @pl.when(place != me)
        def _():
            state_send[place] = low
            back_copy(place).start()
            units.at_owner(maps_low.at[0], maps_in, map_send, map_recv, place).wait_recv()
            units.at_owner(shifts_low.at[0], shifts_in, shift_send, shift_recv, place).wait_recv()

        @pl.when(place == me)
        def _():
            states[place] = low

        return mm(split(state), maps_in[place]) + shifts_in[place].astype(F32)

    lax.fori_loop(0, parts, scan, jnp.zeros((value_dim // units.share, key_dim), F32))

    lax.fori_loop(early, slots // together, within_group, 0)

    def emit(s, carry):
        for i in range(heads * units.share):
            unit = s * heads * units.share + i

            @pl.when(unit != me)
            def _(unit=unit):
                back_arrival(unit).wait_recv()

        for h in range(heads):
            state = units.whole(states, s * heads + h)
            rows_out[s, h] = delta[s, h] - mm(split(mix[s, h]), state, NT)
            mixer = mixer_out[s, h] + mm(split(eff_out[s, h]), state, NT)
            mixer_out[s, h] = mixer
            scale = lax.rsqrt(jnp.sum(mixer * mixer, axis=1, keepdims=True) / value_dim + NORM_EPSILON)
            here = slice(h * value_dim, (h + 1) * value_dim)
            gate_h = gate[s, :, here]
            gated_out[s, :, here] = (mixer * scale * gain[0:1, :] * (gate_h * sigmoid(gate_h))).astype(BF16)
        leave(s, 5, 6, 7)
        return carry

    lax.fori_loop(0, slots, emit, 0)

    def drain(away, carry):
        unit = lax.rem(me + away, parts)
        map_copy(unit).wait_send()
        shift_copy(unit).wait_send()
        back_copy(unit).wait_send()
        return carry

    lax.fori_loop(1, parts, drain, 0)
    edge_copy().wait_send()


def forward_call(parts, head_parts, heads, *operands):
    hidden, query_weight, value_weight, gate_weight = operands[0], operands[2], operands[4], operands[5]
    slots, length, width = hidden.shape
    key_dim, value_dim = query_weight.shape[1] // heads, value_weight.shape[1] // heads
    channels = heads * (2 * key_dim + value_dim)
    share = parts // (slots * heads)
    sds = jax.ShapeDtypeStruct
    dma = pltpu.SemaphoreType.DMA
    per = lambda kind, *tail: sds((slots, heads) + tail, kind)
    each = lambda kind, *tail: sds((slots,) + tail, kind)
    unit = (parts, value_dim // share, key_dim)
    outs = (
        per(BF16, length, key_dim), per(BF16, length, key_dim), per(BF16, length, value_dim),
        per(F32, length, length), per(F32, length, key_dim), per(F32, length, value_dim),
        per(F32, length, value_dim), each(BF16, length, heads * value_dim),
        each(BF16, length, width), each(BF16, length, channels), each(F32, length, heads * value_dim),
        each(BF16, length, width // head_parts), each(F32, length, LANES), each(F32, RIM, channels),
        each(F32, length, LANES), each(F32, 8, length),
        sds(unit, BF16), sds((parts, key_dim, key_dim), BF16), sds((8, channels), F32), sds((8, LANES), F32),
        sds((16, LANES), F32),
    )
    scratch = [
        pltpu.VMEM((2, length + RIM, channels), F32),
        pltpu.VMEM((slots, 2 * RIM, width), BF16),
        pltpu.VMEM((slots, heads, length, value_dim), F32),
        pltpu.VMEM((slots, heads, length, key_dim), F32),
        pltpu.VMEM((slots * heads, key_dim, key_dim), BF16),
        pltpu.VMEM(unit, BF16), pltpu.VMEM(unit, BF16), pltpu.VMEM(unit, BF16), dma((1,)), dma((1,)),
    ] + [dma((parts - 1,))] * 6
    return staged_call(
        functools.partial(forward_kernel, slots, heads, key_dim, value_dim, parts),
        operands, outs, scratch, 2, leaving=tuple(range(13)), slots=slots,
    )


def head_scratch(kinds, stats, slots, head_parts, length, shard):
    lines = head_parts // 2
    dma = pltpu.SemaphoreType.DMA
    return [
        pltpu.VMEM((min(kinds, 2), slots, lines, length, shard), F32),
        pltpu.VMEM((kinds, slots, lines, length, shard), BF16),
        pltpu.VMEM((kinds, slots, lines, length, shard), BF16),
        pltpu.VMEM((min(kinds, 2), slots, lines - 1, length, shard), BF16),
        pltpu.VMEM((min(kinds, 2), slots, lines - 1, length, shard), BF16),
        pltpu.VMEM((stats, slots, 8, length), F32),
        pltpu.VMEM((stats, slots, head_parts - 1, 8, length), F32),
        dma((kinds, slots)), dma((kinds, slots)),
        dma((kinds, slots, lines - 1)), dma((kinds, slots, lines - 1)),
        dma((stats, slots, head_parts - 1)), dma((stats, slots, head_parts - 1)),
    ]


def head_tools(head_parts, refs, stats):
    part, low, from_core, to_line, from_line, stat_own, stat_in = refs[:7]
    core_send, core_recv, line_send, line_recv, stat_send, stat_recv = refs[7:]
    me = lax.axis_index("head")
    place = lax.axis_index("seq")
    lines = head_parts // 2
    core = lax.rem(me, 2)
    line = me // 2
    sibling = 2 * line + (1 - core)
    length, shard = part.shape[3:]
    row, col = grid_masks(length)

    def greet(barrier):
        for away in range(1, head_parts):
            pl.semaphore_signal(
                barrier, inc=1, device_id=(place, lax.rem(me + away, head_parts)), device_id_type=MESH
            )

    def core_copy(kind, s):
        return remote(
            low.at[kind, s], from_core.at[kind, s], core_send.at[kind, s], core_recv.at[kind, s], (place, sibling)
        )

    def line_copy(kind, s, away):
        return remote(
            to_line.at[kind, s, away - 1], from_line.at[kind, s, away - 1],
            line_send.at[kind, s, away - 1], line_recv.at[kind, s, away - 1],
            (place, 2 * lax.rem(line + away, lines) + core),
        )

    def stat_copy(kind, s, away):
        return remote(
            stat_own.at[kind, s], stat_in.at[kind, s, away - 1],
            stat_send.at[kind, s, away - 1], stat_recv.at[kind, s, away - 1],
            (place, lax.rem(me + away, head_parts)),
        )

    def send_part(kind, s, value):
        for y in range(lines):
            even = value[:, 2 * y * shard : (2 * y + 1) * shard]
            odd = value[:, (2 * y + 1) * shard : (2 * y + 2) * shard]
            low[kind, s, y] = jnp.where(core == 0, odd, even).astype(BF16)
            part[kind % 2, s, y] = jnp.where(core == 0, even, odd)
        core_copy(kind, s).start()

    def join_core(kind, s):
        core_copy(kind, s).wait_recv()
        for away in range(1, lines):
            y = lax.rem(line + away, lines)
            joined = part[kind % 2, s, y] + from_core[kind, s, y].astype(F32)
            to_line[kind, s, away - 1] = joined.astype(BF16)
            line_copy(kind, s, away).start()
        part[kind % 2, s, line] = part[kind % 2, s, line] + from_core[kind, s, line].astype(F32)

    def joined_core(kind, s):
        core_copy(kind, s).wait_recv()
        others = [lax.rem(line + away, lines) for away in range(1, lines)]
        joined = [part[kind % 2, s, y] + from_core[kind, s, y].astype(F32) for y in [line] + others]
        return joined[0], joined[1:]

    def join_line(kind, s):
        total = part[kind % 2, s, line]
        for away in range(1, lines):
            line_copy(kind, s, away).wait_recv()
            total = total + from_line[kind, s, away - 1].astype(F32)
        return total

    def send_stat(kind, s, column):
        stat_own[kind, s] = jnp.broadcast_to(turn_to_row(column, row, col), (8, length))
        for away in range(1, head_parts):
            stat_copy(kind, s, away).start()

    def join_stat(kind, s):
        total = stat_own[kind, s]
        for away in range(1, head_parts):
            stat_copy(kind, s, away).wait_recv()
            total = total + stat_in[kind, s, away - 1]
        return turn_to_column(total[0:1, :], row, col)

    def drain(s):
        for kind in range(low.shape[0]):
            core_copy(kind, s).wait_send()
        for kind in range(to_line.shape[0]):
            for away in range(1, lines):
                line_copy(kind, s, away).wait_send()
        for kind in range(stats):
            for away in range(1, head_parts):
                stat_copy(kind, s, away).wait_send()

    return types.SimpleNamespace(
        me=me, place=place, lines=lines, core=core, line=line, sibling=sibling, greet=greet,
        send_part=send_part, join_core=join_core, join_line=join_line, send_stat=send_stat,
        join_stat=join_stat, drain=drain, joined_core=joined_core,
    )


def weight_rows(left, right, store):
    wide = left.shape[2]
    step = min(wide, 256)
    steps = wide // step

    def one(j, carry):
        start = pl.multiple_of(j * step, step)
        block = left[:, :, pl.ds(start, step)]
        store(start, step, raw(block.reshape(-1, step), right, TN).astype(BF16))
        return carry

    lax.fori_loop(0, steps, one, 0)
    if wide % step:
        rest = wide % step
        block = left[:, :, steps * step :]
        store(steps * step, rest, raw(block.reshape(-1, rest), right, TN).astype(BF16))


def middle_kernel(
    slots, head_parts, parts, heads, arrive, leave,
    gated, x_shard, cotangent, lengths, out_weight, gate_weight, up_weight,
    down_weight, gain, mixer, gate, gain_row, eff,
    block_base, gate_part, residual_grad_out, mixer_rows_grad, mixer_grad, gate_grad_out,
    gain_grad_out, output_gain_grad, shifts_in, down_part, up_part, block_line,
    residual, act_all, up_grad_all, gate_grad_all,
    inverse, spread, shifts_low, shift_send, shift_recv,
    spread_line_send, spread_line_recv, spread_core_send, spread_core_recv,
    *refs,
):
    tools = head_tools(head_parts, refs, 2)
    me, place, lines, core, line, sibling = (
        tools.me, tools.place, tools.lines, tools.core, tools.line, tools.sibling
    )
    send_part, join_core, join_line = tools.send_part, tools.join_core, tools.join_line
    send_stat, join_stat = tools.send_stat, tools.join_stat
    length, shard = x_shard.shape[1], x_shard.shape[2]
    width = shard * head_parts
    hidden = gate_weight.shape[0]
    value_dim = mixer.shape[3]
    units = Units(parts, slots * heads)

    barrier = pltpu.get_barrier_semaphore()
    tools.greet(barrier)
    units.greet(barrier)
    gain_grad_out[...] = jnp.zeros_like(gain_grad_out)
    output_gain_grad[...] = jnp.zeros_like(output_gain_grad)
    pl.semaphore_wait(barrier, head_parts - 1 + parts - 1)

    place_row = lax.broadcasted_iota(jnp.int32, (length, LANES), 0) + place * length

    def valid_rows(s):
        count = jnp.zeros((1, 1), jnp.int32)
        for j in range(slots):
            count = jnp.where(s == j, lengths[0:1, j : j + 1], count)
        return jnp.where(place_row < count, 1.0, 0.0)[:, 0:1]

    def shift_copy(unit):
        return units.to_owner(shifts_low.at[unit], shifts_in, shift_send, shift_recv, unit)

    def spread_line_copy(kind, s, away):
        return remote(
            spread.at[kind, s, me], spread.at[kind, s, me],
            spread_line_send.at[kind, s, away - 1], spread_line_recv.at[kind, s, away - 1],
            (place, 2 * lax.rem(line + away, lines) + core),
        )

    def spread_core_copy(kind, s, away):
        y = lax.rem(line + away, lines)
        return remote(
            spread.at[kind, s, 2 * y + core], spread.at[kind, s, 2 * y + core],
            spread_core_send.at[kind, s, away], spread_core_recv.at[kind, s, away], (place, sibling),
        )

    def spread_core_arrival(kind, s, away):
        y = lax.rem(line + away, lines)
        return remote(
            spread.at[kind, s, 2 * y + (1 - core)], spread.at[kind, s, 2 * y + (1 - core)],
            spread_core_send.at[kind, s, away], spread_core_recv.at[kind, s, away], (place, sibling),
        )

    def spread_line_arrival(kind, s, away):
        y = lax.rem(line + lines - away, lines)
        return remote(
            spread.at[kind, s, 2 * y + core], spread.at[kind, s, 2 * y + core],
            spread_line_send.at[kind, s, away - 1], spread_line_recv.at[kind, s, away - 1],
            (place, 2 * y + core),
        )

    def send_spread(kind, s, value):
        spread[kind, s, me] = value
        for away in range(1, lines):
            spread_line_copy(kind, s, away).start()
        spread_core_copy(kind, s, 0).start()

    def pass_spread(kind, s):
        for away in range(1, lines):
            spread_line_arrival(kind, s, lines - away).wait_recv()
            spread_core_copy(kind, s, away).start()

    def take_spread(kind, s):
        for away in range(lines):
            spread_core_arrival(kind, s, away).wait_recv()
        return jnp.concatenate([spread[kind, s, j] for j in range(head_parts)], axis=1)

    def attention(s):
        send_part(0, s, raw(gated[s], out_weight[...], NN))

    def rows_in(s):
        total = x_shard[s].astype(F32) + valid_rows(s) * join_line(0, s)
        residual[s] = total
        send_stat(0, s, jnp.sum(total * total, axis=1, keepdims=True))

    def norm_second(s):
        inv = lax.rsqrt(join_stat(0, s) / width + NORM_EPSILON)
        inverse[s] = jnp.broadcast_to(inv, (length, LANES))
        send_spread(0, s, (residual[s] * inv * gain[0:1, :]).astype(BF16))

    def swiglu(s):
        normed = take_spread(0, s)
        valid = valid_rows(s)
        gate_values = raw(normed, gate_weight[...], NT)
        up_values = raw(normed, up_weight[...], NT)
        act_grad = raw(cotangent[s], down_weight[...], NT) * valid
        sig = sigmoid(gate_values)
        silu = gate_values * sig
        act_all[s] = (silu * up_values * valid).astype(BF16)
        up_grad = (act_grad * silu).astype(BF16)
        gate_grad = (act_grad * up_values * sig * (1.0 + gate_values * (1.0 - sig))).astype(BF16)
        up_grad_all[s] = up_grad
        gate_grad_all[s] = gate_grad
        send_part(1, s, raw(up_grad, up_weight[...], NN) + raw(gate_grad, gate_weight[...], NN))

    def swiglu_out(s):
        send_part(2, s, raw(act_all[s], down_weight[...], NN))

    def block_rows(s):
        valid = valid_rows(s)
        own, others = tools.joined_core(2, s)
        block_base[s] = residual[s] + valid * own
        for i, other in enumerate(others):
            block_line[s, i] = (valid * other).astype(BF16)
        leave(s, 0, 11)

    def norm_back(s):
        grad = join_line(1, s)
        inv = inverse[s][:, 0:1]
        gain_grad_out[0:1, :] += jnp.sum(grad * residual[s] * inv, axis=0, keepdims=True)
        weighted = grad * gain[0:1, :]
        residual_grad_out[s] = weighted
        send_stat(1, s, jnp.sum(weighted * residual[s], axis=1, keepdims=True))

    def residual_back(s):
        stat = join_stat(1, s) / width
        inv = inverse[s][:, 0:1]
        cot = cotangent[s, :, pl.ds(pl.multiple_of(me * shard, shard), shard)].astype(F32)
        grad = cot + inv * (residual_grad_out[s] - residual[s] * (inv * inv * stat))
        residual_grad_out[s] = grad
        leave(s, 2)
        send_spread(1, s, (valid_rows(s) * grad).astype(BF16))

    def gate_back(s, gated_grad):
        out_gain = gain_row[0:1, :]
        for h in range(heads):
            here = slice(h * value_dim, (h + 1) * value_dim)
            grad = gated_grad[:, here]
            mixer_h = mixer[s, h]
            gate_h = gate[s, :, here]
            scale = lax.rsqrt(jnp.sum(mixer_h * mixer_h, axis=1, keepdims=True) / value_dim + NORM_EPSILON)
            sig = sigmoid(gate_h)
            unit_rows = mixer_h * scale
            gate_grad_out[s, :, here] = (
                grad * unit_rows * out_gain * (sig * (1.0 + gate_h * (1.0 - sig)))
            ).astype(BF16)
            scaled_grad = grad * (gate_h * sig)
            output_gain_grad[0:1, :] += jnp.sum(scaled_grad * unit_rows, axis=0, keepdims=True)
            unit_grad = scaled_grad * out_gain
            stat = jnp.sum(unit_grad * mixer_h, axis=1, keepdims=True) / value_dim
            mixer_grad_h = scale * (unit_grad - mixer_h * (scale * scale * stat))
            mixer_grad[s, h] = mixer_grad_h
            entering = mm(split(mixer_grad_h), split(eff[s, h]), TN).astype(BF16)
            for i, piece in enumerate(units.pieces(entering)):
                shifts_low[(s * heads + h) * units.share + i] = piece

        for i in range(heads * units.share):
            unit = s * heads * units.share + i

            @pl.when(unit != units.me)
            def _(unit=unit):
                shift_copy(unit).start()

            @pl.when(unit == units.me)
            def _(unit=unit):
                shifts_in[unit] = shifts_low[unit]

    def mixer_rows(s):
        grad = take_spread(1, s)
        mixer_rows_grad[s] = grad
        gate_back(s, raw(grad, out_weight[...], NT))
        leave(s, 3, 4, 5)

    stages = (
        (7, functools.partial(pass_spread, 1)),
        (6, residual_back),
        (5, norm_back),
        (4, functools.partial(join_core, 1)),
        (3, functools.partial(pass_spread, 0)),
        (2, norm_second),
        (1, rows_in),
        (0, attention),
        (7, block_rows),
        (0, functools.partial(join_core, 0)),
        (7, mixer_rows),
        (3, swiglu),
        (6, swiglu_out),
    )

    def step(t, carry):
        @pl.when(t == 3)
        def _():
            arrive(0)

        @pl.when(t == 7)
        def _():
            arrive(1)

        for offset, stage in stages:
            s = t - offset

            @pl.when((s >= 0) & (s < slots))
            def _(stage=stage, s=s):
                stage(s)

        def normed_rows():
            return jnp.concatenate(
                [spread[0, :, j].reshape(slots * length, shard) for j in range(head_parts)], axis=1
            )

        def cotangent_rows():
            return cotangent[...].reshape(-1, width)

        for late, left, right, target, index in (
            (3, act_all, cotangent_rows, down_part, 9),
            (4, up_grad_all, normed_rows, up_part, 10),
            (5, gate_grad_all, normed_rows, gate_part, 1),
        ):

            @pl.when(t == slots + late)
            def _(left=left, right=right, target=target, index=index):
                def store(start, size, block):
                    target[pl.ds(start, size), :] = block

                weight_rows(left, right(), store)
                if target.shape[0] > hidden:
                    target[hidden:, :] = jnp.zeros((target.shape[0] - hidden, width), BF16)
                leave(None, index)

        return carry

    lax.fori_loop(0, slots + 7, step, 0)

    def drain(s, carry):
        tools.drain(s)
        for kind in range(2):
            for away in range(1, lines):
                spread_line_copy(kind, s, away).wait_send()
            for away in range(lines):
                spread_core_copy(kind, s, away).wait_send()
        return carry

    lax.fori_loop(0, slots, drain, 0)

    def take_units(away, carry):
        unit = lax.rem(units.me + away, parts)
        units.at_owner(shifts_low.at[0], shifts_in, shift_send, shift_recv, unit).wait_recv()
        return carry

    lax.fori_loop(1, parts, take_units, 0)

    def drain_units(away, carry):
        shift_copy(lax.rem(units.me + away, parts)).wait_send()
        return carry

    lax.fori_loop(1, parts, drain_units, 0)


def by_columns(rows, wide, parts):
    return rows % 32 == 0 and wide % (LANES * parts) == 0


def padded_rows(count, wide, parts):
    return count if by_columns(count, wide, parts) else count + -count % (32 * parts)


def middle_call(parts, head_parts, heads, *operands):
    gated, x_shard, gate_weight, mixer, eff = (operands[i] for i in (0, 1, 5, 9, 12))
    slots, length, shard = x_shard.shape
    width = shard * head_parts
    hidden = gate_weight.shape[0]
    lines = head_parts // 2
    value_dim, key_dim = mixer.shape[3], eff.shape[3]
    unit = (parts, value_dim * slots * heads // parts, key_dim)
    sds = jax.ShapeDtypeStruct
    dma = pltpu.SemaphoreType.DMA
    product = sds((padded_rows(hidden, width, parts), width), BF16)
    rows = sds((slots, length, shard), F32)
    outs = (
        rows, product, rows,
        sds((slots, length, width), BF16), sds(mixer.shape, F32),
        sds(gated.shape, BF16), sds((8, shard), F32), sds((8, value_dim), F32), sds(unit, BF16), product, product,
        sds((slots, lines - 1, length, shard), BF16),
    )
    scratch = (
        [
            pltpu.VMEM(rows.shape, F32),
            pltpu.VMEM((slots, length, hidden), BF16),
            pltpu.VMEM((slots, length, hidden), BF16),
            pltpu.VMEM((slots, length, hidden), BF16),
            pltpu.VMEM((slots, length, LANES), F32),
            pltpu.VMEM((2, slots, head_parts, length, shard), BF16),
            pltpu.VMEM(unit, BF16), dma((parts - 1,)), dma((parts - 1,)),
            dma((2, slots, lines - 1)), dma((2, slots, lines - 1)),
            dma((2, slots, lines)), dma((2, slots, lines)),
        ]
        + head_scratch(3, 2, slots, head_parts, length, shard)
    )
    return staged_call(
        functools.partial(middle_kernel, slots, head_parts, parts, heads),
        operands, outs, scratch, 0, late=((5, 6, 7, 2), (9, 10, 12)), leaving=(0, 1, 2, 3, 4, 5, 9, 10, 11),
        slots=slots,
    )


def ring_scratch(parts, shapes):
    dma = pltpu.SemaphoreType.DMA
    count = len(shapes)
    blocks = [
        (rows // 2, wide // parts) if by_columns(rows, wide, parts) else (rows // (2 * parts), wide)
        for rows, wide in shapes
    ]
    return [pltpu.VMEM((2, parts) + block, BF16) for block in blocks] + [dma((count, 2)), dma((count, 2, parts - 1)), dma((count, 2)), dma((count, 2, parts - 1)), dma((count, 2))]


def ring_tools(parts, ins, outs, held, send, recv, spread_send, spread_recv, own):
    count = len(ins)
    index = lax.axis_index("seq")
    other = lax.axis_index("head")
    side = lax.rem(index, 2)
    level = index // 2
    levels = parts // 2
    position = jnp.where(side == 1, level, parts - 1 - level)
    up = jnp.where(side == 1, jnp.where(level == levels - 1, index - 1, index + 2),
                   jnp.where(level == 0, index + 1, index - 2))
    down = jnp.where(side == 1, jnp.where(level == 0, index - 1, index - 2),
                     jnp.where(level == levels - 1, index + 1, index + 2))
    targets = (up, down)
    def greet(barrier):
        for target in targets:
            pl.semaphore_signal(barrier, inc=1, device_id=(target, other), device_id_type=MESH)

    def block_of(a, way, chunk):
        rows, wide = ins[a].shape
        if by_columns(rows, wide, parts):
            half, step = rows // 2, wide // parts
            return pl.ds(way * half, half), pl.ds(pl.multiple_of(chunk * step, step), step)
        size = rows // (2 * parts)
        return pl.ds(pl.multiple_of((chunk * 2 + way) * size, size), size), pl.ds(0, wide)

    def chunk_at(way, step):
        if way == 0:
            return lax.rem(position - step + 2 * parts, parts)
        return lax.rem(position + step + 2 * parts, parts)

    def sum_copy(a, way, step):
        return remote(
            held[a].at[way, step], held[a].at[way, step + 1], send.at[a, way], recv.at[a, way, step],
            (targets[way], other),
        )

    def spread_copy(a, way, step):
        block = block_of(a, way, chunk_at(way, step - 1))
        return remote(
            outs[a].at[block], outs[a].at[block], spread_send.at[a, way], spread_recv.at[a, way, step],
            (targets[way], other),
        )

    def spread_first(a, way):
        block = block_of(a, way, chunk_at(way, parts - 1))
        return remote(
            held[a].at[way, parts - 1], outs[a].at[block], spread_send.at[a, way],
            spread_recv.at[a, way, 0], (targets[way], other),
        )

    def own_copy(a, way):
        block = block_of(a, way, chunk_at(way, parts - 1))
        return pltpu.make_async_copy(held[a].at[way, parts - 1], outs[a].at[block], own.at[a, way])

    def spread_arrival(a, way, step):
        block = block_of(a, way, chunk_at(way, step))
        return remote(
            outs[a].at[block], outs[a].at[block], spread_send.at[a, way], spread_recv.at[a, way, step],
            (targets[way], other),
        )

    lanes = [(a, way) for a in range(count) for way in range(2)]
    last = parts - 2

    def add(step, a, way):
        sum_copy(a, way, step).wait_recv()
        mine = ins[a][block_of(a, way, chunk_at(way, step + 1))].astype(F32)
        return (held[a][way, step + 1].astype(F32) + mine).astype(BF16)

    def begin():
        for a, way in lanes:
            held[a][way, 0] = ins[a][block_of(a, way, chunk_at(way, 0))]
            sum_copy(a, way, 0).start()

    def one(step):
        for a, way in lanes:
            held[a][way, step + 1] = add(step, a, way)
            sum_copy(a, way, step).wait_send()
            sum_copy(a, way, step + 1).start()

    def turn():
        for a, way in lanes:
            held[a][way, parts - 1] = add(last, a, way)
            sum_copy(a, way, last).wait_send()
            spread_first(a, way).start()
            own_copy(a, way).start()

    def pass_first():
        for a, way in lanes:
            spread_arrival(a, way, 0).wait_recv()
            spread_first(a, way).wait_send()
            spread_copy(a, way, 1).start()

    def pass_on(step):
        for a, way in lanes:
            spread_arrival(a, way, step).wait_recv()
            spread_copy(a, way, step).wait_send()
            spread_copy(a, way, step + 1).start()

    def finish():
        for a, way in lanes:
            spread_arrival(a, way, last).wait_recv()
            spread_copy(a, way, last).wait_send()
            own_copy(a, way).wait()

    def tick(k):
        @pl.when(k < last)
        def _():
            one(k)

        @pl.when(k == last)
        def _():
            turn()

        @pl.when(k == last + 1)
        def _():
            pass_first()

        @pl.when(k > last + 1)
        def _():
            pass_on(k - last - 1)

    return types.SimpleNamespace(
        greet=greet, begin=begin, tick=tick, finish=finish, ticks=2 * parts - 3, up=up, down=down
    )


def backward_kernel(
    slots, heads, key_dim, value_dim, parts, head_parts, arrive, leave,
    mixer_grad, shifts_in, gated, mixer_rows_grad, normed, gate_grad,
    pre, rim, ab, abt, taps_ref, lanes, cols,
    queries, keys, value_rows, inverse_all, delta_rows, states, maps_in, gate_part,
    query_weight, key_weight, value_weight, gate_weight, ab_weight, x_shard, inv_first, residual_grad, input_gain,
    gain_part, mixed_part, up_part, down_part, block_base, block_line,
    input_grad_out, small_sum, gate_sum, out_sum, first_sum, unit_sum, value_sum, up_sum, down_sum, block_out,
    ab_grad_out, taps_grad_out, lane_grad_out, out_part, first_part,
    ext, conv_grad, tail, rim_own, rim_in, leavings, leaving_send,
    small_lines, small_own, small_in, gain_own, gain_in, block_in, block_send, block_recv,
    back_send, back_recv, rim_send, rim_recv, small_send, small_recv, gain_send, gain_recv, *refs,
):
    length = pre.shape[1]
    taps = 4
    width = normed.shape[2]
    values = gated.shape[2]
    units = Units(parts, slots * heads)
    me = units.me
    tools = head_tools(head_parts, refs[27:], 1)
    place, head = me, units.other
    pre_grad_out = pre
    shard = x_shard.shape[2]
    channels = pre.shape[2]
    unit_wide = 2 * heads * key_dim
    unit_own = mixer_rows_grad.at[:, 0:unit_wide]
    value_own = mixer_rows_grad.at[:, unit_wide:channels]
    rings = (
        ring_tools(parts, (gate_part, up_part), (gate_sum, up_sum), refs[0:2], *refs[2:7]),
        ring_tools(
            parts, (down_part, out_part, first_part), (down_sum, out_sum, first_sum), refs[7:10], *refs[10:15]
        ),
        ring_tools(parts, (unit_own,), (unit_sum,), refs[15:16], *refs[16:21]),
        ring_tools(parts, (value_own,), (value_sum,), refs[21:22], *refs[22:27]),
    )
    barrier = pltpu.get_barrier_semaphore()
    units.greet(barrier)
    tools.greet(barrier)
    row, col = grid_masks(length)
    taps_grad_out[...] = jnp.zeros_like(taps_grad_out)
    lane_grad_out[...] = jnp.zeros_like(lane_grad_out)
    pl.semaphore_wait(barrier, parts - 1 + head_parts - 1)
    rings[0].begin()

    def back_copy(place):
        ahead = units.ahead(place)
        return remote(
            leaving_send.at[place], leavings.at[me], back_send.at[ahead], back_recv.at[ahead],
            (place, units.other),
        )

    def back_arrival(unit):
        behind = units.behind(unit)
        return remote(
            leaving_send.at[unit], leavings.at[unit], back_send.at[behind], back_recv.at[behind],
            (unit, units.other),
        )

    def rim_copy():
        return remote(
            rim_own, rim_in, rim_send.at[0], rim_recv.at[0], (lax.rem(me + parts - 1, parts), units.other)
        )

    def scan(hop, leaving):
        place = parts - 1 - hop
        low = leaving.astype(BF16)

        @pl.when(place != me)
        def _():
            leaving_send[place] = low
            back_copy(place).start()

        @pl.when(place == me)
        def _():
            leavings[place] = low

        return mm(split(leaving), maps_in[place], NT) + shifts_in[place].astype(F32)

    lax.fori_loop(0, parts, scan, jnp.zeros((value_dim // units.share, key_dim), F32))
    arrive(0)

    def store_out(start, size, block):
        out_part[pl.ds(start, size), :] = block

    def store_first(start, size, block):
        first_part[pl.ds(start, size), :] = block

    weight_rows(gated, mixer_rows_grad[...], store_out)
    weight_rows(normed, gate_grad[...].reshape(-1, values), store_first)
    rings[1].begin()
    arrive(1)

    def block_copy(s, away):
        target = 2 * lax.rem(tools.line + away, tools.lines) + tools.core
        return remote(
            block_line.at[s, away - 1], block_in.at[s, away - 1], block_send.at[s, away - 1],
            block_recv.at[s, away - 1], (place, target),
        )

    for s in range(slots):
        for away in range(1, tools.lines):
            block_copy(s, away).start()
    rings[0].tick(0)

    def delta_slot(s, carry):
        for i in range(heads * units.share):
            unit = s * heads * units.share + i

            @pl.when(unit != me)
            def _(unit=unit):
                back_arrival(unit).wait_recv()

        ext[0:RIM, :] = rim[s]
        ext[RIM : RIM + length, :] = pre[s].astype(F32)
        lane = lax.broadcasted_iota(jnp.int32, (length, LANES), 1)
        log_cols, strength_cols = gates_of(ab[s], lanes[0:1, :], lanes[1:2, :])
        log_rows, strength_rows = gates_of(abt[s], cols[0:8, 0:1], cols[8:16, 0:1])
        key_start = heads * key_dim
        value_start = 2 * heads * key_dim
        strict = row > col
        grads = jnp.zeros((length, LANES), F32)
        conv_grad[0:RIM, :] = jnp.zeros((RIM, conv_grad.shape[1]), F32)
        conv_grad[RIM + length : 2 * RIM + length, :] = jnp.zeros((RIM, conv_grad.shape[1]), F32)

        def activation(start, width):
            total = taps_ref[0:1, start : start + width] * ext[pl.ds(RIM - taps + 1, length), start : start + width]
            for tap in range(1, taps):
                total = total + (
                    taps_ref[tap : tap + 1, start : start + width]
                    * ext[pl.ds(RIM - taps + 1 + tap, length), start : start + width]
                )
            sig = sigmoid(total)
            return total * sig, sig * (1.0 + total * (1.0 - sig))

        def unit_back(grad, start, scale_by):
            act, slope = activation(start, key_dim)
            scale = lax.rsqrt(jnp.sum(act * act, axis=1, keepdims=True) + UNIT_EPSILON)
            inner = jnp.sum(act * grad, axis=1, keepdims=True)
            back = scale_by * scale * (grad - act * (scale * scale * inner))
            conv_grad[RIM : RIM + length, start : start + key_dim] = back * slope

        for h in range(heads):
            query, key, value = queries[s, h], keys[s, h], value_rows[s, h]
            query_f, key_f = query.astype(F32), key.astype(F32)
            strength = strength_cols[:, heads + h : heads + h + 1]
            cum_col, cum_row, end, decayed = decay_of(
                log_cols[:, h : h + 1], log_rows[h : h + 1, :], row, col
            )
            rise = jnp.exp(cum_col)
            end_weight = jnp.exp(end - cum_col)
            state = units.whole(states, s * heads + h)
            leaving = units.whole(leavings, s * heads + h)
            state_f, leaving_f = state.astype(F32), leaving.astype(F32)
            rows = split(delta_rows[s, h])
            out_grad = split(mixer_grad[s, h])
            products = mm(key, key, NT)
            scores = decayed * mm(query, key, NT)
            rows_grad = mm(split(scores), out_grad, TN) + end_weight * mm(key, leaving, NT)
            scores_grad = mm(out_grad, rows, NT)
            query_grad = rise * mm(out_grad, state)
            right_grad = mm(split(inverse_all[s, h]), split(rows_grad), TN)
            key_state = mm(key, state, NT)
            triangle_grad = -jnp.where(strict, mm(split(right_grad), rows, NT), 0.0)
            value_grad = strength * right_grad
            strength_grad = jnp.sum(right_grad * (value.astype(F32) - rise * key_state), axis=1, keepdims=True)
            read_grad = -rise * value_grad
            cum_grad = jnp.sum(read_grad * key_state, axis=1, keepdims=True)
            key_grad = mm(split(read_grad), state)
            decayed_grad = triangle_grad * decayed
            strength_grad = strength_grad + jnp.sum(decayed_grad * products, axis=1, keepdims=True)
            weighted = strength * decayed_grad
            both = weighted * products + scores_grad * scores
            products_grad = split(weighted)
            overlap_grad = split(scores_grad * decayed)
            cum_grad = cum_grad + jnp.sum(both, axis=1, keepdims=True) + jnp.sum(query_f * query_grad, axis=1, keepdims=True)
            query_grad = query_grad + mm(overlap_grad, key)
            key_grad = (
                key_grad + mm(overlap_grad, query, TN) + mm(products_grad, key) + mm(products_grad, key, TN)
            )
            moved = mm(rows, leaving)
            key_grad = key_grad + end_weight * moved
            end_part = jnp.sum(moved * key_f, axis=1, keepdims=True) * end_weight
            cum_grad = cum_grad - end_part
            last = jnp.sum(end_part, axis=0, keepdims=True) + jnp.exp(end) * jnp.sum(
                jnp.sum(leaving_f * state_f, axis=1, keepdims=True), axis=0, keepdims=True
            )
            turned = jnp.sum(jnp.where(row == col, cum_grad, 0.0), axis=0, keepdims=True)
            turned = turned - jnp.sum(both, axis=0, keepdims=True)
            log_grad = jnp.sum(jnp.where(row <= col, turned, 0.0), axis=1, keepdims=True) + last
            grads = jnp.where(lane == h, log_grad, grads)
            grads = jnp.where(lane == heads + h, strength_grad, grads)
            unit_back(query_grad, h * key_dim, key_dim ** (-0.5))
            unit_back(key_grad, key_start + h * key_dim, 1.0)
            if h == 0:
                rings[0].tick(s + 1)
            _, slope = activation(value_start + h * value_dim, value_dim)
            conv_grad[RIM : RIM + length, value_start + h * value_dim : value_start + (h + 1) * value_dim] = (
                value_grad * slope
            )

        softened = -lanes[0:1, :] * sigmoid(ab[s] + lanes[1:2, :])
        decay_part = grads * softened
        is_log = lane < heads
        ab_grad_out[s] = jnp.where(is_log, decay_part, grads * strength_cols * (1.0 - strength_cols))
        lane_grad_out[0:1, :] += jnp.sum(jnp.where(is_log, grads * log_cols, 0.0), axis=0, keepdims=True)
        lane_grad_out[1:2, :] += jnp.sum(jnp.where(is_log, decay_part, 0.0), axis=0, keepdims=True)
        main = conv_grad[RIM : RIM + length, :]
        pre_grad = jnp.zeros_like(main)
        rim_grad = jnp.zeros((RIM, conv_grad.shape[1]), F32)
        for tap in range(taps):
            weight = taps_ref[tap : tap + 1, :]
            taps_grad_out[tap : tap + 1, :] += jnp.sum(
                main * ext[pl.ds(RIM - taps + 1 + tap, length), :], axis=0, keepdims=True
            )
            pre_grad = pre_grad + weight * conv_grad[pl.ds(RIM + taps - 1 - tap, length), :]
            rim_grad = rim_grad + weight * conv_grad[pl.ds(taps - 1 - tap, RIM), :]
        pre_grad_out[s] = pre_grad.astype(BF16)
        tail[s] = pre_grad[length - 2 * RIM : length, :]
        rim_own[s] = rim_grad
        rings[1].tick(s)
        return carry

    lax.fori_loop(0, slots, delta_slot, 0)
    rim_copy().start()

    rings[0].tick(slots + 1)
    rings[1].tick(slots)
    rim_copy().wait_recv()
    inside = me < parts - 1
    for s in range(slots):
        late = jnp.where(inside, rim_in[s], 0.0)
        end = tail[s]
        shifted_in = jnp.concatenate([jnp.zeros_like(late), late], axis=0)
        pre_grad_out[s, length - 2 * RIM : length, :] = (end + shifted_in).astype(BF16)
    rim_copy().wait_send()

    def gain_copy(away):
        return remote(
            gain_own, gain_in.at[away - 1], gain_send.at[away - 1], gain_recv.at[away - 1],
            (place, lax.rem(head + away, head_parts)),
        )

    def small_copy(away):
        return remote(
            small_own, small_in.at[away - 1], small_send.at[away - 1], small_recv.at[away - 1],
            (lax.rem(place + away, parts), head),
        )

    def store_unit(start, size, block):
        unit_own[pl.ds(start, size), :] = block

    def store_value(start, size, block):
        value_own[pl.ds(start, size), :] = block

    weight_rows(normed, pre_grad_out[:, :, :unit_wide].reshape(-1, unit_wide), store_unit)
    rings[2].begin()
    weight_rows(normed, pre_grad_out[:, :, unit_wide:].reshape(-1, channels - unit_wide), store_value)
    rings[3].begin()

    def products(s, carry):
        low = ab_grad_out[s].astype(BF16)
        half = unit_wide // 2
        tools.send_part(
            0, s,
            raw(pre_grad_out[s, :, :half], query_weight[...], NT)
            + raw(pre_grad_out[s, :, half:unit_wide], key_weight[...], NT)
            + raw(pre_grad_out[s, :, unit_wide:], value_weight[...], NT)
            + raw(gate_grad[s], gate_weight[...], NT)
            + raw(low, ab_weight[...], NN),
        )
        ring_round(s)
        return carry

    ticks = rings[0].ticks

    def ring_round(j):
        for ring, step in (
            (rings[0], slots + 2 + j), (rings[2], 2 * j), (rings[3], 2 * j),
            (rings[1], slots + 1 + j), (rings[2], 2 * j + 1), (rings[3], 2 * j + 1),
        ):

            @pl.when(step < ticks)
            def _(ring=ring, step=step):
                ring.tick(step)

    arrive(2)
    lax.fori_loop(0, slots, products, 0)
    arrive(3)


    def first_join(s, carry):
        tools.join_core(0, s)
        return carry

    lax.fori_loop(0, slots, first_join, 0)
    ring_round(jnp.int32(slots))
    small_lines[...] = jnp.zeros_like(small_lines)
    gain_own[...] = gain_part[...]
    for away in range(1, head_parts):
        gain_copy(away).start()

    def second_join(s, carry):
        grad = tools.join_line(0, s)
        x = x_shard[s].astype(F32)
        inv = inv_first[s][:, 0:1]
        weighted = grad * input_gain[:, pl.ds(pl.multiple_of(head * shard, shard), shard)]
        input_grad_out[s] = weighted
        tools.send_stat(0, s, jnp.sum(weighted * x, axis=1, keepdims=True))
        return carry + jnp.sum(grad * x * inv, axis=0, keepdims=True)

    gain_line = lax.fori_loop(0, slots, second_join, jnp.zeros((1, shard), F32))
    ring_round(jnp.int32(slots + 1))

    def input_rows(s, carry):
        stat = tools.join_stat(0, s) / width
        inv = inv_first[s][:, 0:1]
        input_grad_out[s] = residual_grad[s] + inv * (
            input_grad_out[s] - x_shard[s].astype(F32) * (inv * inv * stat)
        )
        return carry

    lax.fori_loop(0, slots, input_rows, 0)
    gain_total = gain_own[...]
    for away in range(1, head_parts):
        gain_copy(away).wait_recv()
        gain_total = gain_total + gain_in[away - 1]
    low = ab_grad_out[...].astype(BF16).reshape(-1, LANES)
    ab_lines = raw(low, normed[...].reshape(-1, width), TN)
    at = 0
    for lines in [taps_grad_out[t : t + 1, :] for t in range(taps)] + [
        ab_lines[t : t + 1, :] for t in range(2 * heads)
    ] + [gain_total[0:1, :], lane_grad_out[0:1, :], lane_grad_out[1:2, :], mixed_part[0:1, :], gain_line]:
        for j in range(lines.shape[1] // LANES):
            small_lines[at : at + 1, :] = lines[:, j * LANES : (j + 1) * LANES]
            at += 1
    small_own[...] = small_lines[...].astype(BF16)

    def small_start(away, carry):
        small_copy(away).start()
        return carry

    lax.fori_loop(1, parts, small_start, 0)

    def rest(j, carry):
        ring_round(j)
        return carry

    lax.fori_loop(slots + 2, ticks - slots - 1, rest, 0)
    small_sum[...] = small_lines[...]

    def small_join(away, carry):
        small_copy(away).wait_recv()
        small_sum[...] += small_in[away - 1].astype(F32)
        small_copy(away).wait_send()
        return carry

    lax.fori_loop(1, parts, small_join, 0)
    for s in range(slots):
        total = block_base[s]
        for away in range(1, tools.lines):
            block_copy(s, away).wait_recv()
            total = total + block_in[s, away - 1].astype(F32)
            block_copy(s, away).wait_send()
        block_out[s] = total.astype(BF16)
    for away in range(1, head_parts):
        gain_copy(away).wait_send()

    def drain(s, carry):
        tools.drain(s)
        return carry

    lax.fori_loop(0, slots, drain, 0)
    def drain_units(away, carry):
        back_copy(lax.rem(me + away, parts)).wait_send()
        return carry

    lax.fori_loop(1, parts, drain_units, 0)
    for ring in rings:
        ring.finish()


def backward_call(parts, head_parts, heads, taps, *operands):
    gated, normed, gate_grad, pre, ab, keys, value_rows, states, gate_part, x_shard, gain_part, down_part = (
        operands[i] for i in (2, 4, 5, 6, 8, 14, 15, 18, 20, 26, 30, 33)
    )
    slots, length, channels = pre.shape
    value_dim, key_dim = value_rows.shape[3], keys.shape[3]
    width, shard = normed.shape[2], x_shard.shape[2]
    lines = (taps * channels + 2 * heads * width + gain_part.shape[1] + 2 * shard) // LANES + 2
    lines += -lines % 16
    sds = jax.ShapeDtypeStruct
    dma = pltpu.SemaphoreType.DMA
    out_shape = (padded_rows(gated.shape[2], width, parts), width)
    first_shape = (width, gate_grad.shape[2])
    unit_shape = (width, 2 * heads * key_dim)
    value_shape = (width, heads * value_dim)
    sums = (gate_part.shape, out_shape, first_shape, unit_shape, value_shape, gate_part.shape, down_part.shape)
    outs = (sds(x_shard.shape, F32), sds((lines, LANES), F32)) + tuple(sds(a, BF16) for a in sums + (x_shard.shape,))
    away = head_parts // 2 - 1
    unit = pltpu.VMEM(states.shape, BF16)
    edge = pltpu.VMEM((slots, RIM, channels), F32)
    scratch = (
        [
            pltpu.VMEM(ab.shape, F32), pltpu.VMEM((8, channels), F32),
            pltpu.VMEM((8, LANES), F32),
        ]
        + [pltpu.VMEM(a, BF16) for a in sums[1:3]]
        + [
            pltpu.VMEM((length + RIM, channels), F32), pltpu.VMEM((length + 2 * RIM, channels), F32),
            pltpu.VMEM((slots, 2 * RIM, channels), F32), edge, edge, unit, unit,
            pltpu.VMEM((lines, LANES), F32), pltpu.VMEM((lines, LANES), BF16),
            pltpu.VMEM((parts - 1, lines, LANES), BF16),
            pltpu.VMEM(gain_part.shape, F32), pltpu.VMEM((head_parts - 1,) + gain_part.shape, F32),
            pltpu.VMEM((slots, away, length, shard), BF16), dma((slots, away)), dma((slots, away)),
            dma((parts - 1,)), dma((parts - 1,)), dma((1,)), dma((1,)),
            dma((parts - 1,)), dma((parts - 1,)), dma((head_parts - 1,)), dma((head_parts - 1,)),
        ]
        + ring_scratch(parts, [gate_part.shape, gate_part.shape])
        + ring_scratch(parts, [down_part.shape, out_shape, first_shape])
        + ring_scratch(parts, [unit_shape])
        + ring_scratch(parts, [value_shape])
        + head_scratch(1, 1, slots, head_parts, length, shard)
    )
    return staged_call(
        functools.partial(backward_kernel, slots, heads, key_dim, value_dim, parts, head_parts),
        operands, outs, scratch, 3,
        late=(
            (2, 3, 4, 5, 33), (0, 6, 7, 8, 9, 13, 14, 15, 16, 17, 18, 35), (21, 22, 23, 24, 25),
            (26, 27, 28, 29, 30, 31, 34),
        ),
        kept=(2, 3, 4, 5, 6, 7, 8), flops=5 * 10**10,
    )


def per_device(
    hidden_in, lengths, input_gain, query_weight, key_weight, value_weight, alpha_weight, beta_weight,
    decay_log, decay_bias, query_kernel, key_kernel, value_kernel, gate_weight, output_gain,
    output_weight, mixed_gain, swiglu_gate, swiglu_up, swiglu_down, cotangent,
):
    slots, segment, width = hidden_in.shape
    heads = decay_log.shape[0]
    key_dim = query_kernel.shape[1] // heads
    value_dim = value_kernel.shape[1] // heads
    taps = query_kernel.shape[0]
    split_key = heads * key_dim
    channels = 2 * split_key + heads * value_dim
    head_parts = lax.axis_size("head")
    seq_parts = lax.axis_size("seq")
    shard = width // head_parts

    ab_weight = jnp.concatenate(
        [alpha_weight.T, beta_weight.T, jnp.zeros((LANES - 2 * heads, width), BF16)], axis=0
    )
    gain_row = output_gain[None, :]

    (
        query, key, value, inverse, eff, delta_rows, mixer, gated, normed_first, pre_all, gate_pre, x_low,
        inv_first, rim_pre, ab_pre, ab_rows, states, maps_in, kernel, lane_gates, col_gates,
    ) = forward_call(
        seq_parts, head_parts, heads, hidden_in, input_gain[None, :],
        query_weight, key_weight, value_weight, gate_weight, ab_weight, query_kernel, key_kernel, value_kernel,
        decay_log[None, :], decay_bias[None, :], gain_row,
    )
    (
        block_base, gate_part, residual_grad, mixer_rows_grad, mixer_grad, gate_grad, mixed_part, gain_part,
        shifts_in, down_part, up_part, block_line,
    ) = middle_call(
        seq_parts, head_parts, heads, gated, x_low, cotangent, lengths[None, :], output_weight, swiglu_gate.T,
        swiglu_up.T, swiglu_down, mixed_gain[None, :], mixer, gate_pre, gain_row, eff,
    )
    (
        input_grad, small_sum, gate_sum, out_sum, gate_first_sum, unit_sum, value_sum, up_sum, down_sum,
        block_out,
    ) = backward_call(
        seq_parts, head_parts, heads, taps, mixer_grad, shifts_in, gated,
        mixer_rows_grad.reshape(slots * segment, width), normed_first, gate_grad,
        pre_all, rim_pre, ab_pre, ab_rows, kernel, lane_gates, col_gates, query, key, value, inverse, delta_rows,
        states, maps_in, gate_part, query_weight, key_weight, value_weight, gate_weight, ab_weight, x_low,
        inv_first, residual_grad, input_gain[None, :], gain_part, mixed_part,
        up_part, down_part, block_base, block_line,
    )
    hidden = swiglu_gate.shape[1]
    flat_small = small_sum.reshape(-1)
    pieces, at = [], 0
    for size in (taps * channels, 2 * heads * width, value_dim, LANES, LANES, shard, shard):
        pieces.append(flat_small[at : at + size])
        at += size
    taps_sum = pieces[0].reshape(taps, channels)
    ab_sum = pieces[1].reshape(2 * heads, width).T
    value_share = value_dim // head_parts
    output_gain_grad = lax.dynamic_slice_in_dim(
        pieces[2], lax.axis_index("head") * value_share, value_share, 0
    )
    return (
        block_out,
        input_grad,
        pieces[6],
        unit_sum[:, :split_key].astype(F32),
        unit_sum[:, split_key:].astype(F32),
        value_sum.astype(F32),
        ab_sum[:, :heads],
        ab_sum[:, heads:],
        pieces[3][:heads],
        pieces[4][:heads],
        taps_sum[:, :split_key],
        taps_sum[:, split_key : 2 * split_key],
        taps_sum[:, 2 * split_key :],
        gate_first_sum.astype(F32),
        output_gain_grad,
        out_sum[: heads * value_dim].astype(F32),
        pieces[5],
        gate_sum[:hidden].astype(F32).T,
        up_sum[:hidden].astype(F32).T,
        down_sum[:hidden].astype(F32),
    )


def solution(mesh):
    seq, cols, lines = P(None, "seq", None), P(None, "head"), P("head", None)
    one = P("head")
    placed = (
        seq, P(), P(), cols, cols, cols, cols, cols, one, one, cols, cols, cols, cols, P(), lines, one,
        cols, cols, lines, seq,
    )
    both = P(None, "seq", "head")
    return jax.shard_map(
        per_device,
        mesh=mesh,
        in_specs=placed,
        out_specs=(
            both, both, one, cols, cols, cols, cols, cols, one, one, cols, cols, cols, cols, one, lines,
            one, cols, cols, lines,
        ),
        check_vma=False,
    )
```
